32 devices in a mesh: group: 4 (over y, x), member: 8 (over z, core).
Axes of the slice: x: 2, y: 2, z: 4, core: 2. Of those that a mesh axis runs over, the one named last changes fastest.
Arguments:
- mesh_vector: bfloat16 [32768, 128], P(('group', 'member')), may hold values from -6 to 6
- cluster_position: int32 [32768], P(('group', 'member')), may hold values from 0 to 32767, as said below
- cluster_sizes: int32 [32], replicated, may hold values from 256 to 1792, as said below
- block_ranks: int32 [62], replicated, may hold values from 32 to 128, as said below
- diag_block: bfloat16 [2, 57344, 1792], P(None, ('group', 'member')), may hold values from -0.09375 to 0.09375
- top_left: bfloat16 [2, 2, 57344, 128], P(None, None, ('group', 'member')), may hold values from -0.375 to 0.375
- top_right: bfloat16 [2, 2, 57344, 128], P(None, None, ('group', 'member'))
- low_left: bfloat16 [3, 2, 57344, 64], P(None, None, ('group', 'member')), may hold values from -0.5 to 0.5
- low_right: bfloat16 [3, 2, 57344, 64], P(None, None, ('group', 'member'))
Outputs:
- product: float32 [32768, 128], P(('group', 'member'))
The draws below stay inside these ranges and needn't reach their ends.
Inputs may be any that keep to these rules, and one draw needn't show every extreme that they name: `cluster_position`: A permutation of the unknowns. In cluster order every aligned run of 32 positions holds exactly one row of each device, so each device holds exactly size / 32 rows of every cluster. `cluster_sizes`: multiples of 32 that sum to 32768; one is exactly 1792. `block_ranks`: entries 0 .. 5 lie in 64 .. 128, the others in 32 .. 64; entry 0 is 128.
All inputs are finite; a program needn't handle non-finite values.
Results may differ from the reference program's by a relative error of at most 0.0027.
Values may be sent and summed in bfloat16 or wider, within the bound.
No kernel may reach another device: no remote copies, remote signals or barrier semaphores. Data moves between devices by JAX's collectives and lax.ppermute only.
A program may use at most 64 MiB of HBM per device.

```python
import jax
import jax.numpy as jnp
from jax import lax

COLS = 128
R = 1024
K = 128
KM = 64
LEAVES = 32
NU = 32768
CAP = 1792
NS = 57344
GLEVELS = 2
MLEVELS = 3
TOPNODES = 6
HEAP = 62


def cluster_layout(key):
    layout_key = jax.random.fold_in(key, 101)
    average = R // LEAVES
    widest = (3 * average + 3) // 4
    pairs_count = LEAVES // 2
    pairing = jax.random.permutation(jax.random.fold_in(layout_key, 1), LEAVES)
    spread = jax.random.randint(jax.random.fold_in(layout_key, 2), (pairs_count,), 0, widest + 1)
    spread = spread.at[0].set(widest)
    paired_counts = jnp.concatenate([average + spread, average - spread]).astype(jnp.int32)
    counts = jnp.zeros((LEAVES,), jnp.int32).at[pairing].set(paired_counts)
    size_list = counts * LEAVES
    window_keys = jax.random.split(jax.random.fold_in(layout_key, 3), R)
    owners_of = jax.vmap(lambda one_key: jax.random.permutation(one_key, LEAVES))(window_keys)
    inverse = jnp.argsort(owners_of, axis=1).astype(jnp.int32)
    local_keys = jax.random.split(jax.random.fold_in(layout_key, 4), LEAVES)
    windows = jax.vmap(lambda one_key: jax.random.permutation(one_key, R))(local_keys).astype(jnp.int32)
    sources = jnp.arange(LEAVES, dtype=jnp.int32)[:, None]
    offsets = inverse[windows, sources]
    positions = windows * LEAVES + offsets
    return (size_list.astype(jnp.int32), positions.reshape(-1).astype(jnp.int32))


def draw_cluster_sizes(key, part):
    return cluster_layout(key)[0]


def draw_cluster_position(key, part):
    return cluster_layout(key)[1]


def draw_block_ranks(key, part):
    key = jax.random.fold_in(key, 7)
    positions_heap = jnp.arange(HEAP, dtype=jnp.int32)
    upper = positions_heap < TOPNODES
    lowest = jnp.where(upper, K // 2, KM // 2)
    highest = jnp.where(upper, K, KM)
    raw = jax.random.randint(key, (HEAP,), 0, 1 << 20)
    ranks = raw % (highest - lowest + 1) + lowest
    ranks = ranks.at[0].set(K)
    ranks = ranks.at[HEAP - 1].set(KM // 2)
    return ranks.astype(jnp.int32)


def factor_values(key, shape):
    return jax.random.normal(key, shape, jnp.float32)


def draw_top_right(key, part):
    key = jax.random.fold_in(key, 5)
    level_ids = jnp.arange(GLEVELS, dtype=jnp.float32) + 1.0
    scaling = (2.0 * NU / 2.0 ** level_ids) ** (-0.5)
    values = factor_values(key, (GLEVELS, 2, NS, K))
    return (values * scaling[:, None, None, None]).astype(jnp.bfloat16)


def draw_low_right(key, part):
    key = jax.random.fold_in(key, 9)
    level_ids = jnp.arange(MLEVELS, dtype=jnp.float32) + 1.0 + GLEVELS
    scaling = (2.0 * NU / 2.0 ** level_ids) ** (-0.5)
    values = factor_values(key, (MLEVELS, 2, NS, KM))
    return (values * scaling[:, None, None, None]).astype(jnp.bfloat16)


def shard_levels(own_key, dims, cuts, smallest, top_value):
    def one(dim, shards_of):
        draws = jax.random.uniform(jax.random.fold_in(jax.random.fold_in(own_key, 6), dim), (shards_of,), jnp.float32, smallest / len(cuts), top_value / len(cuts))
        return jnp.repeat(jnp.exp(draws), dims[dim] // shards_of).reshape((-1,) + (1,) * (len(dims) - dim - 1))

    factor_of = one(*cuts[0])
    for cut in cuts[1:]:
        factor_of = factor_of * one(*cut)
    return factor_of


def centred(own_key, dims, scale, most, pieces=(), kind=jnp.bfloat16):
    array = jax.random.normal(own_key, dims, jnp.float32) * scale
    if len(pieces) > 0:
        array = shard_levels(own_key, dims, pieces, -0.22, 0.18) * array
    return jnp.clip(array, min=-most, max=most).astype(kind)


def setup_inputs(seed: int = 0) -> dict:
    splits = jax.random.split(jax.random.key(seed), 10)
    return {
        "mesh_vector": centred(splits[0], (NU, COLS), 1.0, 6.0, ((0, 32),)),
        "cluster_position": draw_cluster_position(jax.random.fold_in(splits[9], 71), 0),
        "cluster_sizes": draw_cluster_sizes(jax.random.fold_in(splits[9], 71), 0),
        "block_ranks": draw_block_ranks(jax.random.fold_in(splits[9], 71), 0),
        "diag_block": centred(splits[4], (2, NS, CAP), (2 * CAP) ** -0.5, 0.09375, ((1, 32),)),
        "top_left": centred(splits[5], (GLEVELS, 2, NS, K), (2 * K) ** -0.5, 0.375, ((2, 32),)),
        "top_right": draw_top_right(jax.random.fold_in(splits[9], 71), 0),
        "low_left": centred(splits[7], (MLEVELS, 2, NS, KM), (2 * KM) ** -0.5, 0.5, ((2, 32),)),
        "low_right": draw_low_right(jax.random.fold_in(splits[9], 71), 0),
    }


def rotate(values):
    middle = values.shape[-1] // 2
    return jnp.concatenate([-values[..., middle:], values[..., :middle]], axis=-1)


def reference(mesh_vector, cluster_position, cluster_sizes, block_ranks, diag_block, top_left, top_right, low_left, low_right):
    leaves = cluster_sizes.shape[0]
    capacity = diag_block.shape[2]
    total_slots = leaves * capacity
    cluster_ends = jnp.cumsum(cluster_sizes).astype(jnp.int32)
    starts = (cluster_ends - cluster_sizes).astype(jnp.int32)
    owners = jnp.sum((cluster_position[:, None] >= cluster_ends[None, :]).astype(jnp.int32), axis=1)
    slot_ids = (owners * capacity + cluster_position - starts[owners]).astype(jnp.int32)
    values = jnp.zeros((total_slots, COLS), jnp.bfloat16).at[slot_ids].set(mesh_vector)
    turned = rotate(values)

    def diagonal_term(leaf_index):
        offset = (leaf_index * capacity).astype(jnp.int32)
        diag_piece = lax.dynamic_slice_in_dim(diag_block, offset, capacity, 1)
        plain = lax.dynamic_slice_in_dim(values, offset, capacity, 0)
        twisted = lax.dynamic_slice_in_dim(turned, offset, capacity, 0)
        return jnp.dot(diag_piece[0], plain, preferred_element_type=jnp.float32) + jnp.dot(diag_piece[1], twisted, preferred_element_type=jnp.float32)

    result = lax.map(diagonal_term, jnp.arange(leaves, dtype=jnp.int32)).reshape(total_slots, COLS)
    pair_full = jnp.stack([values, turned]).astype(jnp.float32)
    for tree_level in range(1, GLEVELS + MLEVELS + 1):
        if tree_level <= GLEVELS:
            right_factor = top_right[tree_level - 1]
            left_factor = top_left[tree_level - 1]
        else:
            right_factor = low_right[tree_level - 1 - GLEVELS]
            left_factor = low_left[tree_level - 1 - GLEVELS]
        nodes = 2 ** tree_level
        rank_cap = right_factor.shape[-1]
        node_rows = total_slots // nodes
        right_full = right_factor.astype(jnp.float32).reshape(2, nodes, node_rows, rank_cap)
        partial_value = jnp.einsum("pask,pasc->akc", right_full, pair_full.reshape(2, nodes, node_rows, COLS))
        sibling = partial_value.reshape(nodes // 2, 2, rank_cap, COLS)[:, ::-1].reshape(nodes, rank_cap, COLS)
        node_ranks = block_ranks[nodes - 2: 2 * nodes - 2]
        keep_mask = jnp.arange(rank_cap, dtype=jnp.int32)[None, :] < node_ranks[:, None]
        coefficient = jnp.where(keep_mask[:, :, None], sibling, 0.0).astype(jnp.bfloat16)
        coefficient_pair = jnp.stack([coefficient, rotate(coefficient)]).astype(jnp.float32)
        left_full = left_factor.astype(jnp.float32).reshape(2, nodes, node_rows, rank_cap)
        result = result + jnp.einsum("pask,pakc->asc", left_full, coefficient_pair).reshape(total_slots, COLS)
    return result[slot_ids]
```

```python
import functools

import jax
import jax.numpy as jnp
from jax import lax
from jax.experimental import pallas as pl
from jax.experimental.pallas import tpu as pltpu
from jax.sharding import PartitionSpec as P

F32 = jnp.float32
BF16 = jnp.bfloat16
I32 = jnp.int32
VMEM = pl.BlockSpec(memory_space=pltpu.VMEM)
SMEM = pl.BlockSpec(memory_space=pltpu.SMEM)
HBM = pl.BlockSpec(memory_space=pltpu.HBM)
DMA = pltpu.SemaphoreType.DMA


def iota(shape, dim):
    return lax.broadcasted_iota(I32, shape, dim)


def hot(mask):
    return jnp.where(mask, 1.0, 0.0).astype(BF16)


def dot(a, b, over=(1, 0)):
    return lax.dot_general(
        a, b, (((over[0],), (over[1],)), ((), ())), preferred_element_type=F32
    )


def call(kernel, outs, ins, args, flops, moved, limit, scratch=(), **more):
    return pl.pallas_call(
        kernel,
        out_shape=outs,
        in_specs=ins,
        out_specs=more.pop("out_specs", [VMEM] * len(outs)),
        scratch_shapes=scratch,
        cost_estimate=pl.CostEstimate(flops=flops, bytes_accessed=moved, transcendentals=0),
        compiler_params=pltpu.CompilerParams(vmem_limit_bytes=limit << 20),
        **more,
    )(*args)


def partner(block, axis, apart):
    count = lax.axis_size(axis)
    route = []
    for low in range(count):
        high = low | 1 << apart
        if high != low and high < count:
            route += [(low, high), (high, low)]
    return lax.ppermute(block, axis, route)


def far(*arrays):
    return [pltpu.with_memory_space_constraint(array, pltpu.HBM) for array in arrays]


def turn(block):
    half = block.shape[1] // 2
    return jnp.where(iota(block.shape, 1) < half, -1.0, 1.0) * pltpu.roll(block, half, 1)


def pack_kernel(leaves, bucket, sizes_in, position_in, rows_in, packed, windows, *scratch):
    sizes, position, rows, ordered, sems = scratch
    copies = [
        pltpu.make_async_copy(source, target, sems.at[i])
        for i, (source, target) in enumerate(
            [(sizes_in, sizes), (position_in, position), (rows_in, rows)]
        )
    ]
    for copy in copies:
        copy.start()
    for copy in copies[:2]:
        copy.wait()
    count = rows.shape[0]
    padded = packed.shape[1]
    shift = leaves.bit_length() - 1
    here = position[...]
    window = jnp.right_shift(here, shift)
    zero = jnp.zeros((1, count), I32)
    owner, first = zero, zero
    starts = [0]
    for c in range(leaves):
        starts.append(starts[-1] + jnp.right_shift(sizes[c], shift))
        beyond = window >= starts[-1]
        owner = owner + beyond.astype(I32)
        first = jnp.where(beyond, starts[-1], first)
    offset = jnp.bitwise_and(here, leaves - 1).astype(F32)
    picked = jnp.where(iota((leaves, count), 0) == owner, offset, 0.0).astype(BF16)
    offsets = dot(picked, hot(iota((128, count), 0) == window - first), (1, 1))
    windows[...] = jnp.transpose(jnp.broadcast_to(window, (128, count)))
    copies[2].wait()
    values = rows[...]
    block = 256
    for low in range(0, count, block):
        ordered[low : low + block, :] = dot(hot(iota((block, count), 0) + low == window), values)
    ordered[count:, :] = jnp.zeros((padded, 128), F32)
    line = iota((padded, 128), 0)
    for c in range(leaves):
        data = ordered[pl.ds(starts[c], padded), :]
        data = jnp.where(line < starts[c + 1] - starts[c], data, 0.0)
        data = jnp.where(line == bucket, offsets[c : c + 1, :], data)
        packed[c] = data.astype(BF16)


def stage_kernel(left_top_in, left_low_in, after, left_top, left_low, raw, sems):
    copies = [
        pltpu.make_async_copy(left_low_in, raw, sems.at[0]),
        pltpu.make_async_copy(left_top_in, left_top, sems.at[1]),
    ]
    for copy in copies:
        copy.start()
    copies[0].wait()
    levels, parts, width, capacity = raw.shape
    left_low[...] = jnp.transpose(raw[...].reshape(levels * parts * width, capacity))
    copies[1].wait()


def field_kernel(leaves, bucket, place, arrived, right_top_in, right_low_in, *rest):
    pair, targets, send, keep, whole, right_top, right_low, sems = rest
    copies = [
        pltpu.make_async_copy(right_low_in, right_low, sems.at[0]),
        pltpu.make_async_copy(right_top_in, right_top, sems.at[1]),
    ]
    for copy in copies:
        copy.start()
    capacity = leaves * bucket
    padded = arrived.shape[1]
    part = leaves * 8
    core = jnp.bitwise_and(place[0], 1)
    last = arrived[:, padded - 16 :, :].reshape(leaves * 16, 128)
    carrier = iota((leaves, leaves * 16), 1) == iota((leaves, leaves * 16), 0) * 16 + bucket % 16
    offsets = dot(hot(carrier), last).astype(BF16)
    spread = hot(jnp.right_shift(iota((leaves, part), 1), 3) == iota((leaves, part), 0))
    spread_offsets = dot(offsets, spread, (0, 0))
    lane_window = jnp.bitwise_and(iota((8, part), 1), 7)
    own = lane_window == iota((8, part), 0)
    for g in range(padded // 8):
        size = min(part, capacity - g * part)
        if size <= 0:
            continue
        rows = spread_offsets[g * 8 : g * 8 + 8, :]
        offset = jnp.sum(jnp.where(own, rows, 0.0), axis=0, keepdims=True).astype(I32)
        target = offset + lane_window[:1, :] * leaves
        targets[g * part : (g + 1) * part, :] = jnp.transpose(
            jnp.broadcast_to(target, (128, part))
        )
        if g % 2 == 0:
            both = arrived[:, g * 8 : g * 8 + 16, :].astype(F32)
        chunk = both[:, g % 2 * 8 : g % 2 * 8 + 8, :].reshape(part, 128).astype(BF16)
        placed = dot(hot(iota((part, part), 0) == target), chunk)
        pair[0, g * part : g * part + size, :] = placed[:size].astype(BF16)
        pair[1, g * part : g * part + size, :] = turn(placed)[:size].astype(BF16)
    for copy in copies:
        copy.wait()
    levels, _, width, _ = right_low.shape
    top_levels, _, _, top_width = right_top.shape
    total = jnp.zeros((levels * width, 128), F32)
    tops = jnp.zeros((128, top_levels * top_width), F32)
    for p in range(2):
        total += dot(right_low[:, p].reshape(levels * width, capacity), pair[p])
        factors = jnp.concatenate([right_top[level, p] for level in range(top_levels)], axis=1)
        tops += dot(jnp.transpose(pair[p]), factors)
    for level in range(top_levels):
        whole[level * 128 : (level + 1) * 128, :] = tops[:, level * top_width : (level + 1) * top_width]
    whole[top_levels * 128 :, :] = total
    at = 0
    for low, half in segments(top_levels, levels, width):
        mine = pl.multiple_of(low + core * half, 8)
        other = pl.multiple_of(low + (1 - core) * half, 8)
        keep[at : at + half, :] = whole[pl.ds(mine, half), :]
        send[at : at + half, :] = whole[pl.ds(other, half), :]
        at += half
    send[at:, :] = total[(levels - 1) * width :]


def segments(top_levels, levels, width):
    tops = [(level * 128, 64) for level in range(top_levels)]
    return tops + [(top_levels * 128 + level * width, width // 2) for level in range(levels - 1)]


def diag_kernel(block, pair, after, out):
    out[...] = dot(block[0], pair[0]) + dot(block[1], pair[1])


def out_kernel(leaves, bucket, pieces, place, *rest):
    bases = rest[:pieces]
    left_top, left_low, nearest, own, theirs, targets, packed, spare, ordered = rest[pieces:]
    capacity = leaves * bucket
    part = leaves * 8
    groups = spare.shape[0] // part
    top_levels = left_top.shape[0]
    width = nearest.shape[0]
    levels = left_low.shape[1] // (2 * width)
    core = jnp.bitwise_and(place[0], 1)
    coefs = []
    at = 0
    for _, half in segments(top_levels, levels, width):
        a, b = own[at : at + half, :].astype(F32), theirs[at : at + half, :].astype(F32)
        first, second = jnp.where(core == 0, a, b), jnp.where(core == 0, b, a)
        coefs.append(jnp.concatenate([first, second], axis=0))
        at += half
    coefs.append(nearest[...])
    tops, lows = [], []
    for level, coef in enumerate(coefs):
        lanes = level < top_levels
        coef = jnp.where(iota(coef.shape, 1 if lanes else 0) < place[1 + level], coef, 0.0)
        if lanes:
            half = coef.shape[0] // 2
            tops += [coef, jnp.concatenate([-coef[half:], coef[:half]], axis=0)]
        else:
            lows += [coef, turn(coef)]
    stacked = jnp.concatenate([jnp.transpose(coef) for coef in tops] + lows, axis=0).astype(BF16)
    cut = capacity // pieces
    for i in range(pieces):
        rows = slice(i * cut, (i + 1) * cut)
        factors = [left_top[level, p, rows, :] for level in range(top_levels) for p in range(2)]
        factors = jnp.concatenate(factors + [left_low[rows, :]], axis=1)
        spare[rows, :] = (bases[i][...] + dot(factors, stacked)).astype(BF16)
    if groups * part > capacity:
        spare[capacity:, :] = jnp.zeros((groups * part - capacity, 128), BF16)
    lanes = iota((part, 128), 1)
    for g in range(groups):
        target = targets[g * part : (g + 1) * part, :]
        picks = [hot(target == lanes + low) for low in range(0, part, 128)]
        moved = dot(jnp.concatenate(picks, axis=1), spare[g * part : (g + 1) * part, :])
        ordered[:, g * 8 : g * 8 + 8, :] = moved.reshape(leaves, 8, 128)
    packed[...] = ordered[:, :bucket, :].reshape(capacity, 128).astype(BF16)


def unpack_kernel(leaves, bucket, sizes, windows, returned, out, wide, ordered):
    count = windows.shape[0]
    shift = leaves.bit_length() - 1
    wide[...] = returned[...].astype(F32)
    start = 0
    for c in range(leaves):
        ordered[pl.ds(start, bucket), :] = wide[c * bucket : (c + 1) * bucket, :]
        start += jnp.right_shift(sizes[c], shift)
    values = ordered[:count, :].astype(BF16)
    block = 256
    lanes = iota((block, 128), 1)
    for low in range(0, count, block):
        window = windows[low : low + block, :]
        picks = [hot(window == lanes + at) for at in range(0, count, 128)]
        out[low : low + block, :] = dot(jnp.concatenate(picks, axis=1), values)


def on_device(
    mesh_vector,
    cluster_position,
    cluster_sizes,
    block_ranks,
    diag_block,
    top_left,
    top_right,
    low_left,
    low_right,
):
    groups = lax.axis_size("group")
    members = lax.axis_size("member")
    leaves = groups * members
    group_levels = groups.bit_length() - 1
    member_levels = members.bit_length() - 1
    levels = group_levels + member_levels
    device = lax.axis_index("group") * members + lax.axis_index("member")
    capacity = diag_block.shape[1]
    bucket = capacity // leaves
    padded = (bucket + 16) // 16 * 16
    filled = (bucket + 7) // 8 * 8
    count, columns = mesh_vector.shape
    everyone = ("group", "member")
    low_left = jnp.swapaxes(low_left, 2, 3)
    low_right = jnp.swapaxes(low_right, 2, 3)
    width = low_left.shape[2]
    top_width = top_left.shape[3]
    far_flops = 4 * capacity * columns * (group_levels * top_width + member_levels * width)

    level_ids = jnp.arange(1, levels + 1, dtype=I32)
    ranks = block_ranks[(1 << level_ids) - 2 + jnp.right_shift(device, levels - level_ids)]
    place = jnp.concatenate([device[None].astype(I32), ranks])

    packed, windows = call(
        functools.partial(pack_kernel, leaves, bucket),
        [
            jax.ShapeDtypeStruct((leaves, padded, columns), BF16),
            jax.ShapeDtypeStruct((count, 128), I32),
        ],
        [HBM] * 3,
        far(cluster_sizes, cluster_position.reshape(1, count), mesh_vector),
        2 * count * count * columns,
        4 << 20,
        16,
        scratch=[
            pltpu.SMEM((leaves,), I32),
            pltpu.VMEM((1, count), I32),
            pltpu.VMEM((count, columns), BF16),
            pltpu.VMEM((count + padded, columns), F32),
            DMA((3,)),
        ],
    )
    arrived = lax.all_to_all(packed, everyone, split_axis=0, concat_axis=0, tiled=True)
    shared = group_levels * columns // 2 + (member_levels - 1) * width // 2
    pair, targets, send, keep = call(
        functools.partial(field_kernel, leaves, bucket),
        [
            jax.ShapeDtypeStruct((2, capacity, columns), BF16),
            jax.ShapeDtypeStruct((leaves * filled, 128), I32),
            jax.ShapeDtypeStruct((shared + width, columns), F32),
            jax.ShapeDtypeStruct((shared, columns), F32),
        ],
        [SMEM, VMEM, HBM, HBM],
        (place, arrived, *far(top_right, low_right)),
        far_flops,
        6 << 20,
        24,
        scratch=[
            pltpu.VMEM((group_levels * columns + member_levels * width, columns), F32),
            pltpu.VMEM(top_right.shape, BF16),
            pltpu.VMEM(low_right.shape, BF16),
            DMA((2,)),
        ],
    )
    pieces = 2
    cut = capacity // pieces
    rows = cut // 4

    def diagonal(i, after):
        return call(
            diag_kernel,
            jax.ShapeDtypeStruct((cut, columns), F32),
            [
                pl.BlockSpec((2, rows, capacity), lambda j: (0, j + 4 * i, 0)),
                pl.BlockSpec((2, capacity, columns), lambda j: (0, 0, 0)),
                pl.BlockSpec(memory_space=pl.ANY),
            ],
            (*far(diag_block), pair, after),
            4 * cut * capacity * columns,
            4 * cut * capacity,
            16,
            grid=(4,),
            out_specs=pl.BlockSpec((rows, columns), lambda j: (j, 0)),
        )

    received = partner(send, "member", 0)
    nearest = received[shared:]
    running = keep + received[:shared]
    bases = []
    coefs = []
    for bit in range(1, member_levels):
        rest = running.shape[0] - width // 2
        received = partner(running, "member", bit)
        if len(bases) < pieces:
            bases.append(diagonal(len(bases), running))
            received, bases[-1] = lax.optimization_barrier((received, bases[-1]))
        coefs.insert(0, received[rest:].astype(BF16))
        running = running[:rest] + received[:rest]
    left_top, left_low = call(
        stage_kernel,
        [
            pltpu.VMEM(top_left.shape, BF16),
            pltpu.VMEM((capacity, member_levels * 2 * width), BF16),
        ],
        [HBM, HBM, pl.BlockSpec(memory_space=pl.ANY)],
        (*far(top_left, low_left), running),
        0,
        8 << 20,
        16,
        scratch=[pltpu.VMEM(low_left.shape, BF16), DMA((2,))],
    )
    half = columns // 2
    tops = [None] * group_levels
    for apart in range(1, groups):
        level = group_levels - apart.bit_length()
        sent = running[level * half : (level + 1) * half]
        if apart == 1:
            sent = sent.astype(BF16)
        route = [(low, low ^ apart) for low in range(groups)]
        heard = lax.ppermute(sent, "group", route)
        tops[level] = heard if tops[level] is None else tops[level] + heard
    left_top, left_low, tops = lax.optimization_barrier((left_top, left_low, tops))
    own = jnp.concatenate([top.astype(BF16) for top in tops] + coefs)
    theirs = partner(own, "member", 0)

    leaving = call(
        functools.partial(out_kernel, leaves, bucket, pieces),
        [jax.ShapeDtypeStruct((capacity, columns), BF16)],
        [SMEM] + [VMEM] * (pieces + 6),
        (place, *bases, left_top, left_low, nearest, own, theirs, targets),
        far_flops,
        6 << 20,
        24,
        scratch=[
            pltpu.VMEM((leaves * filled, 128), BF16),
            pltpu.VMEM((leaves, filled, 128), F32),
        ],
    )[0]
    returned = lax.all_to_all(
        leaving.reshape(leaves, bucket, columns), everyone, split_axis=0, concat_axis=0, tiled=True
    )
    return call(
        functools.partial(unpack_kernel, leaves, bucket),
        [jax.ShapeDtypeStruct((count, columns), F32)],
        [SMEM] + [VMEM] * 2,
        (cluster_sizes, windows, returned.reshape(capacity, columns)),
        2 * count * count * columns,
        2 << 20,
        16,
        scratch=[
            pltpu.VMEM((capacity, 128), F32),
            pltpu.VMEM((count + filled, 128), F32),
        ],
    )[0]


def solution(mesh):
    return jax.shard_map(
        on_device,
        mesh=mesh,
        in_specs=(
            P(("group", "member"), None),
            P(("group", "member")),
            P(),
            P(),
            P(None, ("group", "member"), None),
            P(None, None, ("group", "member"), None),
            P(None, None, ("group", "member"), None),
            P(None, None, ("group", "member"), None),
            P(None, None, ("group", "member"), None),
        ),
        out_specs=P(("group", "member"), None),
        check_vma=False,
    )
```

```python
import functools

import jax
import jax.numpy as jnp
from jax import lax
from jax.experimental import pallas as pl
from jax.experimental.pallas import tpu as pltpu
from jax.sharding import PartitionSpec as P

F32 = jnp.float32
BF16 = jnp.bfloat16
I32 = jnp.int32
VMEM = pl.BlockSpec(memory_space=pltpu.VMEM)
SMEM = pl.BlockSpec(memory_space=pltpu.SMEM)
HBM = pl.BlockSpec(memory_space=pltpu.HBM)
DMA = pltpu.SemaphoreType.DMA


def iota(shape, dim):
    return lax.broadcasted_iota(I32, shape, dim)


def hot(mask):
    return jnp.where(mask, 1.0, 0.0).astype(BF16)


def dot(a, b, over=(1, 0)):
    return lax.dot_general(
        a, b, (((over[0],), (over[1],)), ((), ())), preferred_element_type=F32
    )


def call(kernel, outs, ins, args, flops, moved, limit, scratch=(), **more):
    return pl.pallas_call(
        kernel,
        out_shape=outs,
        in_specs=ins,
        out_specs=more.pop("out_specs", [VMEM] * len(outs)),
        scratch_shapes=scratch,
        cost_estimate=pl.CostEstimate(flops=flops, bytes_accessed=moved, transcendentals=0),
        compiler_params=pltpu.CompilerParams(vmem_limit_bytes=limit << 20),
        **more,
    )(*args)


def partner(block, axis, apart):
    count = lax.axis_size(axis)
    route = []
    for low in range(count):
        high = low | 1 << apart
        if high != low and high < count:
            route += [(low, high), (high, low)]
    return lax.ppermute(block, axis, route)


def far(*arrays):
    return [pltpu.with_memory_space_constraint(array, pltpu.HBM) for array in arrays]


def turn(block):
    half = block.shape[1] // 2
    return jnp.where(iota(block.shape, 1) < half, -1.0, 1.0) * pltpu.roll(block, half, 1)


def pack_kernel(leaves, bucket, sizes_in, position_in, rows_in, packed, places, *scratch):
    sizes, position, rows, ordered, sems = scratch
    copies = [
        pltpu.make_async_copy(source, target, sems.at[i])
        for i, (source, target) in enumerate(
            [(sizes_in, sizes), (position_in, position), (rows_in, rows)]
        )
    ]
    for copy in copies:
        copy.start()
    for copy in copies[:2]:
        copy.wait()
    count = rows.shape[0]
    padded = packed.shape[1]
    shift = leaves.bit_length() - 1
    here = position[...]
    window = jnp.right_shift(here, shift)
    zero = jnp.zeros((1, count), I32)
    owner, first = zero, zero
    starts = [0]
    for c in range(leaves):
        starts.append(starts[-1] + jnp.right_shift(sizes[c], shift))
        beyond = window >= starts[-1]
        owner = owner + beyond.astype(I32)
        first = jnp.where(beyond, starts[-1], first)
    offset = jnp.bitwise_and(here, leaves - 1).astype(F32)
    picked = jnp.where(iota((leaves, count), 0) == owner, offset, 0.0).astype(BF16)
    offsets = dot(picked, hot(iota((128, count), 0) == window - first), (1, 1))
    places[...] = jnp.transpose(jnp.broadcast_to(owner * bucket + window - first, (128, count)))
    copies[2].wait()
    values = rows[...]
    block = 256
    for low in range(0, count, block):
        ordered[low : low + block, :] = dot(hot(iota((block, count), 0) + low == window), values)
    ordered[count:, :] = jnp.zeros((padded, 128), F32)
    line = iota((padded, 128), 0)
    for c in range(leaves):
        data = ordered[pl.ds(starts[c], padded), :]
        data = jnp.where(line < starts[c + 1] - starts[c], data, 0.0)
        data = jnp.where(line == bucket, offsets[c : c + 1, :], data)
        packed[c] = data.astype(BF16)


def near_kernel(source, target, sem):
    copy = pltpu.make_async_copy(source, target, sem)
    copy.start()
    copy.wait()


def stage_kernel(left_top_in, left_low_in, targets, places, after, *rest):
    left_top, left_low, slots, order, raw, sems = rest
    copies = [
        pltpu.make_async_copy(left_low_in, raw, sems.at[0]),
        pltpu.make_async_copy(left_top_in, left_top, sems.at[1]),
    ]
    for copy in copies:
        copy.start()
    groups, part = targets.shape
    lanes = iota((part, 128), 1)
    for g in range(groups):
        target = jnp.transpose(jnp.broadcast_to(targets[g : g + 1, :], (128, part)))
        for low in range(0, part, 128):
            slots[g * part : (g + 1) * part, low : low + 128] = hot(target == lanes + low)
    count, slots_out = order.shape
    block = 256
    lanes = iota((block, 128), 1)
    for low in range(0, count, block):
        place = places[low : low + block, :]
        for at in range(0, slots_out, 128):
            order[low : low + block, at : at + 128] = hot(place == lanes + at)
    copies[0].wait()
    levels, parts, width, capacity = raw.shape
    left_low[...] = jnp.transpose(raw[...].reshape(levels * parts * width, capacity))
    copies[1].wait()


def field_kernel(leaves, bucket, place, arrived, right_top, right_low_in, *rest):
    pair, targets, send, keep, whole, right_low, sem = rest
    copy = pltpu.make_async_copy(right_low_in, right_low, sem)
    copy.start()
    capacity = leaves * bucket
    padded = arrived.shape[1]
    part = leaves * 8
    core = jnp.bitwise_and(place[0], 1)
    last = arrived[:, padded - 16 :, :].reshape(leaves * 16, 128)
    carrier = iota((leaves, leaves * 16), 1) == iota((leaves, leaves * 16), 0) * 16 + bucket % 16
    offsets = dot(hot(carrier), last).astype(BF16)
    spread = hot(jnp.right_shift(iota((leaves, part), 1), 3) == iota((leaves, part), 0))
    spread_offsets = dot(offsets, spread, (0, 0))
    lane_window = jnp.bitwise_and(iota((8, part), 1), 7)
    own = lane_window == iota((8, part), 0)
    for g in range(padded // 8):
        size = min(part, capacity - g * part)
        if size <= 0:
            continue
        rows = spread_offsets[g * 8 : g * 8 + 8, :]
        offset = jnp.sum(jnp.where(own, rows, 0.0), axis=0, keepdims=True).astype(I32)
        target = offset + lane_window[:1, :] * leaves
        targets[g : g + 1, :] = target
        if g % 2 == 0:
            both = arrived[:, g * 8 : g * 8 + 16, :].astype(F32)
        chunk = both[:, g % 2 * 8 : g % 2 * 8 + 8, :].reshape(part, 128).astype(BF16)
        placed = dot(hot(iota((part, part), 0) == target), chunk)
        pair[0, g * part : g * part + size, :] = placed[:size].astype(BF16)
        pair[1, g * part : g * part + size, :] = turn(placed)[:size].astype(BF16)
    copy.wait()
    levels, _, width, _ = right_low.shape
    top_levels, _, _, top_width = right_top.shape
    total = jnp.zeros((levels * width, 128), F32)
    tops = jnp.zeros((128, top_levels * top_width), F32)
    for p in range(2):
        total += dot(right_low[:, p].reshape(levels * width, capacity), pair[p])
        factors = jnp.concatenate([right_top[level, p] for level in range(top_levels)], axis=1)
        tops += dot(jnp.transpose(pair[p]), factors)
    for level in range(top_levels):
        whole[level * 128 : (level + 1) * 128, :] = tops[:, level * top_width : (level + 1) * top_width]
    whole[top_levels * 128 :, :] = total
    at = 0
    for low, half in segments(top_levels, levels, width):
        mine = pl.multiple_of(low + core * half, 8)
        other = pl.multiple_of(low + (1 - core) * half, 8)
        keep[at : at + half, :] = whole[pl.ds(mine, half), :]
        send[at : at + half, :] = whole[pl.ds(other, half), :]
        at += half
    send[at:, :] = total[(levels - 1) * width :]


def segments(top_levels, levels, width):
    tops = [(level * 128, 64) for level in range(top_levels)]
    return tops + [(top_levels * 128 + level * width, width // 2) for level in range(levels - 1)]


def diag_kernel(first, block_in, pair, after, out, block, sems):
    count, _, height, _ = block.shape
    copies = []
    for j in range(count):
        rows = pl.ds((first + j) * height, height)
        copies.append(pltpu.make_async_copy(block_in.at[:, rows, :], block.at[j], sems.at[j]))
        copies[j].start()
    for j in range(count):
        copies[j].wait()
        out[j * height : (j + 1) * height, :] = dot(block[j, 0], pair[0]) + dot(block[j, 1], pair[1])


def merged(core, own, theirs, at, half):
    a, b = own[at : at + half, :].astype(F32), theirs[at : at + half, :].astype(F32)
    return jnp.concatenate([jnp.where(core == 0, a, b), jnp.where(core == 0, b, a)], axis=0)


def low_kernel(pieces, place, *rest):
    bases = rest[:pieces]
    left_low, nearest, own, theirs, out = rest[pieces:]
    width = nearest.shape[0]
    levels = left_low.shape[1] // (2 * width)
    tops = place.shape[0] - 1 - levels
    core = jnp.bitwise_and(place[0], 1)
    half = width // 2
    stacked = []
    for level in range(levels):
        if level < levels - 1:
            coef = merged(core, own, theirs, level * half, half)
        else:
            coef = nearest[...]
        coef = jnp.where(iota(coef.shape, 0) < place[1 + tops + level], coef, 0.0)
        stacked += [coef, turn(coef)]
    stacked = jnp.concatenate(stacked, axis=0).astype(BF16)
    low = 0
    for base in bases:
        rows = slice(low, low + base.shape[0])
        out[rows, :] = base[...] + dot(left_low[rows, :], stacked)
        low += base.shape[0]


def out_kernel(bucket, place, base, left_top, own, theirs, slots, packed, spare, ordered):
    capacity = base.shape[0]
    part = slots.shape[1]
    groups = slots.shape[0] // part
    leaves = part // 8
    core = jnp.bitwise_and(place[0], 1)
    levels = left_top.shape[0]
    half = own.shape[0] // levels
    stacked = []
    for level in range(levels):
        coef = merged(core, own, theirs, level * half, half)
        coef = jnp.where(iota(coef.shape, 1) < place[1 + level], coef, 0.0)
        turned = jnp.concatenate([-coef[half:], coef[:half]], axis=0)
        stacked += [jnp.transpose(coef), jnp.transpose(turned)]
    stacked = jnp.concatenate(stacked, axis=0).astype(BF16)
    if groups * part > capacity:
        spare[capacity:, :] = jnp.zeros((groups * part - capacity, 128), BF16)
    factors = [left_top[level, p] for level in range(levels) for p in range(2)]
    total = base[...] + dot(jnp.concatenate(factors, axis=1), stacked)
    spare[:capacity, :] = total.astype(BF16)
    for g in range(groups):
        moved = dot(slots[g * part : (g + 1) * part, :], spare[g * part : (g + 1) * part, :])
        ordered[:, g * 8 : g * 8 + 8, :] = moved.reshape(leaves, 8, 128)
    packed[...] = ordered[:, :bucket, :].reshape(capacity, 128).astype(BF16)


def unpack_kernel(order, returned, out, near, sems):
    count = order.shape[0]
    block = 256
    copies = []
    for low in range(0, count, block):
        rows = pl.ds(low, block)
        near[rows, :] = dot(order[low : low + block, :], returned[...])
        copies.append(pltpu.make_async_copy(near.at[rows, :], out.at[rows, :], sems.at[low // block]))
        copies[-1].start()
    for copy in copies:
        copy.wait()


def on_device(
    mesh_vector,
    cluster_position,
    cluster_sizes,
    block_ranks,
    diag_block,
    top_left,
    top_right,
    low_left,
    low_right,
):
    groups = lax.axis_size("group")
    members = lax.axis_size("member")
    leaves = groups * members
    group_levels = groups.bit_length() - 1
    member_levels = members.bit_length() - 1
    levels = group_levels + member_levels
    device = lax.axis_index("group") * members + lax.axis_index("member")
    capacity = diag_block.shape[1]
    bucket = capacity // leaves
    padded = (bucket + 16) // 16 * 16
    filled = (bucket + 7) // 8 * 8
    count, columns = mesh_vector.shape
    everyone = ("group", "member")
    low_left = jnp.swapaxes(low_left, 2, 3)
    low_right = jnp.swapaxes(low_right, 2, 3)
    width = low_left.shape[2]
    top_width = top_left.shape[3]
    far_flops = 4 * capacity * columns * (group_levels * top_width + member_levels * width)

    level_ids = jnp.arange(1, levels + 1, dtype=I32)
    ranks = block_ranks[(1 << level_ids) - 2 + jnp.right_shift(device, levels - level_ids)]
    place = jnp.concatenate([device[None].astype(I32), ranks])

    packed, places = call(
        functools.partial(pack_kernel, leaves, bucket),
        [
            jax.ShapeDtypeStruct((leaves, padded, columns), BF16),
            jax.ShapeDtypeStruct((count, 128), I32),
        ],
        [HBM] * 3,
        far(cluster_sizes, cluster_position.reshape(1, count), mesh_vector),
        2 * count * count * columns,
        4 << 20,
        16,
        scratch=[
            pltpu.SMEM((leaves,), I32),
            pltpu.VMEM((1, count), I32),
            pltpu.VMEM((count, columns), BF16),
            pltpu.VMEM((count + padded, columns), F32),
            DMA((3,)),
        ],
    )
    arrived = lax.all_to_all(packed, everyone, split_axis=0, concat_axis=0, tiled=True)
    right_top = call(
        near_kernel,
        [pltpu.VMEM(top_right.shape, BF16)],
        [HBM],
        far(top_right),
        0,
        4 << 20,
        16,
        scratch=[DMA],
    )[0]
    shared = group_levels * columns // 2 + (member_levels - 1) * width // 2
    pair, targets, send, keep = call(
        functools.partial(field_kernel, leaves, bucket),
        [
            jax.ShapeDtypeStruct((2, capacity, columns), BF16),
            jax.ShapeDtypeStruct((filled // 8, leaves * 8), I32),
            jax.ShapeDtypeStruct((shared + width, columns), F32),
            jax.ShapeDtypeStruct((shared, columns), F32),
        ],
        [SMEM, VMEM, VMEM, HBM],
        (place, arrived, right_top, *far(low_right)),
        far_flops,
        6 << 20,
        24,
        scratch=[
            pltpu.VMEM((group_levels * columns + member_levels * width, columns), F32),
            pltpu.VMEM(low_right.shape, BF16),
            DMA,
        ],
    )
    height = capacity // 8

    def diagonal(first, chunks, after):
        return call(
            functools.partial(diag_kernel, first),
            [jax.ShapeDtypeStruct((chunks * height, columns), F32)],
            [HBM, VMEM, pl.BlockSpec(memory_space=pl.ANY)],
            (*far(diag_block), pair, after),
            4 * chunks * height * capacity * columns,
            4 * chunks * height * capacity,
            24,
            scratch=[pltpu.VMEM((chunks, 2, height, capacity), BF16), DMA((chunks,))],
        )[0]

    received = partner(send, "member", 0)
    nearest = received[shared:]
    running = keep + received[:shared]
    bases = []
    coefs = []
    for bit in range(1, member_levels):
        rest = running.shape[0] - width // 2
        received = partner(running, "member", bit)
        if bit == 1:
            bases.append(diagonal(0, 5, running))
            received, bases[0] = lax.optimization_barrier((received, bases[0]))
        if bit == member_levels - 1:
            bases.append(diagonal(5, 3, running))
            left_top, left_low, slots, order = call(
                stage_kernel,
                [
                    pltpu.VMEM(top_left.shape, BF16),
                    pltpu.VMEM((capacity, member_levels * 2 * width), BF16),
                    jax.ShapeDtypeStruct((leaves * filled, leaves * 8), BF16),
                    jax.ShapeDtypeStruct((count, capacity), BF16),
                ],
                [HBM, HBM, VMEM, VMEM, pl.BlockSpec(memory_space=pl.ANY)],
                (*far(top_left, low_left), targets, places, running),
                0,
                8 << 20,
                24,
                scratch=[pltpu.VMEM(low_left.shape, BF16), DMA((2,))],
            )
            received, bases[1], left_top, left_low, slots, order = lax.optimization_barrier(
                (received, bases[1], left_top, left_low, slots, order)
            )
        coefs.insert(0, received[rest:].astype(BF16))
        running = running[:rest] + received[:rest]
    half = columns // 2
    tops = [None] * group_levels
    for apart in range(1, groups):
        level = group_levels - apart.bit_length()
        sent = running[level * half : (level + 1) * half]
        if apart == 1:
            sent = sent.astype(BF16)
        route = [(low, low ^ apart) for low in range(groups)]
        heard = lax.ppermute(sent, "group", route)
        tops[level] = heard if tops[level] is None else tops[level] + heard
    own_low = jnp.concatenate(coefs)
    base = call(
        functools.partial(low_kernel, len(bases)),
        [jax.ShapeDtypeStruct((capacity, columns), F32)],
        [SMEM] + [VMEM] * (len(bases) + 4),
        (place, *bases, left_low, nearest, own_low, partner(own_low, "member", 0)),
        4 * capacity * columns * member_levels * width,
        3 << 20,
        16,
    )[0]
    own = jnp.concatenate([top.astype(BF16) for top in tops])
    own, base = lax.optimization_barrier((own, base))
    theirs = partner(own, "member", 0)

    leaving = call(
        functools.partial(out_kernel, bucket),
        [jax.ShapeDtypeStruct((capacity, columns), BF16)],
        [SMEM] + [VMEM] * 5,
        (place, base, left_top, own, theirs, slots),
        4 * capacity * columns * group_levels * top_width,
        4 << 20,
        24,
        scratch=[
            pltpu.VMEM((leaves * filled, 128), BF16),
            pltpu.VMEM((leaves, filled, 128), F32),
        ],
    )[0]
    returned = lax.all_to_all(
        leaving.reshape(leaves, bucket, columns), everyone, split_axis=0, concat_axis=0, tiled=True
    )
    return call(
        unpack_kernel,
        [jax.ShapeDtypeStruct((count, columns), F32)],
        [VMEM] * 2,
        (order, returned.reshape(capacity, columns)),
        2 * capacity * count * columns,
        4 << 20,
        16,
        out_specs=[HBM],
        scratch=[pltpu.VMEM((count, 128), F32), DMA((count // 256,))],
    )[0]


def solution(mesh):
    return jax.shard_map(
        on_device,
        mesh=mesh,
        in_specs=(
            P(("group", "member"), None),
            P(("group", "member")),
            P(),
            P(),
            P(None, ("group", "member"), None),
            P(None, None, ("group", "member"), None),
            P(None, None, ("group", "member"), None),
            P(None, None, ("group", "member"), None),
            P(None, None, ("group", "member"), None),
        ),
        out_specs=P(("group", "member"), None),
        check_vma=False,
    )
```

```python
import functools

import jax
import jax.numpy as jnp
from jax import lax
from jax.experimental import pallas as pl
from jax.experimental.pallas import tpu as pltpu
from jax.sharding import PartitionSpec as P

F32 = jnp.float32
BF16 = jnp.bfloat16
I32 = jnp.int32
VMEM = pl.BlockSpec(memory_space=pltpu.VMEM)
SMEM = pl.BlockSpec(memory_space=pltpu.SMEM)
HBM = pl.BlockSpec(memory_space=pltpu.HBM)
DMA = pltpu.SemaphoreType.DMA


def iota(shape, dim):
    return lax.broadcasted_iota(I32, shape, dim)


def hot(mask):
    return jnp.where(mask, 1.0, 0.0).astype(BF16)


def dot(a, b, over=(1, 0)):
    return lax.dot_general(
        a, b, (((over[0],), (over[1],)), ((), ())), preferred_element_type=F32
    )


def call(kernel, outs, ins, args, flops, moved, limit, scratch=(), **more):
    return pl.pallas_call(
        kernel,
        out_shape=outs,
        in_specs=ins,
        out_specs=more.pop("out_specs", [VMEM] * len(outs)),
        scratch_shapes=scratch,
        cost_estimate=pl.CostEstimate(flops=flops, bytes_accessed=moved, transcendentals=0),
        compiler_params=pltpu.CompilerParams(vmem_limit_bytes=limit << 20),
        **more,
    )(*args)


def partner(block, axis, apart):
    count = lax.axis_size(axis)
    route = []
    for low in range(count):
        high = low | 1 << apart
        if high != low and high < count:
            route += [(low, high), (high, low)]
    return lax.ppermute(block, axis, route)


def far(*arrays):
    return [pltpu.with_memory_space_constraint(array, pltpu.HBM) for array in arrays]


def turn(block):
    half = block.shape[1] // 2
    return jnp.where(iota(block.shape, 1) < half, -1.0, 1.0) * pltpu.roll(block, half, 1)


def pack_kernel(leaves, bucket, sizes_in, position_in, rows_in, packed, places, *scratch):
    sizes, position, rows, ordered, near, sems, out_sems = scratch
    copies = [
        pltpu.make_async_copy(source, target, sems.at[i])
        for i, (source, target) in enumerate(
            [(position_in, position), (rows_in, rows), (sizes_in, sizes)]
        )
    ]
    for copy in copies:
        copy.start()
    copies[0].wait()
    count = rows.shape[0]
    padded = packed.shape[1]
    shift = leaves.bit_length() - 1
    here = position[...]
    window = jnp.right_shift(here, shift)
    copies[1].wait()
    values = rows[...]
    block = 512
    for low in range(0, count, block):
        ordered[low : low + block, :] = dot(hot(iota((block, count), 0) + low == window), values)
    ordered[count:, :] = jnp.zeros((padded, 128), F32)
    copies[2].wait()
    zero = jnp.zeros((1, count), I32)
    owner, first = zero, zero
    starts = [0]
    for c in range(leaves):
        starts.append(starts[-1] + jnp.right_shift(sizes[c], shift))
        beyond = window >= starts[-1]
        owner = owner + beyond.astype(I32)
        first = jnp.where(beyond, starts[-1], first)
    offset = jnp.bitwise_and(here, leaves - 1).astype(F32)
    picked = jnp.where(iota((leaves, count), 0) == owner, offset, 0.0).astype(BF16)
    offsets = dot(picked, hot(iota((128, count), 0) == window - first), (1, 1))
    places[...] = owner * bucket + window - first
    line = iota((padded, 128), 0)
    chunk = leaves // 4
    out = []
    for c in range(leaves):
        data = ordered[pl.ds(starts[c], padded), :]
        data = jnp.where(line < starts[c + 1] - starts[c], data, 0.0)
        data = jnp.where(line == bucket, offsets[c : c + 1, :], data)
        near[c] = data.astype(BF16)
        if c % chunk == chunk - 1:
            part = pl.ds(c + 1 - chunk, chunk)
            out.append(pltpu.make_async_copy(near.at[part], packed.at[part], out_sems.at[c // chunk]))
            out[-1].start()
    for copy in out:
        copy.wait()


def near_kernel(right_top_in, right_low_in, right, raw, sems):
    tops, _, _, top_width = right_top_in.shape
    levels, _, width, _ = right_low_in.shape
    copies = [pltpu.make_async_copy(right_top_in, raw, sems.at[0])]
    for level in range(levels):
        low = tops * top_width + level * width
        for p in range(2):
            target = right.at[p, pl.ds(low, width), :]
            sem = sems.at[1 + 2 * level + p]
            copies.append(pltpu.make_async_copy(right_low_in.at[level, p], target, sem))
    for copy in copies:
        copy.start()
    copies[0].wait()
    for level in range(tops):
        for p in range(2):
            right[p, level * top_width : (level + 1) * top_width, :] = jnp.transpose(raw[level, p])
    for copy in copies[1:]:
        copy.wait()


def way_kernel(targets, places, after, slots, order):
    groups, part = targets.shape
    lanes = iota((part, 128), 1)
    for g in range(groups):
        target = jnp.transpose(jnp.broadcast_to(targets[g : g + 1, :], (128, part)))
        for low in range(0, part, 128):
            slots[g * part : (g + 1) * part, low : low + 128] = hot(target == lanes + low)
    count, slots_out = order.shape
    place = jnp.transpose(jnp.broadcast_to(places[...], (128, count)))
    block = 256
    lanes = iota((block, 128), 1)
    for low in range(0, count, block):
        for at in range(0, slots_out, 128):
            order[low : low + block, at : at + 128] = hot(place[low : low + block] == lanes + at)


def stage_kernel(left_top_in, left_low_in, after, left_top, left_low, raw, sems):
    copies = [
        pltpu.make_async_copy(left_low_in, raw, sems.at[0]),
        pltpu.make_async_copy(left_top_in, left_top, sems.at[1]),
    ]
    for copy in copies:
        copy.start()
    copies[0].wait()
    levels, parts, width, capacity = raw.shape
    left_low[...] = jnp.transpose(raw[...].reshape(levels * parts * width, capacity))
    copies[1].wait()


def field_kernel(leaves, bucket, tops, levels, place, arrived, right, *rest):
    pair, targets, send, keep, whole = rest
    capacity = leaves * bucket
    padded = arrived.shape[1]
    part = leaves * 8
    core = jnp.bitwise_and(place[0], 1)
    last = arrived[:, padded - 16 :, :].reshape(leaves * 16, 128)
    carrier = iota((leaves, leaves * 16), 1) == iota((leaves, leaves * 16), 0) * 16 + bucket % 16
    offsets = dot(hot(carrier), last).astype(BF16)
    spread = hot(jnp.right_shift(iota((leaves, part), 1), 3) == iota((leaves, part), 0))
    spread_offsets = dot(offsets, spread, (0, 0))
    lane_window = jnp.bitwise_and(iota((8, part), 1), 7)
    own = lane_window == iota((8, part), 0)
    for g in range(padded // 8):
        size = min(part, capacity - g * part)
        if size <= 0:
            continue
        rows = spread_offsets[g * 8 : g * 8 + 8, :]
        offset = jnp.sum(jnp.where(own, rows, 0.0), axis=0, keepdims=True).astype(I32)
        target = offset + lane_window[:1, :] * leaves
        targets[g : g + 1, :] = target
        if g % 2 == 0:
            both = arrived[:, g * 8 : g * 8 + 16, :].astype(F32)
        chunk = both[:, g % 2 * 8 : g % 2 * 8 + 8, :].reshape(part, 128).astype(BF16)
        placed = dot(hot(iota((part, part), 0) == target), chunk)
        pair[0, g * part : g * part + size, :] = placed[:size].astype(BF16)
        pair[1, g * part : g * part + size, :] = turn(placed)[:size].astype(BF16)
    whole[...] = dot(right[0], pair[0]) + dot(right[1], pair[1])
    at = 0
    for low, half in segments(tops, levels):
        mine = pl.multiple_of(low + core * half, 8)
        other = pl.multiple_of(low + (1 - core) * half, 8)
        keep[at : at + half, :] = whole[pl.ds(mine, half), :]
        send[at : at + half, :] = whole[pl.ds(other, half), :]
        at += half
    send[at:, :] = whole[whole.shape[0] + at - send.shape[0] :, :]


def segments(tops, lows):
    found, low = [], 0
    for count, width in (tops, (lows[0] - 1, lows[1])):
        for _ in range(count):
            found.append((low, width // 2))
            low += width
    return found


def diag_kernel(first, block_in, pair, after, out, block, sems):
    count, _, height, _ = block.shape
    copies = []
    for j in range(count):
        rows = pl.ds((first + j) * height, height)
        copies.append(pltpu.make_async_copy(block_in.at[:, rows, :], block.at[j], sems.at[j]))
        copies[j].start()
    for j in range(count):
        copies[j].wait()
        out[j * height : (j + 1) * height, :] = dot(block[j, 0], pair[0]) + dot(block[j, 1], pair[1])


def merged(core, own, theirs, at, half):
    a, b = own[at : at + half, :].astype(F32), theirs[at : at + half, :].astype(F32)
    return jnp.concatenate([jnp.where(core == 0, a, b), jnp.where(core == 0, b, a)], axis=0)


def low_kernel(pieces, place, *rest):
    bases = rest[:pieces]
    left_low, nearest, own, theirs, out = rest[pieces:]
    width = nearest.shape[0]
    levels = left_low.shape[1] // (2 * width)
    tops = place.shape[0] - 1 - levels
    core = jnp.bitwise_and(place[0], 1)
    half = width // 2
    stacked = []
    for level in range(levels):
        if level < levels - 1:
            coef = merged(core, own, theirs, level * half, half)
        else:
            coef = nearest[...]
        coef = jnp.where(iota(coef.shape, 0) < place[1 + tops + level], coef, 0.0)
        stacked += [coef, turn(coef)]
    stacked = jnp.concatenate(stacked, axis=0).astype(BF16)
    low = 0
    for base in bases:
        rows = slice(low, low + base.shape[0])
        out[rows, :] = base[...] + dot(left_low[rows, :], stacked)
        low += base.shape[0]


def out_kernel(bucket, place, base, left_top, own, theirs, slots, packed, spare, ordered):
    capacity = base.shape[0]
    part = slots.shape[1]
    groups = slots.shape[0] // part
    leaves = part // 8
    core = jnp.bitwise_and(place[0], 1)
    levels = left_top.shape[0]
    half = own.shape[0] // levels
    stacked = []
    for level in range(levels):
        coef = merged(core, own, theirs, level * half, half)
        coef = jnp.where(iota(coef.shape, 0) < place[1 + level], coef, 0.0)
        stacked += [coef, turn(coef)]
    stacked = jnp.concatenate(stacked, axis=0).astype(BF16)
    if groups * part > capacity:
        spare[capacity:, :] = jnp.zeros((groups * part - capacity, 128), BF16)
    factors = [left_top[level, p] for level in range(levels) for p in range(2)]
    total = base[...] + dot(jnp.concatenate(factors, axis=1), stacked)
    spare[:capacity, :] = total.astype(BF16)
    for g in range(groups):
        moved = dot(slots[g * part : (g + 1) * part, :], spare[g * part : (g + 1) * part, :])
        ordered[:, g * 8 : g * 8 + 8, :] = moved.reshape(leaves, 8, 128)
    packed[...] = ordered[:, :bucket, :].reshape(capacity, 128).astype(BF16)


def unpack_kernel(order, returned, out, near, sems):
    count = order.shape[0]
    block = 512
    copies = []
    for low in range(0, count, block):
        rows = pl.ds(low, block)
        near[rows, :] = dot(order[low : low + block, :], returned[...])
        copies.append(pltpu.make_async_copy(near.at[rows, :], out.at[rows, :], sems.at[low // block]))
        copies[-1].start()
    for copy in copies:
        copy.wait()


def on_device(
    mesh_vector,
    cluster_position,
    cluster_sizes,
    block_ranks,
    diag_block,
    top_left,
    top_right,
    low_left,
    low_right,
):
    groups = lax.axis_size("group")
    members = lax.axis_size("member")
    leaves = groups * members
    group_levels = groups.bit_length() - 1
    member_levels = members.bit_length() - 1
    levels = group_levels + member_levels
    device = lax.axis_index("group") * members + lax.axis_index("member")
    capacity = diag_block.shape[1]
    bucket = capacity // leaves
    padded = (bucket + 16) // 16 * 16
    filled = (bucket + 7) // 8 * 8
    count, columns = mesh_vector.shape
    everyone = ("group", "member")
    low_left = jnp.swapaxes(low_left, 2, 3)
    low_right = jnp.swapaxes(low_right, 2, 3)
    width = low_left.shape[2]
    top_width = top_left.shape[3]
    far_flops = 4 * capacity * columns * (group_levels * top_width + member_levels * width)

    level_ids = jnp.arange(1, levels + 1, dtype=I32)
    ranks = block_ranks[(1 << level_ids) - 2 + jnp.right_shift(device, levels - level_ids)]
    place = jnp.concatenate([device[None].astype(I32), ranks])

    packed, places = call(
        functools.partial(pack_kernel, leaves, bucket),
        [
            jax.ShapeDtypeStruct((leaves, padded, columns), BF16),
            jax.ShapeDtypeStruct((1, count), I32),
        ],
        [HBM] * 3,
        far(cluster_sizes, cluster_position.reshape(1, count), mesh_vector),
        2 * count * count * columns,
        4 << 20,
        16,
        out_specs=[HBM, VMEM],
        scratch=[
            pltpu.SMEM((leaves,), I32),
            pltpu.VMEM((1, count), I32),
            pltpu.VMEM((count, columns), BF16),
            pltpu.VMEM((count + padded, columns), F32),
            pltpu.VMEM((leaves, padded, columns), BF16),
            DMA((3,)),
            DMA((4,)),
        ],
    )
    arrived = lax.all_to_all(packed, everyone, split_axis=0, concat_axis=0, tiled=True)
    tops = (group_levels, top_width)
    lows = (member_levels, width)
    ranked = group_levels * top_width + member_levels * width
    right = call(
        near_kernel,
        [pltpu.VMEM((2, ranked, capacity), BF16)],
        [HBM] * 2,
        far(top_right, low_right),
        0,
        6 << 20,
        16,
        scratch=[pltpu.VMEM(top_right.shape, BF16), DMA((1 + 2 * member_levels,))],
    )[0]
    shared = (ranked - width) // 2
    pair, targets, send, keep = call(
        functools.partial(field_kernel, leaves, bucket, tops, lows),
        [
            jax.ShapeDtypeStruct((2, capacity, columns), BF16),
            jax.ShapeDtypeStruct((filled // 8, leaves * 8), I32),
            jax.ShapeDtypeStruct((shared + width, columns), F32),
            jax.ShapeDtypeStruct((shared, columns), F32),
        ],
        [SMEM, VMEM, VMEM],
        (place, arrived, right),
        far_flops,
        6 << 20,
        24,
        scratch=[pltpu.VMEM((ranked, columns), F32)],
    )
    height = capacity // 8

    def diagonal(first, chunks, after):
        return call(
            functools.partial(diag_kernel, first),
            [jax.ShapeDtypeStruct((chunks * height, columns), F32)],
            [HBM, VMEM, pl.BlockSpec(memory_space=pl.ANY)],
            (*far(diag_block), pair, after),
            4 * chunks * height * capacity * columns,
            4 * chunks * height * capacity,
            24,
            scratch=[pltpu.VMEM((chunks, 2, height, capacity), BF16), DMA((chunks,))],
        )[0]

    received = partner(send, "member", 0)
    slots, order = call(
        way_kernel,
        [
            jax.ShapeDtypeStruct((leaves * filled, leaves * 8), BF16),
            jax.ShapeDtypeStruct((count, capacity), BF16),
        ],
        [VMEM, VMEM, pl.BlockSpec(memory_space=pl.ANY)],
        (targets, places, send),
        0,
        8 << 20,
        16,
    )
    received, slots, order = lax.optimization_barrier((received, slots, order))
    nearest = received[shared:]
    running = keep + received[:shared]
    bases = []
    coefs = []
    for bit in range(1, member_levels):
        rest = running.shape[0] - width // 2
        received = partner(running, "member", bit)
        if bit == 1:
            bases.append(diagonal(0, 5, running))
            received, bases[0] = lax.optimization_barrier((received, bases[0]))
        if bit == member_levels - 1:
            bases.append(diagonal(5, 3, running))
            left_top, left_low = call(
                stage_kernel,
                [
                    pltpu.VMEM(top_left.shape, BF16),
                    pltpu.VMEM((capacity, member_levels * 2 * width), BF16),
                ],
                [HBM, HBM, pl.BlockSpec(memory_space=pl.ANY)],
                (*far(top_left, low_left), running),
                0,
                8 << 20,
                24,
                scratch=[pltpu.VMEM(low_left.shape, BF16), DMA((2,))],
            )
            received, bases[1], left_top, left_low = lax.optimization_barrier(
                (received, bases[1], left_top, left_low)
            )
        coefs.insert(0, received[rest:].astype(BF16))
        running = running[:rest] + received[:rest]
    half = top_width // 2
    tops = [None] * group_levels
    for apart in range(1, groups):
        level = group_levels - apart.bit_length()
        sent = running[level * half : (level + 1) * half]
        if apart == 1:
            sent = sent.astype(BF16)
        route = [(low, low ^ apart) for low in range(groups)]
        heard = lax.ppermute(sent, "group", route)
        tops[level] = heard if tops[level] is None else tops[level] + heard
    own_low = jnp.concatenate(coefs)
    base = call(
        functools.partial(low_kernel, len(bases)),
        [jax.ShapeDtypeStruct((capacity, columns), F32)],
        [SMEM] + [VMEM] * (len(bases) + 4),
        (place, *bases, left_low, nearest, own_low, partner(own_low, "member", 0)),
        4 * capacity * columns * member_levels * width,
        3 << 20,
        16,
    )[0]
    own = jnp.concatenate([top.astype(BF16) for top in tops])
    own, base = lax.optimization_barrier((own, base))
    theirs = partner(own, "member", 0)

    leaving = call(
        functools.partial(out_kernel, bucket),
        [jax.ShapeDtypeStruct((capacity, columns), BF16)],
        [SMEM] + [VMEM] * 5,
        (place, base, left_top, own, theirs, slots),
        4 * capacity * columns * group_levels * top_width,
        4 << 20,
        24,
        scratch=[
            pltpu.VMEM((leaves * filled, 128), BF16),
            pltpu.VMEM((leaves, filled, 128), F32),
        ],
    )[0]
    returned = lax.all_to_all(
        leaving.reshape(leaves, bucket, columns), everyone, split_axis=0, concat_axis=0, tiled=True
    )
    return call(
        unpack_kernel,
        [jax.ShapeDtypeStruct((count, columns), F32)],
        [VMEM] * 2,
        (order, returned.reshape(capacity, columns)),
        2 * capacity * count * columns,
        4 << 20,
        16,
        out_specs=[HBM],
        scratch=[pltpu.VMEM((count, 128), F32), DMA((count // 512,))],
    )[0]


def solution(mesh):
    return jax.shard_map(
        on_device,
        mesh=mesh,
        in_specs=(
            P(("group", "member"), None),
            P(("group", "member")),
            P(),
            P(),
            P(None, ("group", "member"), None),
            P(None, None, ("group", "member"), None),
            P(None, None, ("group", "member"), None),
            P(None, None, ("group", "member"), None),
            P(None, None, ("group", "member"), None),
        ),
        out_specs=P(("group", "member"), None),
        check_vma=False,
    )
```

```python
import functools

import jax
import jax.numpy as jnp
from jax import lax
from jax.experimental import pallas as pl
from jax.experimental.pallas import tpu as pltpu
from jax.sharding import PartitionSpec as P

F32 = jnp.float32
BF16 = jnp.bfloat16
I32 = jnp.int32
VMEM = pl.BlockSpec(memory_space=pltpu.VMEM)
SMEM = pl.BlockSpec(memory_space=pltpu.SMEM)
HBM = pl.BlockSpec(memory_space=pltpu.HBM)
DMA = pltpu.SemaphoreType.DMA


def iota(shape, dim):
    return lax.broadcasted_iota(I32, shape, dim)


def hot(mask):
    return jnp.where(mask, 1.0, 0.0).astype(BF16)


def dot(a, b, over=(1, 0)):
    return lax.dot_general(
        a, b, (((over[0],), (over[1],)), ((), ())), preferred_element_type=F32
    )


def call(kernel, outs, ins, args, flops, moved, limit, scratch=(), **more):
    return pl.pallas_call(
        kernel,
        out_shape=outs,
        in_specs=ins,
        out_specs=more.pop("out_specs", [VMEM] * len(outs)),
        scratch_shapes=scratch,
        cost_estimate=pl.CostEstimate(flops=flops, bytes_accessed=moved, transcendentals=0),
        compiler_params=pltpu.CompilerParams(vmem_limit_bytes=limit << 20),
        **more,
    )(*args)


def partner(block, axis, apart):
    count = lax.axis_size(axis)
    route = []
    for low in range(count):
        high = low | 1 << apart
        if high != low and high < count:
            route += [(low, high), (high, low)]
    return lax.ppermute(block, axis, route)


def far(*arrays):
    return [pltpu.with_memory_space_constraint(array, pltpu.HBM) for array in arrays]


def turn(block):
    half = block.shape[1] // 2
    return jnp.where(iota(block.shape, 1) < half, -1.0, 1.0) * pltpu.roll(block, half, 1)


def pack_kernel(leaves, bucket, sizes_in, position_in, rows_in, packed, places, *scratch):
    sizes, position, rows, ordered, near, sems, out_sems = scratch
    copies = [
        pltpu.make_async_copy(source, target, sems.at[i])
        for i, (source, target) in enumerate(
            [(position_in, position), (rows_in, rows), (sizes_in, sizes)]
        )
    ]
    for copy in copies:
        copy.start()
    copies[0].wait()
    count = rows.shape[0]
    padded = packed.shape[1]
    shift = leaves.bit_length() - 1
    here = position[...]
    window = jnp.right_shift(here, shift)
    copies[1].wait()
    values = rows[...]
    block = 512
    for low in range(0, count, block):
        ordered[low : low + block, :] = dot(hot(iota((block, count), 0) + low == window), values)
    ordered[count:, :] = jnp.zeros((padded, 128), F32)
    copies[2].wait()
    zero = jnp.zeros((1, count), I32)
    owner, first = zero, zero
    starts = [0]
    for c in range(leaves):
        starts.append(starts[-1] + jnp.right_shift(sizes[c], shift))
        beyond = window >= starts[-1]
        owner = owner + beyond.astype(I32)
        first = jnp.where(beyond, starts[-1], first)
    offset = jnp.bitwise_and(here, leaves - 1).astype(F32)
    picked = jnp.where(iota((leaves, count), 0) == owner, offset, 0.0).astype(BF16)
    offsets = dot(picked, hot(iota((128, count), 0) == window - first), (1, 1))
    places[...] = owner * bucket + window - first
    line = iota((padded, 128), 0)
    chunk = leaves // 4
    out = []
    for c in range(leaves):
        data = ordered[pl.ds(starts[c], padded), :]
        data = jnp.where(line < starts[c + 1] - starts[c], data, 0.0)
        data = jnp.where(line == bucket, offsets[c : c + 1, :], data)
        near[c] = data.astype(BF16)
        if c % chunk == chunk - 1:
            part = pl.ds(c + 1 - chunk, chunk)
            out.append(pltpu.make_async_copy(near.at[part], packed.at[part], out_sems.at[c // chunk]))
            out[-1].start()
    for copy in out:
        copy.wait()


def near_kernel(right_top_in, right_low_in, right, raw, sems):
    tops, _, _, top_width = right_top_in.shape
    levels, _, width, _ = right_low_in.shape
    copies = [pltpu.make_async_copy(right_top_in, raw, sems.at[0])]
    for level in range(levels):
        low = tops * top_width + level * width
        for p in range(2):
            target = right.at[p, pl.ds(low, width), :]
            sem = sems.at[1 + 2 * level + p]
            copies.append(pltpu.make_async_copy(right_low_in.at[level, p], target, sem))
    for copy in copies:
        copy.start()
    copies[0].wait()
    for level in range(tops):
        for p in range(2):
            right[p, level * top_width : (level + 1) * top_width, :] = jnp.transpose(raw[level, p])
    for copy in copies[1:]:
        copy.wait()


def way_kernel(targets, places, after, slots, order, upper):
    groups, part = targets.shape
    lanes = iota((part, 128), 1)
    for g in range(groups):
        target = jnp.transpose(jnp.broadcast_to(targets[g : g + 1, :], (128, part)))
        for low in range(0, part, 128):
            slots[g * part : (g + 1) * part, low : low + 128] = hot(target == lanes + low)
    count, folded = order.shape
    place = jnp.transpose(jnp.broadcast_to(places[...], (128, count)))
    beyond = place >= folded
    upper[...] = beyond.astype(I32)
    place = jnp.where(beyond, place - folded, place)
    block = 256
    lanes = iota((block, 128), 1)
    for low in range(0, count, block):
        for at in range(0, folded, 128):
            order[low : low + block, at : at + 128] = hot(place[low : low + block] == lanes + at)


def stage_kernel(left_top_in, left_low_in, after, left_top, left_low, raw, sems):
    copies = [
        pltpu.make_async_copy(left_low_in, raw, sems.at[0]),
        pltpu.make_async_copy(left_top_in, left_top, sems.at[1]),
    ]
    for copy in copies:
        copy.start()
    copies[0].wait()
    levels, parts, width, capacity = raw.shape
    left_low[...] = jnp.transpose(raw[...].reshape(levels * parts * width, capacity))
    copies[1].wait()


def field_kernel(leaves, bucket, tops, levels, place, arrived, right, *rest):
    pair, targets, send, keep, whole = rest
    capacity = leaves * bucket
    padded = arrived.shape[1]
    part = leaves * 8
    groups = targets.shape[0]
    core = jnp.bitwise_and(place[0], 1)
    last = arrived[:, padded - 16 :, :].reshape(leaves * 16, 128)
    carrier = iota((leaves, leaves * 16), 1) == iota((leaves, leaves * 16), 0) * 16 + bucket % 16
    offsets = dot(hot(carrier), last).astype(BF16)
    spread = hot(jnp.right_shift(iota((leaves, part), 1), 3) == iota((leaves, part), 0))
    spread_offsets = dot(offsets, spread, (0, 0))[: groups * 8].reshape(groups, 8, part)
    lane_window = jnp.bitwise_and(iota((8, part), 1), 7)
    own = (lane_window == iota((8, part), 0))[None]
    target = jnp.sum(jnp.where(own, spread_offsets, 0.0), axis=1).astype(I32)
    target = target + lane_window[:1, :] * leaves
    targets[...] = target
    for g in range(groups):
        size = min(part, capacity - g * part)
        if g % 2 == 0:
            both = arrived[:, g * 8 : g * 8 + 16, :].astype(F32)
        chunk = both[:, g % 2 * 8 : g % 2 * 8 + 8, :].reshape(part, 128).astype(BF16)
        placed = dot(hot(iota((part, part), 0) == target[g : g + 1, :]), chunk)
        pair[0, g * part : g * part + size, :] = placed[:size].astype(BF16)
        pair[1, g * part : g * part + size, :] = turn(placed)[:size].astype(BF16)
    top_rows = tops * 128
    width = (right.shape[1] - top_rows) // levels
    plain = jnp.transpose(pair[0])
    turned = jnp.concatenate([-plain[64:], plain[:64]], axis=0)
    upper = dot(plain, right[0, :top_rows, :], (1, 1)) + dot(turned, right[1, :top_rows, :], (1, 1))
    for level in range(tops):
        whole[level * 128 : (level + 1) * 128, :] = upper[:, level * 128 : (level + 1) * 128]
    lower = dot(right[0, top_rows:, :], pair[0]) + dot(right[1, top_rows:, :], pair[1])
    whole[top_rows:, :] = lower
    at = 0
    low = 0
    for half in [tops * 64] + [width // 2] * (levels - 1):
        mine = pl.multiple_of(low + core * half, 8)
        other = pl.multiple_of(low + (1 - core) * half, 8)
        keep[at : at + half, :] = whole[pl.ds(mine, half), :]
        send[at : at + half, :] = whole[pl.ds(other, half), :]
        at += half
        low += 2 * half
    send[at:, :] = lower[(levels - 1) * width :]


def diag_kernel(first, block_in, pair, after, out, block, sems):
    count, _, height, _ = block.shape
    copies = []
    for j in range(count):
        rows = pl.ds((first + j) * height, height)
        copies.append(pltpu.make_async_copy(block_in.at[:, rows, :], block.at[j], sems.at[j]))
        copies[j].start()
    for j in range(count):
        copies[j].wait()
        out[j * height : (j + 1) * height, :] = dot(block[j, 0], pair[0]) + dot(block[j, 1], pair[1])


def merged(core, own, theirs, at, half):
    a, b = own[at : at + half, :].astype(F32), theirs[at : at + half, :].astype(F32)
    return jnp.concatenate([jnp.where(core == 0, a, b), jnp.where(core == 0, b, a)], axis=0)


def low_kernel(pieces, place, *rest):
    bases = rest[:pieces]
    left_low, nearest, own, theirs, out = rest[pieces:]
    width = nearest.shape[0]
    levels = left_low.shape[1] // (2 * width)
    tops = place.shape[0] - 1 - levels
    core = jnp.bitwise_and(place[0], 1)
    half = width // 2
    stacked = []
    for level in range(levels):
        if level < levels - 1:
            coef = merged(core, own, theirs, level * half, half)
        else:
            coef = nearest[...]
        coef = jnp.where(iota(coef.shape, 0) < place[1 + tops + level], coef, 0.0)
        stacked += [coef, turn(coef)]
    stacked = jnp.concatenate(stacked, axis=0).astype(BF16)
    low = 0
    for base in bases:
        rows = slice(low, low + base.shape[0])
        out[rows, :] = base[...] + dot(left_low[rows, :], stacked)
        low += base.shape[0]


def out_kernel(bucket, place, base, left_top, own, theirs, slots, packed, spare, ordered):
    capacity = base.shape[0]
    part = slots.shape[1]
    groups = slots.shape[0] // part
    leaves = part // 8
    core = jnp.bitwise_and(place[0], 1)
    levels = left_top.shape[0]
    half = own.shape[0]
    stacked = []
    for level in range(levels):
        coef = jnp.where(core == level, own[...], theirs[...]).astype(F32)
        coef = jnp.where(iota(coef.shape, 1) < place[1 + level], coef, 0.0)
        turned = jnp.concatenate([-coef[half // 2 :], coef[: half // 2]], axis=0)
        stacked += [jnp.transpose(coef), jnp.transpose(turned)]
    stacked = jnp.concatenate(stacked, axis=0).astype(BF16)
    if groups * part > capacity:
        spare[capacity:, :] = jnp.zeros((groups * part - capacity, 128), BF16)
    factors = [left_top[level, p] for level in range(levels) for p in range(2)]
    total = base[...] + dot(jnp.concatenate(factors, axis=1), stacked)
    spare[:capacity, :] = total.astype(BF16)
    for g in range(groups):
        moved = dot(slots[g * part : (g + 1) * part, :], spare[g * part : (g + 1) * part, :])
        ordered[:, g * 8 : g * 8 + 8, :] = moved.reshape(leaves, 8, 128)
    packed[...] = ordered[:, :bucket, :].reshape(capacity, 128).astype(BF16)


def unpack_kernel(order, upper, returned, out, near, sems):
    count, folded = order.shape
    wide = jnp.concatenate([returned[:folded, :], returned[folded:, :]], axis=1)
    block = 512
    copies = []
    for low in range(0, count, block):
        rows = pl.ds(low, block)
        both = dot(order[low : low + block, :], wide)
        near[rows, :] = jnp.where(upper[low : low + block, :] != 0, both[:, 128:], both[:, :128])
        copies.append(pltpu.make_async_copy(near.at[rows, :], out.at[rows, :], sems.at[low // block]))
        copies[-1].start()
    for copy in copies:
        copy.wait()


def on_device(
    mesh_vector,
    cluster_position,
    cluster_sizes,
    block_ranks,
    diag_block,
    top_left,
    top_right,
    low_left,
    low_right,
):
    groups = lax.axis_size("group")
    members = lax.axis_size("member")
    leaves = groups * members
    group_levels = groups.bit_length() - 1
    member_levels = members.bit_length() - 1
    levels = group_levels + member_levels
    device = lax.axis_index("group") * members + lax.axis_index("member")
    capacity = diag_block.shape[1]
    bucket = capacity // leaves
    padded = (bucket + 16) // 16 * 16
    filled = (bucket + 7) // 8 * 8
    count, columns = mesh_vector.shape
    everyone = ("group", "member")
    low_left = jnp.swapaxes(low_left, 2, 3)
    low_right = jnp.swapaxes(low_right, 2, 3)
    width = low_left.shape[2]
    top_width = top_left.shape[3]
    far_flops = 4 * capacity * columns * (group_levels * top_width + member_levels * width)

    level_ids = jnp.arange(1, levels + 1, dtype=I32)
    ranks = block_ranks[(1 << level_ids) - 2 + jnp.right_shift(device, levels - level_ids)]
    place = jnp.concatenate([device[None].astype(I32), ranks])

    packed, places = call(
        functools.partial(pack_kernel, leaves, bucket),
        [
            jax.ShapeDtypeStruct((leaves, padded, columns), BF16),
            jax.ShapeDtypeStruct((1, count), I32),
        ],
        [HBM] * 3,
        far(cluster_sizes, cluster_position.reshape(1, count), mesh_vector),
        2 * count * count * columns,
        4 << 20,
        16,
        out_specs=[HBM, VMEM],
        scratch=[
            pltpu.SMEM((leaves,), I32),
            pltpu.VMEM((1, count), I32),
            pltpu.VMEM((count, columns), BF16),
            pltpu.VMEM((count + padded, columns), F32),
            pltpu.VMEM((leaves, padded, columns), BF16),
            DMA((3,)),
            DMA((4,)),
        ],
    )
    arrived = lax.all_to_all(packed, everyone, split_axis=0, concat_axis=0, tiled=True)
    ranked = group_levels * top_width + member_levels * width
    right = call(
        near_kernel,
        [pltpu.VMEM((2, ranked, capacity), BF16)],
        [HBM] * 2,
        far(top_right, low_right),
        0,
        6 << 20,
        16,
        scratch=[pltpu.VMEM(top_right.shape, BF16), DMA((1 + 2 * member_levels,))],
    )[0]
    tops = group_levels * columns // 2
    shared = tops + (member_levels - 1) * width // 2
    pair, targets, send, keep = call(
        functools.partial(field_kernel, leaves, bucket, group_levels, member_levels),
        [
            jax.ShapeDtypeStruct((2, capacity, columns), BF16),
            jax.ShapeDtypeStruct((filled // 8, leaves * 8), I32),
            jax.ShapeDtypeStruct((shared + width, columns), F32),
            jax.ShapeDtypeStruct((shared, columns), F32),
        ],
        [SMEM, VMEM, VMEM],
        (place, arrived, right),
        far_flops,
        6 << 20,
        24,
        scratch=[pltpu.VMEM((2 * shared + width, columns), F32)],
    )
    height = capacity // 8

    def diagonal(first, chunks, after):
        return call(
            functools.partial(diag_kernel, first),
            [jax.ShapeDtypeStruct((chunks * height, columns), F32)],
            [HBM, VMEM, pl.BlockSpec(memory_space=pl.ANY)],
            (*far(diag_block), pair, after),
            4 * chunks * height * capacity * columns,
            4 * chunks * height * capacity,
            24,
            scratch=[pltpu.VMEM((chunks, 2, height, capacity), BF16), DMA((chunks,))],
        )[0]

    received = partner(send, "member", 0)
    slots, order, upper = call(
        way_kernel,
        [
            jax.ShapeDtypeStruct((leaves * filled, leaves * 8), BF16),
            jax.ShapeDtypeStruct((count, capacity // 2), BF16),
            jax.ShapeDtypeStruct((count, 128), I32),
        ],
        [VMEM, VMEM, pl.BlockSpec(memory_space=pl.ANY)],
        (targets, places, send),
        0,
        8 << 20,
        16,
    )
    received, slots, order, upper = lax.optimization_barrier((received, slots, order, upper))
    nearest = received[shared:]
    running = keep + received[:shared]
    bases = []
    coefs = []
    for bit in range(1, member_levels):
        rest = running.shape[0] - width // 2
        received = partner(running, "member", bit)
        if bit == 1:
            bases.append(diagonal(0, 5, running))
            received, bases[0] = lax.optimization_barrier((received, bases[0]))
        if bit == member_levels - 1:
            bases.append(diagonal(5, 3, running))
            left_top, left_low = call(
                stage_kernel,
                [
                    pltpu.VMEM(top_left.shape, BF16),
                    pltpu.VMEM((capacity, member_levels * 2 * width), BF16),
                ],
                [HBM, HBM, pl.BlockSpec(memory_space=pl.ANY)],
                (*far(top_left, low_left), running),
                0,
                8 << 20,
                24,
                scratch=[pltpu.VMEM(low_left.shape, BF16), DMA((2,))],
            )
            received, bases[1], left_top, left_low = lax.optimization_barrier(
                (received, bases[1], left_top, left_low)
            )
        coefs.insert(0, received[rest:].astype(BF16))
        running = running[:rest] + received[:rest]
    routes = [[], []]
    for low in range(groups):
        for near in range(0, members, 2):
            at = low * members + near
            routes[0] += [(at, (low ^ 2) * members + near), (at + 1, (low ^ 1) * members + near + 1)]
            routes[1] += [(at + core, (low ^ 3) * members + near + core) for core in range(2)]
    heard = [lax.ppermute(running, everyone, route) for route in routes]
    own_low = jnp.concatenate(coefs)
    base = call(
        functools.partial(low_kernel, len(bases)),
        [jax.ShapeDtypeStruct((capacity, columns), F32)],
        [SMEM] + [VMEM] * (len(bases) + 4),
        (place, *bases, left_low, nearest, own_low, partner(own_low, "member", 0)),
        4 * capacity * columns * member_levels * width,
        3 << 20,
        16,
    )[0]
    second = jnp.where(jnp.bitwise_and(device, 1) == 0, heard[1], 0.0)
    own = (heard[0] + second).astype(BF16)
    own, base = lax.optimization_barrier((own, base))
    theirs = partner(own, "member", 0)

    leaving = call(
        functools.partial(out_kernel, bucket),
        [jax.ShapeDtypeStruct((capacity, columns), BF16)],
        [SMEM] + [VMEM] * 5,
        (place, base, left_top, own, theirs, slots),
        4 * capacity * columns * group_levels * top_width,
        4 << 20,
        24,
        scratch=[
            pltpu.VMEM((leaves * filled, 128), BF16),
            pltpu.VMEM((leaves, filled, 128), F32),
        ],
    )[0]
    returned = lax.all_to_all(
        leaving.reshape(leaves, bucket, columns), everyone, split_axis=0, concat_axis=0, tiled=True
    )
    return call(
        unpack_kernel,
        [jax.ShapeDtypeStruct((count, columns), F32)],
        [VMEM] * 3,
        (order, upper, returned.reshape(capacity, columns)),
        2 * capacity * count * columns,
        4 << 20,
        16,
        out_specs=[HBM],
        scratch=[pltpu.VMEM((count, 128), F32), DMA((count // 512,))],
    )[0]


def solution(mesh):
    return jax.shard_map(
        on_device,
        mesh=mesh,
        in_specs=(
            P(("group", "member"), None),
            P(("group", "member")),
            P(),
            P(),
            P(None, ("group", "member"), None),
            P(None, None, ("group", "member"), None),
            P(None, None, ("group", "member"), None),
            P(None, None, ("group", "member"), None),
            P(None, None, ("group", "member"), None),
        ),
        out_specs=P(("group", "member"), None),
        check_vma=False,
    )
```

```python
import functools

import jax
import jax.numpy as jnp
from jax import lax
from jax.experimental import pallas as pl
from jax.experimental.pallas import tpu as pltpu
from jax.sharding import PartitionSpec as P

F32 = jnp.float32
BF16 = jnp.bfloat16
I32 = jnp.int32
VMEM = pl.BlockSpec(memory_space=pltpu.VMEM)
SMEM = pl.BlockSpec(memory_space=pltpu.SMEM)
HBM = pl.BlockSpec(memory_space=pltpu.HBM)
DMA = pltpu.SemaphoreType.DMA


def iota(shape, dim):
    return lax.broadcasted_iota(I32, shape, dim)


def hot(mask):
    return jnp.where(mask, 1.0, 0.0).astype(BF16)


def dot(a, b, over=(1, 0)):
    return lax.dot_general(
        a, b, (((over[0],), (over[1],)), ((), ())), preferred_element_type=F32
    )


def call(kernel, outs, ins, args, flops, moved, limit, scratch=(), **more):
    return pl.pallas_call(
        kernel,
        out_shape=outs,
        in_specs=ins,
        out_specs=more.pop("out_specs", [VMEM] * len(outs)),
        scratch_shapes=scratch,
        cost_estimate=pl.CostEstimate(flops=flops, bytes_accessed=moved, transcendentals=0),
        compiler_params=pltpu.CompilerParams(vmem_limit_bytes=limit << 20),
        **more,
    )(*args)


def partner(block, axis, apart):
    count = lax.axis_size(axis)
    route = []
    for low in range(count):
        high = low | 1 << apart
        if high != low and high < count:
            route += [(low, high), (high, low)]
    return lax.ppermute(block, axis, route)


def far(*arrays):
    return [pltpu.with_memory_space_constraint(array, pltpu.HBM) for array in arrays]


def turn(block):
    half = block.shape[1] // 2
    return jnp.where(iota(block.shape, 1) < half, -1.0, 1.0) * pltpu.roll(block, half, 1)


def pack_kernel(leaves, bucket, sizes_in, position_in, rows_in, packed, places, *scratch):
    sizes, position, rows, ordered, near, sems, out_sems = scratch
    copies = [
        pltpu.make_async_copy(source, target, sems.at[i])
        for i, (source, target) in enumerate(
            [(position_in, position), (rows_in, rows), (sizes_in, sizes)]
        )
    ]
    for copy in copies:
        copy.start()
    copies[0].wait()
    count = rows.shape[0]
    padded = packed.shape[1]
    shift = leaves.bit_length() - 1
    here = position[...]
    window = jnp.right_shift(here, shift)
    copies[1].wait()
    values = rows[...]
    block = 512
    for low in range(0, count, block):
        ordered[low : low + block, :] = dot(hot(iota((block, count), 0) + low == window), values)
    ordered[count:, :] = jnp.zeros((padded, 128), F32)
    copies[2].wait()
    zero = jnp.zeros((1, count), I32)
    owner, first = zero, zero
    starts = [0]
    for c in range(leaves):
        starts.append(starts[-1] + jnp.right_shift(sizes[c], shift))
        beyond = window >= starts[-1]
        owner = owner + beyond.astype(I32)
        first = jnp.where(beyond, starts[-1], first)
    offset = jnp.bitwise_and(here, leaves - 1).astype(F32)
    picked = jnp.where(iota((leaves, count), 0) == owner, offset, 0.0).astype(BF16)
    offsets = dot(picked, hot(iota((128, count), 0) == window - first), (1, 1))
    places[...] = owner * bucket + window - first
    line = iota((padded, 128), 0)
    chunk = leaves // 4
    out = []
    for c in range(leaves):
        data = ordered[pl.ds(starts[c], padded), :]
        data = jnp.where(line < starts[c + 1] - starts[c], data, 0.0)
        data = jnp.where(line == bucket, offsets[c : c + 1, :], data)
        near[c] = data.astype(BF16)
        if c % chunk == chunk - 1:
            part = pl.ds(c + 1 - chunk, chunk)
            out.append(pltpu.make_async_copy(near.at[part], packed.at[part], out_sems.at[c // chunk]))
            out[-1].start()
    for copy in out:
        copy.wait()


def near_kernel(right_top_in, right_low_in, right, sems):
    tops, parts, capacity, width = right_top_in.shape
    levels, _, rows, _ = right_low_in.shape
    pairs = []
    for level in range(tops):
        for p in range(parts):
            place = (pl.ds(p * capacity, capacity), pl.ds(level * width, width))
            pairs.append((right_top_in.at[level, p], right.at[place]))
    at = parts * capacity
    for low in range(0, capacity, 256):
        for p in range(parts):
            for level in range(levels):
                source = right_low_in.at[level, p, :, pl.ds(low, 256)]
                pairs.append((source, right.at[pl.ds(at, rows), :]))
                at += rows
    copies = [pltpu.make_async_copy(a, b, sems.at[i]) for i, (a, b) in enumerate(pairs)]
    for copy in copies:
        copy.start()
    for copy in copies:
        copy.wait()


def way_kernel(targets, places, after, slots, order, upper):
    groups, part = targets.shape
    lanes = iota((part, 128), 1)
    for g in range(groups):
        target = jnp.transpose(jnp.broadcast_to(targets[g : g + 1, :], (128, part)))
        for low in range(0, part, 128):
            slots[g * part : (g + 1) * part, low : low + 128] = hot(target == lanes + low)
    count, folded = order.shape
    place = jnp.transpose(jnp.broadcast_to(places[...], (128, count)))
    beyond = place >= folded
    upper[...] = beyond.astype(I32)
    place = jnp.where(beyond, place - folded, place)
    block = 256
    lanes = iota((block, 128), 1)
    for low in range(0, count, block):
        for at in range(0, folded, 128):
            order[low : low + block, at : at + 128] = hot(place[low : low + block] == lanes + at)


def stage_kernel(left_top_in, left_low_in, after, left_top, left_low, raw, sems):
    copies = [
        pltpu.make_async_copy(left_low_in, raw, sems.at[0]),
        pltpu.make_async_copy(left_top_in, left_top, sems.at[1]),
    ]
    for copy in copies:
        copy.start()
    copies[0].wait()
    levels, parts, width, capacity = raw.shape
    left_low[...] = jnp.transpose(raw[...].reshape(levels * parts * width, capacity))
    copies[1].wait()


def field_kernel(leaves, bucket, tops, levels, place, arrived, right, *rest):
    pair, targets, send, keep, gate, whole = rest
    capacity = leaves * bucket
    padded = arrived.shape[1]
    part = leaves * 8
    groups = targets.shape[0]
    core = jnp.bitwise_and(place[0], 1)
    last = arrived[:, padded - 16 :, :].reshape(leaves * 16, 128)
    carrier = iota((leaves, leaves * 16), 1) == iota((leaves, leaves * 16), 0) * 16 + bucket % 16
    offsets = dot(hot(carrier), last).astype(BF16)
    spread = hot(jnp.right_shift(iota((leaves, part), 1), 3) == iota((leaves, part), 0))
    spread_offsets = dot(offsets, spread, (0, 0))[: groups * 8].reshape(groups, 8, part)
    lane_window = jnp.bitwise_and(iota((8, part), 1), 7)
    own = (lane_window == iota((8, part), 0))[None]
    target = jnp.sum(jnp.where(own, spread_offsets, 0.0), axis=1).astype(I32)
    target = target + lane_window[:1, :] * leaves
    targets[...] = target
    for g in range(groups):
        size = min(part, capacity - g * part)
        if g % 2 == 0:
            both = arrived[:, g * 8 : g * 8 + 16, :].astype(F32)
        chunk = both[:, g % 2 * 8 : g % 2 * 8 + 8, :].reshape(part, 128).astype(BF16)
        placed = dot(hot(iota((part, part), 0) == target[g : g + 1, :]), chunk)
        pair[0, g * part : g * part + size, :] = placed[:size].astype(BF16)
        pair[1, g * part : g * part + size, :] = turn(placed)[:size].astype(BF16)
    plain = jnp.transpose(pair[0])
    turned = jnp.concatenate([-plain[64:], plain[:64]], axis=0)
    upper = dot(plain, right[:capacity, :]) + dot(turned, right[capacity : 2 * capacity, :])
    top_rows = tops * 128
    for level in range(tops):
        whole[level * 128 : (level + 1) * 128, :] = upper[:, level * 128 : (level + 1) * 128]
    rows = whole.shape[0] - top_rows
    width = rows // levels
    lower = jnp.zeros((rows, 128), F32)
    at = 2 * capacity
    for low in range(0, capacity, 256):
        for p in range(2):
            lower += dot(right[at : at + rows, :], pair[p, low : low + 256, :])
            at += rows
    whole[top_rows:, :] = lower
    gate[...] = jnp.broadcast_to((1 - core).astype(F32), gate.shape)
    at = 0
    low = 0
    for half in [tops * 64] + [width // 2] * (levels - 1):
        mine = pl.multiple_of(low + core * half, 8)
        other = pl.multiple_of(low + (1 - core) * half, 8)
        keep[at : at + half, :] = whole[pl.ds(mine, half), :]
        send[at : at + half, :] = whole[pl.ds(other, half), :]
        at += half
        low += 2 * half
    send[at:, :] = lower[(levels - 1) * width :]


def diag_kernel(first, block_in, pair, after, out, block, sems):
    count, _, height, _ = block.shape
    copies = []
    for j in range(count):
        rows = pl.ds((first + j) * height, height)
        copies.append(pltpu.make_async_copy(block_in.at[:, rows, :], block.at[j], sems.at[j]))
        copies[j].start()
    for j in range(count):
        copies[j].wait()
        out[j * height : (j + 1) * height, :] = dot(block[j, 0], pair[0]) + dot(block[j, 1], pair[1])


def merged(core, own, theirs, at, half):
    a, b = own[at : at + half, :].astype(F32), theirs[at : at + half, :].astype(F32)
    return jnp.concatenate([jnp.where(core == 0, a, b), jnp.where(core == 0, b, a)], axis=0)


def low_kernel(pieces, place, *rest):
    bases = rest[:pieces]
    left_low, nearest, own, theirs, out = rest[pieces:]
    width = nearest.shape[0]
    levels = left_low.shape[1] // (2 * width)
    tops = place.shape[0] - 1 - levels
    core = jnp.bitwise_and(place[0], 1)
    half = width // 2
    stacked = []
    for level in range(levels):
        if level < levels - 1:
            coef = merged(core, own, theirs, level * half, half)
        else:
            coef = nearest[...]
        coef = jnp.where(iota(coef.shape, 0) < place[1 + tops + level], coef, 0.0)
        stacked += [coef, turn(coef)]
    stacked = jnp.concatenate(stacked, axis=0).astype(BF16)
    low = 0
    for base in bases:
        rows = slice(low, low + base.shape[0])
        out[rows, :] = base[...] + dot(left_low[rows, :], stacked)
        low += base.shape[0]


def out_kernel(bucket, place, base, left_top, own, theirs, slots, packed, spare, ordered):
    capacity = base.shape[0]
    part = slots.shape[1]
    groups = slots.shape[0] // part
    leaves = part // 8
    core = jnp.bitwise_and(place[0], 1)
    levels = left_top.shape[0]
    half = own.shape[0]
    stacked = []
    for level in range(levels):
        coef = jnp.where(core == level, own[...], theirs[...]).astype(F32)
        coef = jnp.where(iota(coef.shape, 1) < place[1 + level], coef, 0.0)
        turned = jnp.concatenate([-coef[half // 2 :], coef[: half // 2]], axis=0)
        stacked += [jnp.transpose(coef), jnp.transpose(turned)]
    stacked = jnp.concatenate(stacked, axis=0).astype(BF16)
    if groups * part > capacity:
        spare[capacity:, :] = jnp.zeros((groups * part - capacity, 128), BF16)
    factors = [left_top[level, p] for level in range(levels) for p in range(2)]
    total = base[...] + dot(jnp.concatenate(factors, axis=1), stacked)
    spare[:capacity, :] = total.astype(BF16)
    for g in range(groups):
        moved = dot(slots[g * part : (g + 1) * part, :], spare[g * part : (g + 1) * part, :])
        ordered[:, g * 8 : g * 8 + 8, :] = moved.reshape(leaves, 8, 128)
    packed[...] = ordered[:, :bucket, :].reshape(capacity, 128).astype(BF16)


def unpack_kernel(order, upper, returned, out, near, sems):
    count, folded = order.shape
    wide = jnp.concatenate([returned[:folded, :], returned[folded:, :]], axis=1)
    block = 512
    copies = []
    for low in range(0, count, block):
        rows = pl.ds(low, block)
        both = dot(order[low : low + block, :], wide)
        near[rows, :] = jnp.where(upper[low : low + block, :] != 0, both[:, 128:], both[:, :128])
        copies.append(pltpu.make_async_copy(near.at[rows, :], out.at[rows, :], sems.at[low // block]))
        copies[-1].start()
    for copy in copies:
        copy.wait()


def on_device(
    mesh_vector,
    cluster_position,
    cluster_sizes,
    block_ranks,
    diag_block,
    top_left,
    top_right,
    low_left,
    low_right,
):
    groups = lax.axis_size("group")
    members = lax.axis_size("member")
    leaves = groups * members
    group_levels = groups.bit_length() - 1
    member_levels = members.bit_length() - 1
    levels = group_levels + member_levels
    device = lax.axis_index("group") * members + lax.axis_index("member")
    capacity = diag_block.shape[1]
    bucket = capacity // leaves
    padded = (bucket + 16) // 16 * 16
    filled = (bucket + 7) // 8 * 8
    count, columns = mesh_vector.shape
    everyone = ("group", "member")
    low_left = jnp.swapaxes(low_left, 2, 3)
    low_right = jnp.swapaxes(low_right, 2, 3)
    width = low_left.shape[2]
    top_width = top_left.shape[3]
    far_flops = 4 * capacity * columns * (group_levels * top_width + member_levels * width)

    level_ids = jnp.arange(1, levels + 1, dtype=I32)
    ranks = block_ranks[(1 << level_ids) - 2 + jnp.right_shift(device, levels - level_ids)]
    place = jnp.concatenate([device[None].astype(I32), ranks])

    packed, places = call(
        functools.partial(pack_kernel, leaves, bucket),
        [
            jax.ShapeDtypeStruct((leaves, padded, columns), BF16),
            jax.ShapeDtypeStruct((1, count), I32),
        ],
        [HBM] * 3,
        far(cluster_sizes, cluster_position.reshape(1, count), mesh_vector),
        2 * count * count * columns,
        4 << 20,
        16,
        out_specs=[HBM, VMEM],
        scratch=[
            pltpu.SMEM((leaves,), I32),
            pltpu.VMEM((1, count), I32),
            pltpu.VMEM((count, columns), BF16),
            pltpu.VMEM((count + padded, columns), F32),
            pltpu.VMEM((leaves, padded, columns), BF16),
            DMA((3,)),
            DMA((4,)),
        ],
    )
    arrived = lax.all_to_all(packed, everyone, split_axis=0, concat_axis=0, tiled=True)
    ranked = group_levels * top_width + member_levels * width
    right = call(
        near_kernel,
        [pltpu.VMEM((2 * ranked * capacity // 256, 256), BF16)],
        [HBM] * 2,
        far(top_right, low_right),
        0,
        6 << 20,
        16,
        scratch=[DMA((2 * group_levels + 2 * member_levels * capacity // 256,))],
    )[0]
    tops = group_levels * columns // 2
    shared = tops + (member_levels - 1) * width // 2
    pair, targets, send, keep, gate = call(
        functools.partial(field_kernel, leaves, bucket, group_levels, member_levels),
        [
            jax.ShapeDtypeStruct((2, capacity, columns), BF16),
            jax.ShapeDtypeStruct((filled // 8, leaves * 8), I32),
            jax.ShapeDtypeStruct((shared + width, columns), F32),
            jax.ShapeDtypeStruct((shared, columns), F32),
            jax.ShapeDtypeStruct((1, columns), F32),
        ],
        [SMEM, VMEM, VMEM],
        (place, arrived, right),
        far_flops,
        6 << 20,
        24,
        scratch=[pltpu.VMEM((2 * shared + width, columns), F32)],
    )
    height = capacity // 8

    def diagonal(first, chunks, after):
        return call(
            functools.partial(diag_kernel, first),
            [jax.ShapeDtypeStruct((chunks * height, columns), F32)],
            [HBM, VMEM, pl.BlockSpec(memory_space=pl.ANY)],
            (*far(diag_block), pair, after),
            4 * chunks * height * capacity * columns,
            4 * chunks * height * capacity,
            24,
            scratch=[pltpu.VMEM((chunks, 2, height, capacity), BF16), DMA((chunks,))],
        )[0]

    received = partner(send, "member", 0)
    slots, order, upper = call(
        way_kernel,
        [
            jax.ShapeDtypeStruct((leaves * filled, leaves * 8), BF16),
            jax.ShapeDtypeStruct((count, capacity // 2), BF16),
            jax.ShapeDtypeStruct((count, 128), I32),
        ],
        [VMEM, VMEM, pl.BlockSpec(memory_space=pl.ANY)],
        (targets, places, send),
        0,
        8 << 20,
        16,
    )
    received, slots, order, upper = lax.optimization_barrier((received, slots, order, upper))
    nearest = received[shared:]
    running = keep + received[:shared]
    bases = []
    coefs = []
    for bit in range(1, member_levels):
        rest = running.shape[0] - width // 2
        received = partner(running, "member", bit)
        if bit == 1:
            bases.append(diagonal(0, 5, running))
            received, bases[0] = lax.optimization_barrier((received, bases[0]))
        if bit == member_levels - 1:
            bases.append(diagonal(5, 3, running))
            received, bases[1] = lax.optimization_barrier((received, bases[1]))
        coefs.insert(0, received[rest:].astype(BF16))
        running = running[:rest] + received[:rest]
    routes = [[], []]
    for low in range(groups):
        for near in range(0, members, 2):
            at = low * members + near
            routes[0] += [(at, (low ^ 2) * members + near), (at + 1, (low ^ 1) * members + near + 1)]
            routes[1] += [(at + core, (low ^ 3) * members + near + core) for core in range(2)]
    heard = [lax.ppermute(running, everyone, route) for route in routes]
    left_top, left_low = call(
        stage_kernel,
        [
            pltpu.VMEM(top_left.shape, BF16),
            pltpu.VMEM((capacity, member_levels * 2 * width), BF16),
        ],
        [HBM, HBM, pl.BlockSpec(memory_space=pl.ANY)],
        (*far(top_left, low_left), running),
        0,
        8 << 20,
        24,
        scratch=[pltpu.VMEM(low_left.shape, BF16), DMA((2,))],
    )
    heard, left_top, left_low = lax.optimization_barrier((heard, left_top, left_low))
    own = (heard[0] + jnp.where(gate > 0, heard[1], 0.0)).astype(BF16)
    own_low = jnp.concatenate(coefs)
    their_low, own = lax.optimization_barrier((partner(own_low, "member", 0), own))
    theirs = partner(own, "member", 0)
    base = call(
        functools.partial(low_kernel, len(bases)),
        [jax.ShapeDtypeStruct((capacity, columns), F32)],
        [SMEM] + [VMEM] * (len(bases) + 4),
        (place, *bases, left_low, nearest, own_low, their_low),
        4 * capacity * columns * member_levels * width,
        3 << 20,
        16,
    )[0]

    leaving = call(
        functools.partial(out_kernel, bucket),
        [jax.ShapeDtypeStruct((capacity, columns), BF16)],
        [SMEM] + [VMEM] * 5,
        (place, base, left_top, own, theirs, slots),
        4 * capacity * columns * group_levels * top_width,
        4 << 20,
        24,
        scratch=[
            pltpu.VMEM((leaves * filled, 128), BF16),
            pltpu.VMEM((leaves, filled, 128), F32),
        ],
    )[0]
    returned = lax.all_to_all(
        leaving.reshape(leaves, bucket, columns), everyone, split_axis=0, concat_axis=0, tiled=True
    )
    return call(
        unpack_kernel,
        [jax.ShapeDtypeStruct((count, columns), F32)],
        [VMEM] * 3,
        (order, upper, returned.reshape(capacity, columns)),
        2 * capacity * count * columns,
        4 << 20,
        16,
        out_specs=[HBM],
        scratch=[pltpu.VMEM((count, 128), F32), DMA((count // 512,))],
    )[0]


def solution(mesh):
    return jax.shard_map(
        on_device,
        mesh=mesh,
        in_specs=(
            P(("group", "member"), None),
            P(("group", "member")),
            P(),
            P(),
            P(None, ("group", "member"), None),
            P(None, None, ("group", "member"), None),
            P(None, None, ("group", "member"), None),
            P(None, None, ("group", "member"), None),
            P(None, None, ("group", "member"), None),
        ),
        out_specs=P(("group", "member"), None),
        check_vma=False,
    )
```

```python
import functools

import jax
import jax.numpy as jnp
from jax import lax
from jax.experimental import pallas as pl
from jax.experimental.pallas import tpu as pltpu
from jax.sharding import PartitionSpec as P

F32 = jnp.float32
BF16 = jnp.bfloat16
I32 = jnp.int32
VMEM = pl.BlockSpec(memory_space=pltpu.VMEM)
SMEM = pl.BlockSpec(memory_space=pltpu.SMEM)
HBM = pl.BlockSpec(memory_space=pltpu.HBM)
DMA = pltpu.SemaphoreType.DMA


def iota(shape, dim):
    return lax.broadcasted_iota(I32, shape, dim)


def hot(mask):
    return jnp.where(mask, 1.0, 0.0).astype(BF16)


def dot(a, b, over=(1, 0)):
    return lax.dot_general(
        a, b, (((over[0],), (over[1],)), ((), ())), preferred_element_type=F32
    )


def call(kernel, outs, ins, args, flops, moved, limit, scratch=(), **more):
    return pl.pallas_call(
        kernel,
        out_shape=outs,
        in_specs=ins,
        out_specs=more.pop("out_specs", [VMEM] * len(outs)),
        scratch_shapes=scratch,
        cost_estimate=pl.CostEstimate(flops=flops, bytes_accessed=moved, transcendentals=0),
        compiler_params=pltpu.CompilerParams(vmem_limit_bytes=limit << 20),
        **more,
    )(*args)


def partner(block, axis, apart):
    count = lax.axis_size(axis)
    route = []
    for low in range(count):
        high = low | 1 << apart
        if high != low and high < count:
            route += [(low, high), (high, low)]
    return lax.ppermute(block, axis, route)


def far(*arrays):
    return [pltpu.with_memory_space_constraint(array, pltpu.HBM) for array in arrays]


def turn(block):
    half = block.shape[1] // 2
    return jnp.where(iota(block.shape, 1) < half, -1.0, 1.0) * pltpu.roll(block, half, 1)


def rank_of(ranks, level, levels):
    device = lax.axis_index("group") * lax.axis_size("member") + lax.axis_index("member")
    return ranks[(1 << level) - 2 + jnp.right_shift(device, levels - level)]


def pack_kernel(leaves, bucket, sizes_in, position_in, rows_in, packed, places, *scratch):
    sizes, position, rows, ordered, near, sems, out_sems = scratch
    copies = [
        pltpu.make_async_copy(source, target, sems.at[i])
        for i, (source, target) in enumerate(
            [(position_in, position), (rows_in, rows), (sizes_in, sizes)]
        )
    ]
    for copy in copies:
        copy.start()
    copies[0].wait()
    count = rows.shape[0]
    padded = packed.shape[1]
    shift = leaves.bit_length() - 1
    here = position[...]
    window = jnp.right_shift(here, shift)
    copies[1].wait()
    values = rows[...]
    block = 512
    for low in range(0, count, block):
        ordered[low : low + block, :] = dot(hot(iota((block, count), 0) + low == window), values)
    ordered[count:, :] = jnp.zeros((padded, 128), F32)
    copies[2].wait()
    zero = jnp.zeros((1, count), I32)
    owner, first = zero, zero
    starts = [0]
    for c in range(leaves):
        starts.append(starts[-1] + jnp.right_shift(sizes[c], shift))
        beyond = window >= starts[-1]
        owner = owner + beyond.astype(I32)
        first = jnp.where(beyond, starts[-1], first)
    offset = jnp.bitwise_and(here, leaves - 1).astype(F32)
    picked = jnp.where(iota((leaves, count), 0) == owner, offset, 0.0).astype(BF16)
    offsets = dot(picked, hot(iota((128, count), 0) == window - first), (1, 1))
    places[...] = owner * bucket + window - first
    line = iota((padded, 128), 0)
    chunk = leaves // 8
    out = []
    for c in range(leaves):
        data = ordered[pl.ds(starts[c], padded), :]
        data = jnp.where(line < starts[c + 1] - starts[c], data, 0.0)
        data = jnp.where(line == bucket, offsets[c : c + 1, :], data)
        near[c] = data.astype(BF16)
        if c % chunk == chunk - 1:
            part = pl.ds(c + 1 - chunk, chunk)
            out.append(pltpu.make_async_copy(near.at[part], packed.at[part], out_sems.at[c // chunk]))
            out[-1].start()
    for copy in out:
        copy.wait()


def near_kernel(ranks, right_top_in, right_low_in, right, flags, sems):
    tops, parts, capacity, width = right_top_in.shape
    levels, _, rows, _ = right_low_in.shape
    pairs = []
    for level in range(tops):
        for p in range(parts):
            place = (pl.ds(p * capacity, capacity), pl.ds(level * width, width))
            pairs.append((right_top_in.at[level, p], right.at[place]))
    at = parts * capacity
    for low in range(0, capacity, 256):
        for p in range(parts):
            for level in range(levels):
                source = right_low_in.at[level, p, :, pl.ds(low, 256)]
                pairs.append((source, right.at[pl.ds(at, rows), :]))
                at += rows
    copies = [pltpu.make_async_copy(a, b, sems.at[i]) for i, (a, b) in enumerate(pairs)]
    for copy in copies:
        copy.start()
    row, lane = iota(flags.shape, 0), iota(flags.shape, 1)
    marks = jnp.where(row == 0, 1 - jnp.bitwise_and(lax.axis_index("member"), 1), 0)
    for level in range(1, tops + 1):
        counts = (lane < rank_of(ranks, level, tops + levels)).astype(I32)
        marks = jnp.where(row == level, counts, marks)
    flags[...] = marks.astype(F32)
    for copy in copies:
        copy.wait()


def way_kernel(targets, places, after, slots, order, upper):
    groups, part = targets.shape
    lanes = iota((part, 128), 1)
    for g in range(groups):
        target = jnp.transpose(jnp.broadcast_to(targets[g : g + 1, :], (128, part)))
        for low in range(0, part, 128):
            slots[g * part : (g + 1) * part, low : low + 128] = hot(target == lanes + low)
    count, folded = order.shape
    place = jnp.transpose(jnp.broadcast_to(places[...], (128, count)))
    beyond = place >= folded
    upper[...] = beyond.astype(I32)
    place = jnp.where(beyond, place - folded, place)
    block = 256
    lanes = iota((block, 128), 1)
    for low in range(0, count, block):
        for at in range(0, folded, 128):
            order[low : low + block, at : at + 128] = hot(place[low : low + block] == lanes + at)


def stage_kernel(left_top_in, left_low_in, after, left_top, left_low, raw, sems):
    copies = [
        pltpu.make_async_copy(left_low_in, raw, sems.at[0]),
        pltpu.make_async_copy(left_top_in, left_top, sems.at[1]),
    ]
    for copy in copies:
        copy.start()
    copies[0].wait()
    levels, parts, width, capacity = raw.shape
    left_low[...] = jnp.transpose(raw[...].reshape(levels * parts * width, capacity))
    copies[1].wait()


def field_kernel(leaves, bucket, tops, levels, arrived, right, *rest):
    pair, targets, send, keep, whole = rest
    capacity = leaves * bucket
    padded = arrived.shape[1]
    part = leaves * 8
    groups = targets.shape[0]
    core = jnp.bitwise_and(lax.axis_index("member"), 1)
    last = arrived[:, padded - 16 :, :].reshape(leaves * 16, 128)
    row = iota((leaves * 16, part), 0)
    spread = jnp.right_shift(iota((leaves * 16, part), 1), 3) * 16 + bucket % 16 == row
    spread_offsets = dot(last, hot(spread), (0, 0))[: groups * 8].reshape(groups, 8, part)
    lane_window = jnp.bitwise_and(iota((8, part), 1), 7)
    own = (lane_window == iota((8, part), 0))[None]
    target = jnp.sum(jnp.where(own, spread_offsets, 0.0), axis=1).astype(I32)
    target = target + lane_window[:1, :] * leaves
    targets[...] = target
    for g in range(groups):
        size = min(part, capacity - g * part)
        if g % 2 == 0:
            both = arrived[:, g * 8 : g * 8 + 16, :].astype(F32)
        chunk = both[:, g % 2 * 8 : g % 2 * 8 + 8, :].reshape(part, 128).astype(BF16)
        placed = dot(hot(iota((part, part), 0) == target[g : g + 1, :]), chunk)
        pair[0, g * part : g * part + size, :] = placed[:size].astype(BF16)
        pair[1, g * part : g * part + size, :] = turn(placed)[:size].astype(BF16)
    plain = jnp.transpose(pair[0])
    turned = jnp.concatenate([-plain[64:], plain[:64]], axis=0)
    upper = dot(plain, right[:capacity, :]) + dot(turned, right[capacity : 2 * capacity, :])
    top_rows = tops * 128
    for level in range(tops):
        whole[level * 128 : (level + 1) * 128, :] = upper[:, level * 128 : (level + 1) * 128]
    rows = whole.shape[0] - top_rows
    width = rows // levels
    lower = jnp.zeros((rows, 128), F32)
    at = 2 * capacity
    for low in range(0, capacity, 256):
        for p in range(2):
            lower += dot(right[at : at + rows, :], pair[p, low : low + 256, :])
            at += rows
    whole[top_rows:, :] = lower
    at = 0
    low = 0
    for half in [tops * 64] + [width // 2] * (levels - 1):
        mine = pl.multiple_of(low + core * half, 8)
        other = pl.multiple_of(low + (1 - core) * half, 8)
        keep[at : at + half, :] = whole[pl.ds(mine, half), :]
        send[at : at + half, :] = whole[pl.ds(other, half), :]
        at += half
        low += 2 * half
    send[at:, :] = lower[(levels - 1) * width :]


def diag_kernel(first, block_in, pair, after, out, block, sems):
    count, _, height, _ = block.shape
    copies = []
    for j in range(count):
        rows = pl.ds((first + j) * height, height)
        copies.append(pltpu.make_async_copy(block_in.at[:, rows, :], block.at[j], sems.at[j]))
        copies[j].start()
    for j in range(count):
        copies[j].wait()
        out[j * height : (j + 1) * height, :] = dot(block[j, 0], pair[0]) + dot(block[j, 1], pair[1])


def merged(core, own, theirs, at, half):
    a, b = own[at : at + half, :].astype(F32), theirs[at : at + half, :].astype(F32)
    return jnp.concatenate([jnp.where(core == 0, a, b), jnp.where(core == 0, b, a)], axis=0)


def low_kernel(pieces, tops, ranks, *rest):
    bases = rest[:pieces]
    left_low, nearest, own, theirs, out = rest[pieces:]
    width = nearest.shape[0]
    levels = left_low.shape[1] // (2 * width)
    core = jnp.bitwise_and(lax.axis_index("member"), 1)
    half = width // 2
    stacked = []
    for level in range(levels):
        if level < levels - 1:
            coef = merged(core, own, theirs, level * half, half)
        else:
            coef = nearest[...]
        rank = rank_of(ranks, 1 + tops + level, tops + levels)
        coef = jnp.where(iota(coef.shape, 0) < rank, coef, 0.0)
        stacked += [coef, turn(coef)]
    stacked = jnp.concatenate(stacked, axis=0).astype(BF16)
    low = 0
    for base in bases:
        rows = slice(low, low + base.shape[0])
        out[rows, :] = base[...] + dot(left_low[rows, :], stacked)
        low += base.shape[0]


def out_kernel(bucket, flags, base, left_top, own, theirs, slots, packed, spare, ordered):
    capacity = base.shape[0]
    part = slots.shape[1]
    groups = slots.shape[0] // part
    leaves = part // 8
    first = flags[:1, :] > 0
    levels = left_top.shape[0]
    half = own.shape[0]
    stacked = []
    for level in range(levels):
        pick = (own, theirs) if level == 0 else (theirs, own)
        coef = jnp.where(first, pick[0][...].astype(F32), pick[1][...].astype(F32))
        coef = jnp.where(flags[1 + level : 2 + level, :] > 0, coef, 0.0)
        turned = jnp.concatenate([-coef[half // 2 :], coef[: half // 2]], axis=0)
        stacked += [jnp.transpose(coef), jnp.transpose(turned)]
    stacked = jnp.concatenate(stacked, axis=0).astype(BF16)
    if groups * part > capacity:
        spare[capacity:, :] = jnp.zeros((groups * part - capacity, 128), BF16)
    factors = [left_top[level, p] for level in range(levels) for p in range(2)]
    total = base[...] + dot(jnp.concatenate(factors, axis=1), stacked)
    spare[:capacity, :] = total.astype(BF16)
    for g in range(groups):
        moved = dot(slots[g * part : (g + 1) * part, :], spare[g * part : (g + 1) * part, :])
        ordered[:, g * 8 : g * 8 + 8, :] = moved.reshape(leaves, 8, 128)
    packed[...] = ordered[:, :bucket, :].reshape(capacity, 128).astype(BF16)


def unpack_kernel(order, upper, returned, out, near, sems):
    count, folded = order.shape
    wide = jnp.concatenate([returned[:folded, :], returned[folded:, :]], axis=1)
    block = 256
    copies = []
    for low in range(0, count, block):
        rows = pl.ds(low, block)
        both = dot(order[low : low + block, :], wide)
        near[rows, :] = jnp.where(upper[low : low + block, :] != 0, both[:, 128:], both[:, :128])
        copies.append(pltpu.make_async_copy(near.at[rows, :], out.at[rows, :], sems.at[low // block]))
        copies[-1].start()
    for copy in copies:
        copy.wait()


def on_device(
    mesh_vector,
    cluster_position,
    cluster_sizes,
    block_ranks,
    diag_block,
    top_left,
    top_right,
    low_left,
    low_right,
):
    groups = lax.axis_size("group")
    members = lax.axis_size("member")
    leaves = groups * members
    group_levels = groups.bit_length() - 1
    member_levels = members.bit_length() - 1
    capacity = diag_block.shape[1]
    bucket = capacity // leaves
    padded = (bucket + 16) // 16 * 16
    filled = (bucket + 7) // 8 * 8
    count, columns = mesh_vector.shape
    everyone = ("group", "member")
    low_left = jnp.swapaxes(low_left, 2, 3)
    low_right = jnp.swapaxes(low_right, 2, 3)
    width = low_left.shape[2]
    top_width = top_left.shape[3]
    far_flops = 4 * capacity * columns * (group_levels * top_width + member_levels * width)

    packed, places = call(
        functools.partial(pack_kernel, leaves, bucket),
        [
            jax.ShapeDtypeStruct((leaves, padded, columns), BF16),
            jax.ShapeDtypeStruct((1, count), I32),
        ],
        [HBM] * 3,
        far(cluster_sizes, cluster_position.reshape(1, count), mesh_vector),
        2 * count * count * columns,
        4 << 20,
        16,
        out_specs=[HBM, VMEM],
        scratch=[
            pltpu.SMEM((leaves,), I32),
            pltpu.VMEM((1, count), I32),
            pltpu.VMEM((count, columns), BF16),
            pltpu.VMEM((count + padded, columns), F32),
            pltpu.VMEM((leaves, padded, columns), BF16),
            DMA((3,)),
            DMA((8,)),
        ],
    )
    arrived = lax.all_to_all(packed, everyone, split_axis=0, concat_axis=0, tiled=True)
    ranked = group_levels * top_width + member_levels * width
    right, flags = call(
        near_kernel,
        [
            pltpu.VMEM((2 * ranked * capacity // 256, 256), BF16),
            jax.ShapeDtypeStruct((8, columns), F32),
        ],
        [SMEM, HBM, HBM],
        (block_ranks, *far(top_right, low_right)),
        0,
        6 << 20,
        16,
        scratch=[DMA((2 * group_levels + 2 * member_levels * capacity // 256,))],
    )
    tops = group_levels * columns // 2
    shared = tops + (member_levels - 1) * width // 2
    pair, targets, send, keep = call(
        functools.partial(field_kernel, leaves, bucket, group_levels, member_levels),
        [
            jax.ShapeDtypeStruct((2, capacity, columns), BF16),
            jax.ShapeDtypeStruct((filled // 8, leaves * 8), I32),
            jax.ShapeDtypeStruct((shared + width, columns), F32),
            jax.ShapeDtypeStruct((shared, columns), F32),
        ],
        [VMEM, VMEM],
        (arrived, right),
        far_flops,
        6 << 20,
        24,
        scratch=[pltpu.VMEM((2 * shared + width, columns), F32)],
    )
    height = capacity // 8

    def diagonal(first, chunks, after):
        return call(
            functools.partial(diag_kernel, first),
            [jax.ShapeDtypeStruct((chunks * height, columns), F32)],
            [HBM, VMEM, pl.BlockSpec(memory_space=pl.ANY)],
            (*far(diag_block), pair, after),
            4 * chunks * height * capacity * columns,
            4 * chunks * height * capacity,
            24,
            scratch=[pltpu.VMEM((chunks, 2, height, capacity), BF16), DMA((chunks,))],
        )[0]

    received = partner(send, "member", 0)
    slots, order, upper = call(
        way_kernel,
        [
            jax.ShapeDtypeStruct((leaves * filled, leaves * 8), BF16),
            jax.ShapeDtypeStruct((count, capacity // 2), BF16),
            jax.ShapeDtypeStruct((count, 128), I32),
        ],
        [VMEM, VMEM, pl.BlockSpec(memory_space=pl.ANY)],
        (targets, places, send),
        0,
        8 << 20,
        16,
    )
    received, slots, order, upper = lax.optimization_barrier((received, slots, order, upper))
    nearest = received[shared:]
    running = keep + received[:shared]
    bases = []
    coefs = []
    for bit in range(1, member_levels):
        rest = running.shape[0] - width // 2
        received = partner(running, "member", bit)
        if bit == 1:
            bases.append(diagonal(0, 5, running))
            received, bases[0] = lax.optimization_barrier((received, bases[0]))
        if bit == member_levels - 1:
            bases.append(diagonal(5, 3, running))
            received, bases[1] = lax.optimization_barrier((received, bases[1]))
        coefs.insert(0, received[rest:].astype(BF16))
        running = running[:rest] + received[:rest]
    routes = [[], []]
    for low in range(groups):
        for near in range(0, members, 2):
            at = low * members + near
            routes[0] += [(at, (low ^ 2) * members + near), (at + 1, (low ^ 1) * members + near + 1)]
            routes[1] += [(at + core, (low ^ 3) * members + near + core) for core in range(2)]
    heard = [lax.ppermute(running, everyone, route) for route in routes]
    left_top, left_low = call(
        stage_kernel,
        [
            pltpu.VMEM(top_left.shape, BF16),
            pltpu.VMEM((capacity, member_levels * 2 * width), BF16),
        ],
        [HBM, HBM, pl.BlockSpec(memory_space=pl.ANY)],
        (*far(top_left, low_left), running),
        0,
        8 << 20,
        24,
        scratch=[pltpu.VMEM(low_left.shape, BF16), DMA((2,))],
    )
    heard, left_top, left_low = lax.optimization_barrier((heard, left_top, left_low))
    own = (heard[0] + jnp.where(flags[:1] > 0, heard[1], 0.0)).astype(BF16)
    own_low = jnp.concatenate(coefs)
    their_low, own = lax.optimization_barrier((partner(own_low, "member", 0), own))
    theirs = partner(own, "member", 0)
    base = call(
        functools.partial(low_kernel, len(bases), group_levels),
        [jax.ShapeDtypeStruct((capacity, columns), F32)],
        [SMEM] + [VMEM] * (len(bases) + 4),
        (block_ranks, *bases, left_low, nearest, own_low, their_low),
        4 * capacity * columns * member_levels * width,
        3 << 20,
        16,
    )[0]

    leaving = call(
        functools.partial(out_kernel, bucket),
        [jax.ShapeDtypeStruct((capacity, columns), BF16)],
        [VMEM] * 6,
        (flags, base, left_top, own, theirs, slots),
        4 * capacity * columns * group_levels * top_width,
        4 << 20,
        24,
        scratch=[
            pltpu.VMEM((leaves * filled, 128), BF16),
            pltpu.VMEM((leaves, filled, 128), F32),
        ],
    )[0]
    returned = lax.all_to_all(
        leaving.reshape(leaves, bucket, columns), everyone, split_axis=0, concat_axis=0, tiled=True
    )
    return call(
        unpack_kernel,
        [jax.ShapeDtypeStruct((count, columns), F32)],
        [VMEM] * 3,
        (order, upper, returned.reshape(capacity, columns)),
        2 * capacity * count * columns,
        4 << 20,
        16,
        out_specs=[HBM],
        scratch=[pltpu.VMEM((count, 128), F32), DMA((count // 256,))],
    )[0]


def solution(mesh):
    return jax.shard_map(
        on_device,
        mesh=mesh,
        in_specs=(
            P(("group", "member"), None),
            P(("group", "member")),
            P(),
            P(),
            P(None, ("group", "member"), None),
            P(None, None, ("group", "member"), None),
            P(None, None, ("group", "member"), None),
            P(None, None, ("group", "member"), None),
            P(None, None, ("group", "member"), None),
        ),
        out_specs=P(("group", "member"), None),
        check_vma=False,
    )
```

```python
import functools

import jax
import jax.numpy as jnp
from jax import lax
from jax.experimental import pallas as pl
from jax.experimental.pallas import tpu as pltpu
from jax.sharding import PartitionSpec as P

F32 = jnp.float32
BF16 = jnp.bfloat16
F16 = jnp.float16
I32 = jnp.int32
VMEM = pl.BlockSpec(memory_space=pltpu.VMEM)
SMEM = pl.BlockSpec(memory_space=pltpu.SMEM)
HBM = pl.BlockSpec(memory_space=pltpu.HBM)
DMA = pltpu.SemaphoreType.DMA


def iota(shape, dim):
    return lax.broadcasted_iota(I32, shape, dim)


def hot(mask):
    return jnp.where(mask, 1.0, 0.0).astype(BF16)


def dot(a, b, over=(1, 0)):
    return lax.dot_general(
        a, b, (((over[0],), (over[1],)), ((), ())), preferred_element_type=F32
    )


def call(kernel, outs, ins, args, flops, moved, limit, scratch=(), **more):
    return pl.pallas_call(
        kernel,
        out_shape=outs,
        in_specs=ins,
        out_specs=more.pop("out_specs", [VMEM] * len(outs)),
        scratch_shapes=scratch,
        cost_estimate=pl.CostEstimate(flops=flops, bytes_accessed=moved, transcendentals=0),
        compiler_params=pltpu.CompilerParams(vmem_limit_bytes=limit << 20),
        **more,
    )(*args)


def partner(block, axis, apart):
    count = lax.axis_size(axis)
    route = []
    for low in range(count):
        high = low | 1 << apart
        if high != low and high < count:
            route += [(low, high), (high, low)]
    return lax.ppermute(block, axis, route)


def far(*arrays):
    return [pltpu.with_memory_space_constraint(array, pltpu.HBM) for array in arrays]


def bound(mine, other):
    return jnp.clip(jnp.maximum(mine, other) + 1.0, -100.0, 126.0)


def narrow(rows, power):
    return jnp.concatenate([rows * jnp.exp2(14.0 - power[:1]), power]).astype(F16)


def widen(sent):
    power = sent[-8:].astype(F32)
    return sent[:-8].astype(F32) * jnp.exp2(power[:1] - 14.0), power


def turn(block):
    half = block.shape[1] // 2
    return jnp.where(iota(block.shape, 1) < half, -1.0, 1.0) * pltpu.roll(block, half, 1)


def rank_of(ranks, level, levels):
    device = lax.axis_index("group") * lax.axis_size("member") + lax.axis_index("member")
    return ranks[(1 << level) - 2 + jnp.right_shift(device, levels - level)]


def pack_kernel(leaves, bucket, sizes_in, position_in, rows_in, packed, places, *scratch):
    sizes, position, rows, ordered, near, sems, out_sems = scratch
    copies = [
        pltpu.make_async_copy(source, target, sems.at[i])
        for i, (source, target) in enumerate(
            [(position_in, position), (rows_in, rows), (sizes_in, sizes)]
        )
    ]
    for copy in copies:
        copy.start()
    copies[0].wait()
    count = rows.shape[0]
    padded = packed.shape[1]
    shift = leaves.bit_length() - 1
    here = position[...]
    window = jnp.right_shift(here, shift)
    copies[1].wait()
    values = rows[...]
    block = 512
    for low in range(0, count, block):
        ordered[low : low + block, :] = dot(hot(iota((block, count), 0) + low == window), values)
    ordered[count:, :] = jnp.zeros((padded, 128), F32)
    copies[2].wait()
    zero = jnp.zeros((1, count), I32)
    owner, first = zero, zero
    starts = [0]
    for c in range(leaves):
        starts.append(starts[-1] + jnp.right_shift(sizes[c], shift))
        beyond = window >= starts[-1]
        owner = owner + beyond.astype(I32)
        first = jnp.where(beyond, starts[-1], first)
    offset = jnp.bitwise_and(here, leaves - 1).astype(F32)
    picked = jnp.where(iota((leaves, count), 0) == owner, offset, 0.0).astype(BF16)
    offsets = dot(picked, hot(iota((128, count), 0) == window - first), (1, 1))
    places[...] = owner * bucket + window - first
    line = iota((padded, 128), 0)
    chunk = leaves // 8
    out = []
    for c in range(leaves):
        data = ordered[pl.ds(starts[c], padded), :]
        data = jnp.where(line < starts[c + 1] - starts[c], data, 0.0)
        data = jnp.where(line == bucket, offsets[c : c + 1, :], data)
        near[c] = data.astype(BF16)
        if c % chunk == chunk - 1:
            part = pl.ds(c + 1 - chunk, chunk)
            out.append(pltpu.make_async_copy(near.at[part], packed.at[part], out_sems.at[c // chunk]))
            out[-1].start()
    for copy in out:
        copy.wait()


def near_kernel(ranks, right_top_in, right_low_in, right, flags, sems):
    tops, parts, capacity, width = right_top_in.shape
    levels, _, rows, _ = right_low_in.shape
    pairs = []
    for level in range(tops):
        for p in range(parts):
            place = (pl.ds(p * capacity, capacity), pl.ds(level * width, width))
            pairs.append((right_top_in.at[level, p], right.at[place]))
    at = parts * capacity
    for low in range(0, capacity, 256):
        for p in range(parts):
            for level in range(levels):
                source = right_low_in.at[level, p, :, pl.ds(low, 256)]
                pairs.append((source, right.at[pl.ds(at, rows), :]))
                at += rows
    copies = [pltpu.make_async_copy(a, b, sems.at[i]) for i, (a, b) in enumerate(pairs)]
    for copy in copies:
        copy.start()
    row, lane = iota(flags.shape, 0), iota(flags.shape, 1)
    marks = jnp.where(row == 0, 1 - jnp.bitwise_and(lax.axis_index("member"), 1), 0)
    for level in range(1, tops + 1):
        counts = (lane < rank_of(ranks, level, tops + levels)).astype(I32)
        marks = jnp.where(row == level, counts, marks)
    flags[...] = marks.astype(F32)
    for copy in copies:
        copy.wait()


def way_kernel(targets, places, after, slots, order, upper):
    groups, part = targets.shape
    lanes = iota((part, 128), 1)
    for g in range(groups):
        target = jnp.transpose(jnp.broadcast_to(targets[g : g + 1, :], (128, part)))
        for low in range(0, part, 128):
            slots[g * part : (g + 1) * part, low : low + 128] = hot(target == lanes + low)
    count, folded = order.shape
    place = jnp.transpose(jnp.broadcast_to(places[...], (128, count)))
    beyond = place >= folded
    upper[...] = beyond.astype(I32)
    place = jnp.where(beyond, place - folded, place)
    block = 256
    lanes = iota((block, 128), 1)
    for low in range(0, count, block):
        for at in range(0, folded, 128):
            order[low : low + block, at : at + 128] = hot(place[low : low + block] == lanes + at)


def stage_kernel(left_top_in, left_low_in, after, left_top, left_low, raw, sems):
    copies = [
        pltpu.make_async_copy(left_low_in, raw, sems.at[0]),
        pltpu.make_async_copy(left_top_in, left_top, sems.at[1]),
    ]
    for copy in copies:
        copy.start()
    copies[0].wait()
    levels, parts, width, capacity = raw.shape
    left_low[...] = jnp.transpose(raw[...].reshape(levels * parts * width, capacity))
    copies[1].wait()


def field_kernel(leaves, bucket, tops, levels, arrived, right, *rest):
    pair, targets, send, keep, whole = rest
    capacity = leaves * bucket
    padded = arrived.shape[1]
    part = leaves * 8
    groups = targets.shape[0]
    core = jnp.bitwise_and(lax.axis_index("member"), 1)
    last = arrived[:, padded - 16 :, :].reshape(leaves * 16, 128)
    row = iota((leaves * 16, part), 0)
    spread = jnp.right_shift(iota((leaves * 16, part), 1), 3) * 16 + bucket % 16 == row
    spread_offsets = dot(last, hot(spread), (0, 0))[: groups * 8].reshape(groups, 8, part)
    lane_window = jnp.bitwise_and(iota((8, part), 1), 7)
    own = (lane_window == iota((8, part), 0))[None]
    target = jnp.sum(jnp.where(own, spread_offsets, 0.0), axis=1).astype(I32)
    target = target + lane_window[:1, :] * leaves
    targets[...] = target
    for g in range(groups):
        size = min(part, capacity - g * part)
        if g % 2 == 0:
            both = arrived[:, g * 8 : g * 8 + 16, :].astype(F32)
        chunk = both[:, g % 2 * 8 : g % 2 * 8 + 8, :].reshape(part, 128).astype(BF16)
        placed = dot(hot(iota((part, part), 0) == target[g : g + 1, :]), chunk)
        pair[0, g * part : g * part + size, :] = placed[:size].astype(BF16)
        pair[1, g * part : g * part + size, :] = turn(placed)[:size].astype(BF16)
    plain = jnp.transpose(pair[0])
    turned = jnp.concatenate([-plain[64:], plain[:64]], axis=0)
    upper = dot(plain, right[:capacity, :]) + dot(turned, right[capacity : 2 * capacity, :])
    top_rows = tops * 128
    for level in range(tops):
        whole[level * 128 : (level + 1) * 128, :] = upper[:, level * 128 : (level + 1) * 128]
    rows = whole.shape[0] - top_rows
    width = rows // levels
    lower = jnp.zeros((rows, 128), F32)
    at = 2 * capacity
    for low in range(0, capacity, 256):
        for p in range(2):
            lower += dot(right[at : at + rows, :], pair[p, low : low + 256, :])
            at += rows
    whole[top_rows:, :] = lower
    at = 0
    low = 0
    for half in [tops * 64] + [width // 2] * (levels - 1):
        mine = pl.multiple_of(low + core * half, 8)
        other = pl.multiple_of(low + (1 - core) * half, 8)
        keep[at : at + half, :] = whole[pl.ds(mine, half), :]
        send[at : at + half, :] = whole[pl.ds(other, half), :]
        at += half
        low += 2 * half
    send[at : at + width, :] = lower[(levels - 1) * width :]
    largest = jnp.max(jnp.abs(whole[...]), axis=0, keepdims=True)
    power = jnp.clip(jnp.ceil(jnp.log2(largest + 1e-30)) + 1.0, -100.0, 126.0)
    send[at + width :, :] = jnp.broadcast_to(power, (8, 128))
    keep[at:, :] = jnp.broadcast_to(power, (8, 128))


def diag_kernel(first, block_in, pair, after, out, block, sems):
    count, _, height, _ = block.shape
    copies = []
    for j in range(count):
        rows = pl.ds((first + j) * height, height)
        copies.append(pltpu.make_async_copy(block_in.at[:, rows, :], block.at[j], sems.at[j]))
        copies[j].start()
    for j in range(count):
        copies[j].wait()
        out[j * height : (j + 1) * height, :] = dot(block[j, 0], pair[0]) + dot(block[j, 1], pair[1])


def merged(core, own, theirs, at, half):
    a, b = own[at : at + half, :].astype(F32), theirs[at : at + half, :].astype(F32)
    return jnp.concatenate([jnp.where(core == 0, a, b), jnp.where(core == 0, b, a)], axis=0)


def low_kernel(pieces, tops, ranks, *rest):
    bases = rest[:pieces]
    left_low, nearest, own, theirs, out = rest[pieces:]
    width = nearest.shape[0]
    levels = left_low.shape[1] // (2 * width)
    core = jnp.bitwise_and(lax.axis_index("member"), 1)
    half = width // 2
    stacked = []
    for level in range(levels):
        if level < levels - 1:
            coef = merged(core, own, theirs, level * half, half)
        else:
            coef = nearest[...]
        rank = rank_of(ranks, 1 + tops + level, tops + levels)
        coef = jnp.where(iota(coef.shape, 0) < rank, coef, 0.0)
        stacked += [coef, turn(coef)]
    stacked = jnp.concatenate(stacked, axis=0).astype(BF16)
    low = 0
    for base in bases:
        rows = slice(low, low + base.shape[0])
        out[rows, :] = base[...] + dot(left_low[rows, :], stacked)
        low += base.shape[0]


def out_kernel(bucket, flags, base, left_top, own, theirs, slots, packed, spare, ordered):
    capacity = base.shape[0]
    part = slots.shape[1]
    groups = slots.shape[0] // part
    leaves = part // 8
    first = flags[:1, :] > 0
    levels = left_top.shape[0]
    half = own.shape[0]
    stacked = []
    for level in range(levels):
        pick = (own, theirs) if level == 0 else (theirs, own)
        coef = jnp.where(first, pick[0][...].astype(F32), pick[1][...].astype(F32))
        coef = jnp.where(flags[1 + level : 2 + level, :] > 0, coef, 0.0)
        turned = jnp.concatenate([-coef[half // 2 :], coef[: half // 2]], axis=0)
        stacked += [jnp.transpose(coef), jnp.transpose(turned)]
    stacked = jnp.concatenate(stacked, axis=0).astype(BF16)
    if groups * part > capacity:
        spare[capacity:, :] = jnp.zeros((groups * part - capacity, 128), BF16)
    factors = [left_top[level, p] for level in range(levels) for p in range(2)]
    total = base[...] + dot(jnp.concatenate(factors, axis=1), stacked)
    spare[:capacity, :] = total.astype(BF16)
    for g in range(groups):
        moved = dot(slots[g * part : (g + 1) * part, :], spare[g * part : (g + 1) * part, :])
        ordered[:, g * 8 : g * 8 + 8, :] = moved.reshape(leaves, 8, 128)
    packed[...] = ordered[:, :bucket, :].reshape(capacity, 128).astype(BF16)


def unpack_kernel(order, upper, returned, out, near, sems):
    count, folded = order.shape
    wide = jnp.concatenate([returned[:folded, :], returned[folded:, :]], axis=1)
    block = 256
    copies = []
    for low in range(0, count, block):
        rows = pl.ds(low, block)
        both = dot(order[low : low + block, :], wide)
        near[rows, :] = jnp.where(upper[low : low + block, :] != 0, both[:, 128:], both[:, :128])
        copies.append(pltpu.make_async_copy(near.at[rows, :], out.at[rows, :], sems.at[low // block]))
        copies[-1].start()
    for copy in copies:
        copy.wait()


def on_device(
    mesh_vector,
    cluster_position,
    cluster_sizes,
    block_ranks,
    diag_block,
    top_left,
    top_right,
    low_left,
    low_right,
):
    groups = lax.axis_size("group")
    members = lax.axis_size("member")
    leaves = groups * members
    group_levels = groups.bit_length() - 1
    member_levels = members.bit_length() - 1
    capacity = diag_block.shape[1]
    bucket = capacity // leaves
    padded = (bucket + 16) // 16 * 16
    filled = (bucket + 7) // 8 * 8
    count, columns = mesh_vector.shape
    everyone = ("group", "member")
    low_left = jnp.swapaxes(low_left, 2, 3)
    low_right = jnp.swapaxes(low_right, 2, 3)
    width = low_left.shape[2]
    top_width = top_left.shape[3]
    far_flops = 4 * capacity * columns * (group_levels * top_width + member_levels * width)

    packed, places = call(
        functools.partial(pack_kernel, leaves, bucket),
        [
            jax.ShapeDtypeStruct((leaves, padded, columns), BF16),
            jax.ShapeDtypeStruct((1, count), I32),
        ],
        [HBM] * 3,
        far(cluster_sizes, cluster_position.reshape(1, count), mesh_vector),
        2 * count * count * columns,
        4 << 20,
        16,
        out_specs=[HBM, VMEM],
        scratch=[
            pltpu.SMEM((leaves,), I32),
            pltpu.VMEM((1, count), I32),
            pltpu.VMEM((count, columns), BF16),
            pltpu.VMEM((count + padded, columns), F32),
            pltpu.VMEM((leaves, padded, columns), BF16),
            DMA((3,)),
            DMA((8,)),
        ],
    )
    arrived = lax.all_to_all(packed, everyone, split_axis=0, concat_axis=0, tiled=True)
    ranked = group_levels * top_width + member_levels * width
    right, flags = call(
        near_kernel,
        [
            pltpu.VMEM((2 * ranked * capacity // 256, 256), BF16),
            jax.ShapeDtypeStruct((8, columns), F32),
        ],
        [SMEM, HBM, HBM],
        (block_ranks, *far(top_right, low_right)),
        0,
        6 << 20,
        16,
        scratch=[DMA((2 * group_levels + 2 * member_levels * capacity // 256,))],
    )
    tops = group_levels * columns // 2
    shared = tops + (member_levels - 1) * width // 2
    pair, targets, send, keep = call(
        functools.partial(field_kernel, leaves, bucket, group_levels, member_levels),
        [
            jax.ShapeDtypeStruct((2, capacity, columns), BF16),
            jax.ShapeDtypeStruct((filled // 8, leaves * 8), I32),
            jax.ShapeDtypeStruct((shared + width + 8, columns), F32),
            jax.ShapeDtypeStruct((shared + 8, columns), F32),
        ],
        [VMEM, VMEM],
        (arrived, right),
        far_flops,
        6 << 20,
        24,
        scratch=[pltpu.VMEM((2 * shared + width, columns), F32)],
    )
    height = capacity // 8

    def diagonal(first, chunks, after):
        return call(
            functools.partial(diag_kernel, first),
            [jax.ShapeDtypeStruct((chunks * height, columns), F32)],
            [HBM, VMEM, pl.BlockSpec(memory_space=pl.ANY)],
            (*far(diag_block), pair, after),
            4 * chunks * height * capacity * columns,
            4 * chunks * height * capacity,
            24,
            scratch=[pltpu.VMEM((chunks, 2, height, capacity), BF16), DMA((chunks,))],
        )[0]

    received = partner(send, "member", 0)
    slots, order, upper = call(
        way_kernel,
        [
            jax.ShapeDtypeStruct((leaves * filled, leaves * 8), BF16),
            jax.ShapeDtypeStruct((count, capacity // 2), BF16),
            jax.ShapeDtypeStruct((count, 128), I32),
        ],
        [VMEM, VMEM, pl.BlockSpec(memory_space=pl.ANY)],
        (targets, places, send),
        0,
        8 << 20,
        16,
    )
    received, slots, order, upper = lax.optimization_barrier((received, slots, order, upper))
    nearest = received[shared : shared + width]
    running = keep[:shared] + received[:shared]
    power = bound(keep[shared:], received[shared + width :])
    bases = []
    coefs = []
    for bit in range(1, member_levels):
        rest = running.shape[0] - width // 2
        received = partner(narrow(running, power), "member", bit)
        if bit == 1:
            bases.append(diagonal(0, 4, running))
            received, bases[0] = lax.optimization_barrier((received, bases[0]))
        if bit == member_levels - 1:
            bases.append(diagonal(4, 4, running))
            received, bases[1] = lax.optimization_barrier((received, bases[1]))
        received, other = widen(received)
        power = bound(power, other)
        coefs.insert(0, received[rest:].astype(BF16))
        running = running[:rest] + received[:rest]
    routes = [[], []]
    for low in range(groups):
        for near in range(0, members, 2):
            at = low * members + near
            routes[0] += [(at, (low ^ 2) * members + near), (at + 1, (low ^ 1) * members + near + 1)]
            routes[1] += [(at, (low ^ 3) * members + near), (at + 1, low * members + (near ^ 2) + 1)]
    sums = narrow(running, power)
    heard = [lax.ppermute(sums, everyone, route) for route in routes]
    left_top, left_low = call(
        stage_kernel,
        [
            pltpu.VMEM(top_left.shape, BF16),
            pltpu.VMEM((capacity, member_levels * 2 * width), BF16),
        ],
        [HBM, HBM, pl.BlockSpec(memory_space=pl.ANY)],
        (*far(top_left, low_left), running),
        0,
        8 << 20,
        24,
        scratch=[pltpu.VMEM(low_left.shape, BF16), DMA((2,))],
    )
    heard, left_top, left_low = lax.optimization_barrier((heard, left_top, left_low))
    heard = [widen(block)[0] for block in heard]
    own = (heard[0] + jnp.where(flags[:1] > 0, heard[1], 0.0)).astype(BF16)
    own_low = jnp.concatenate(coefs)
    their_low, own = lax.optimization_barrier((partner(own_low, "member", 0), own))
    theirs = partner(own, "member", 0)
    base = call(
        functools.partial(low_kernel, len(bases), group_levels),
        [jax.ShapeDtypeStruct((capacity, columns), F32)],
        [SMEM] + [VMEM] * (len(bases) + 4),
        (block_ranks, *bases, left_low, nearest, own_low, their_low),
        4 * capacity * columns * member_levels * width,
        3 << 20,
        16,
    )[0]

    leaving = call(
        functools.partial(out_kernel, bucket),
        [jax.ShapeDtypeStruct((capacity, columns), BF16)],
        [VMEM] * 6,
        (flags, base, left_top, own, theirs, slots),
        4 * capacity * columns * group_levels * top_width,
        4 << 20,
        24,
        scratch=[
            pltpu.VMEM((leaves * filled, 128), BF16),
            pltpu.VMEM((leaves, filled, 128), F32),
        ],
    )[0]
    returned = lax.all_to_all(
        leaving.reshape(leaves, bucket, columns), everyone, split_axis=0, concat_axis=0, tiled=True
    )
    return call(
        unpack_kernel,
        [jax.ShapeDtypeStruct((count, columns), F32)],
        [VMEM] * 3,
        (order, upper, returned.reshape(capacity, columns)),
        2 * capacity * count * columns,
        4 << 20,
        16,
        out_specs=[HBM],
        scratch=[pltpu.VMEM((count, 128), F32), DMA((count // 256,))],
    )[0]


def solution(mesh):
    return jax.shard_map(
        on_device,
        mesh=mesh,
        in_specs=(
            P(("group", "member"), None),
            P(("group", "member")),
            P(),
            P(),
            P(None, ("group", "member"), None),
            P(None, None, ("group", "member"), None),
            P(None, None, ("group", "member"), None),
            P(None, None, ("group", "member"), None),
            P(None, None, ("group", "member"), None),
        ),
        out_specs=P(("group", "member"), None),
        check_vma=False,
    )
```

```python
import functools

import jax
import jax.numpy as jnp
from jax import lax
from jax.experimental import pallas as pl
from jax.experimental.pallas import tpu as pltpu
from jax.sharding import PartitionSpec as P

F32 = jnp.float32
BF16 = jnp.bfloat16
F16 = jnp.float16
I32 = jnp.int32
VMEM = pl.BlockSpec(memory_space=pltpu.VMEM)
SMEM = pl.BlockSpec(memory_space=pltpu.SMEM)
HBM = pl.BlockSpec(memory_space=pltpu.HBM)
DMA = pltpu.SemaphoreType.DMA


def iota(shape, dim):
    return lax.broadcasted_iota(I32, shape, dim)


def hot(mask):
    return jnp.where(mask, 1.0, 0.0).astype(BF16)


def dot(a, b, over=(1, 0)):
    return lax.dot_general(
        a, b, (((over[0],), (over[1],)), ((), ())), preferred_element_type=F32
    )


def call(kernel, outs, ins, args, flops, moved, limit, scratch=(), **more):
    return pl.pallas_call(
        kernel,
        out_shape=outs,
        in_specs=ins,
        out_specs=more.pop("out_specs", [VMEM] * len(outs)),
        scratch_shapes=scratch,
        cost_estimate=pl.CostEstimate(flops=flops, bytes_accessed=moved, transcendentals=0),
        compiler_params=pltpu.CompilerParams(vmem_limit_bytes=limit << 20),
        **more,
    )(*args)


def partner(block, axis, apart):
    count = lax.axis_size(axis)
    route = []
    for low in range(count):
        high = low | 1 << apart
        if high != low and high < count:
            route += [(low, high), (high, low)]
    return lax.ppermute(block, axis, route)


def far(*arrays):
    return [pltpu.with_memory_space_constraint(array, pltpu.HBM) for array in arrays]


def bound(mine, other):
    return jnp.clip(jnp.maximum(mine, other) + 1.0, -100.0, 126.0)


def narrow(rows, power):
    return jnp.concatenate([rows * jnp.exp2(14.0 - power[:1]), power]).astype(F16)


def widen(sent):
    power = sent[-8:].astype(F32)
    return sent[:-8].astype(F32) * jnp.exp2(power[:1] - 14.0), power


def turn(block):
    half = block.shape[1] // 2
    return jnp.where(iota(block.shape, 1) < half, -1.0, 1.0) * pltpu.roll(block, half, 1)


def rank_of(ranks, level, levels):
    device = lax.axis_index("group") * lax.axis_size("member") + lax.axis_index("member")
    return ranks[(1 << level) - 2 + jnp.right_shift(device, levels - level)]


def pack_kernel(leaves, bucket, sizes_in, position_in, rows_in, packed, places, *scratch):
    sizes, position, rows, ordered, near, sems, out_sems = scratch
    copies = [
        pltpu.make_async_copy(source, target, sems.at[i])
        for i, (source, target) in enumerate(
            [(position_in, position), (rows_in, rows), (sizes_in, sizes)]
        )
    ]
    for copy in copies:
        copy.start()
    copies[0].wait()
    count = rows.shape[0]
    padded = packed.shape[1]
    shift = leaves.bit_length() - 1
    here = position[...]
    window = jnp.right_shift(here, shift)
    copies[1].wait()
    values = rows[...]
    block = 512
    for low in range(0, count, block):
        ordered[low : low + block, :] = dot(hot(iota((block, count), 0) + low == window), values)
    ordered[count:, :] = jnp.zeros((padded, 128), F32)
    copies[2].wait()
    zero = jnp.zeros((1, count), I32)
    owner, first = zero, zero
    starts = [0]
    for c in range(leaves):
        starts.append(starts[-1] + jnp.right_shift(sizes[c], shift))
        beyond = window >= starts[-1]
        owner = owner + beyond.astype(I32)
        first = jnp.where(beyond, starts[-1], first)
    offset = jnp.bitwise_and(here, leaves - 1).astype(F32)
    picked = jnp.where(iota((leaves, count), 0) == owner, offset, 0.0).astype(BF16)
    offsets = dot(picked, hot(iota((128, count), 0) == window - first), (1, 1))
    places[...] = owner * bucket + window - first
    line = iota((padded, 128), 0)
    chunk = leaves // 8
    out = []
    for c in range(leaves):
        data = ordered[pl.ds(starts[c], padded), :]
        data = jnp.where(line < starts[c + 1] - starts[c], data, 0.0)
        data = jnp.where(line == bucket, offsets[c : c + 1, :], data)
        near[c] = data.astype(BF16)
        if c % chunk == chunk - 1:
            part = pl.ds(c + 1 - chunk, chunk)
            out.append(pltpu.make_async_copy(near.at[part], packed.at[part], out_sems.at[c // chunk]))
            out[-1].start()
    for copy in out:
        copy.wait()


def near_kernel(ranks, right_top_in, right_low_in, right, flags, sems):
    tops, parts, capacity, width = right_top_in.shape
    levels, _, rows, _ = right_low_in.shape
    pairs = []
    for level in range(tops):
        for p in range(parts):
            place = (pl.ds(p * capacity, capacity), pl.ds(level * width, width))
            pairs.append((right_top_in.at[level, p], right.at[place]))
    at = parts * capacity
    for low in range(0, capacity, 256):
        for p in range(parts):
            for level in range(levels):
                source = right_low_in.at[level, p, :, pl.ds(low, 256)]
                pairs.append((source, right.at[pl.ds(at, rows), :]))
                at += rows
    copies = [pltpu.make_async_copy(a, b, sems.at[i]) for i, (a, b) in enumerate(pairs)]
    for copy in copies:
        copy.start()
    row, lane = iota(flags.shape, 0), iota(flags.shape, 1)
    marks = jnp.where(row == 0, 1 - jnp.bitwise_and(lax.axis_index("member"), 1), 0)
    for level in range(1, tops + 1):
        counts = (lane < rank_of(ranks, level, tops + levels)).astype(I32)
        marks = jnp.where(row == level, counts, marks)
    flags[...] = marks.astype(F32)
    for copy in copies:
        copy.wait()


def way_kernel(targets, places, after, slots, order, upper):
    groups, part = targets.shape
    lanes = iota((part, 128), 1)
    for g in range(groups):
        target = jnp.transpose(jnp.broadcast_to(targets[g : g + 1, :], (128, part)))
        for low in range(0, part, 128):
            slots[g * part : (g + 1) * part, low : low + 128] = hot(target == lanes + low)
    count, folded = order.shape
    place = jnp.transpose(jnp.broadcast_to(places[...], (128, count)))
    beyond = place >= folded
    upper[...] = beyond.astype(I32)
    place = jnp.where(beyond, place - folded, place)
    block = 256
    lanes = iota((block, 128), 1)
    for low in range(0, count, block):
        for at in range(0, folded, 128):
            order[low : low + block, at : at + 128] = hot(place[low : low + block] == lanes + at)


def stage_kernel(left_top_in, left_low_in, after, left_top, left_low, raw, sems):
    copies = [
        pltpu.make_async_copy(left_low_in, raw, sems.at[0]),
        pltpu.make_async_copy(left_top_in, left_top, sems.at[1]),
    ]
    for copy in copies:
        copy.start()
    copies[0].wait()
    levels, parts, width, capacity = raw.shape
    left_low[...] = jnp.transpose(raw[...].reshape(levels * parts * width, capacity))
    copies[1].wait()


def field_kernel(leaves, bucket, tops, levels, arrived, right, *rest):
    pair, targets, send, keep, whole = rest
    capacity = leaves * bucket
    padded = arrived.shape[1]
    part = leaves * 8
    groups = targets.shape[0]
    core = jnp.bitwise_and(lax.axis_index("member"), 1)
    last = arrived[:, padded - 16 :, :].reshape(leaves * 16, 128)
    row = iota((leaves * 16, part), 0)
    spread = jnp.right_shift(iota((leaves * 16, part), 1), 3) * 16 + bucket % 16 == row
    spread_offsets = dot(last, hot(spread), (0, 0))[: groups * 8].reshape(groups, 8, part)
    lane_window = jnp.bitwise_and(iota((8, part), 1), 7)
    own = (lane_window == iota((8, part), 0))[None]
    target = jnp.sum(jnp.where(own, spread_offsets, 0.0), axis=1).astype(I32)
    target = target + lane_window[:1, :] * leaves
    targets[...] = target
    for g in range(groups):
        size = min(part, capacity - g * part)
        if g % 2 == 0:
            both = arrived[:, g * 8 : g * 8 + 16, :].astype(F32)
        chunk = both[:, g % 2 * 8 : g % 2 * 8 + 8, :].reshape(part, 128).astype(BF16)
        placed = dot(hot(iota((part, part), 0) == target[g : g + 1, :]), chunk)
        pair[0, g * part : g * part + size, :] = placed[:size].astype(BF16)
        pair[1, g * part : g * part + size, :] = turn(placed)[:size].astype(BF16)
    plain = jnp.transpose(pair[0])
    turned = jnp.concatenate([-plain[64:], plain[:64]], axis=0)
    upper = dot(plain, right[:capacity, :]) + dot(turned, right[capacity : 2 * capacity, :])
    top_rows = tops * 128
    for level in range(tops):
        whole[level * 128 : (level + 1) * 128, :] = upper[:, level * 128 : (level + 1) * 128]
    rows = whole.shape[0] - top_rows
    width = rows // levels
    lower = jnp.zeros((rows, 128), F32)
    at = 2 * capacity
    for low in range(0, capacity, 256):
        for p in range(2):
            lower += dot(right[at : at + rows, :], pair[p, low : low + 256, :])
            at += rows
    whole[top_rows:, :] = lower
    at = 0
    low = 0
    for half in [tops * 64] + [width // 2] * (levels - 1):
        mine = pl.multiple_of(low + core * half, 8)
        other = pl.multiple_of(low + (1 - core) * half, 8)
        keep[at : at + half, :] = whole[pl.ds(mine, half), :]
        send[at : at + half, :] = whole[pl.ds(other, half), :]
        at += half
        low += 2 * half
    send[at : at + width, :] = lower[(levels - 1) * width :]
    largest = jnp.max(jnp.abs(whole[...]), axis=0, keepdims=True)
    power = jnp.clip(jnp.ceil(jnp.log2(largest + 1e-30)) + 1.0, -100.0, 126.0)
    send[at + width :, :] = jnp.broadcast_to(power, (8, 128))
    keep[at:, :] = jnp.broadcast_to(power, (8, 128))


def diag_kernel(first, cuts, block_in, pair, after, out, block, sems):
    low = 0
    copies = []
    for j, rows in enumerate(cuts):
        source = block_in.at[:, pl.ds(first + low, rows), :]
        copies.append(pltpu.make_async_copy(source, block.at[:, pl.ds(low, rows), :], sems.at[j]))
        copies[j].start()
        low += rows
    low = 0
    for copy, rows in zip(copies, cuts):
        copy.wait()
        part = slice(low, low + rows)
        out[part, :] = dot(block[0, part, :], pair[0]) + dot(block[1, part, :], pair[1])
        low += rows


def merged(core, own, theirs, at, half):
    a, b = own[at : at + half, :].astype(F32), theirs[at : at + half, :].astype(F32)
    return jnp.concatenate([jnp.where(core == 0, a, b), jnp.where(core == 0, b, a)], axis=0)


def low_kernel(pieces, tops, ranks, *rest):
    bases = rest[:pieces]
    left_low, nearest, own, theirs, out = rest[pieces:]
    width = nearest.shape[0]
    levels = left_low.shape[1] // (2 * width)
    core = jnp.bitwise_and(lax.axis_index("member"), 1)
    half = width // 2
    stacked = []
    for level in range(levels):
        if level < levels - 1:
            coef = merged(core, own, theirs, level * half, half)
        else:
            coef = nearest[...]
        rank = rank_of(ranks, 1 + tops + level, tops + levels)
        coef = jnp.where(iota(coef.shape, 0) < rank, coef, 0.0)
        stacked += [coef, turn(coef)]
    stacked = jnp.concatenate(stacked, axis=0).astype(BF16)
    low = 0
    for base in bases:
        rows = slice(low, low + base.shape[0])
        out[rows, :] = base[...] + dot(left_low[rows, :], stacked)
        low += base.shape[0]


def upper(level, coef, flags, left_top):
    half = coef.shape[0] // 2
    mark = jnp.where(level == 0, flags[1:2, :], flags[2:3, :])
    coef = jnp.where(mark > 0, coef.astype(F32), 0.0)
    turned = jnp.concatenate([-coef[half:], coef[:half]], axis=0)
    stacked = jnp.concatenate([jnp.transpose(coef), jnp.transpose(turned)], axis=0)
    factors = jnp.concatenate([left_top[level, 0], left_top[level, 1]], axis=1)
    return dot(factors, stacked.astype(BF16))


def own_kernel(flags, base, left_top, own, out):
    core = jnp.bitwise_and(lax.axis_index("member"), 1)
    out[...] = base[...] + upper(core, own[...], flags, left_top)


def out_kernel(bucket, flags, base, left_top, theirs, slots, packed, spare, ordered):
    capacity = base.shape[0]
    part = slots.shape[1]
    groups = slots.shape[0] // part
    leaves = part // 8
    core = jnp.bitwise_and(lax.axis_index("member"), 1)
    if groups * part > capacity:
        spare[capacity:, :] = jnp.zeros((groups * part - capacity, 128), BF16)
    total = base[...] + upper(1 - core, theirs[...], flags, left_top)
    spare[:capacity, :] = total.astype(BF16)
    for g in range(groups):
        moved = dot(slots[g * part : (g + 1) * part, :], spare[g * part : (g + 1) * part, :])
        ordered[:, g * 8 : g * 8 + 8, :] = moved.reshape(leaves, 8, 128)
    packed[...] = ordered[:, :bucket, :].reshape(capacity, 128).astype(BF16)


def unpack_kernel(order, upper, returned, out, near, sems):
    count, folded = order.shape
    wide = jnp.concatenate([returned[:folded, :], returned[folded:, :]], axis=1)
    block = 256
    copies = []
    for low in range(0, count, block):
        rows = pl.ds(low, block)
        both = dot(order[low : low + block, :], wide)
        near[rows, :] = jnp.where(upper[low : low + block, :] != 0, both[:, 128:], both[:, :128])
        copies.append(pltpu.make_async_copy(near.at[rows, :], out.at[rows, :], sems.at[low // block]))
        copies[-1].start()
    for copy in copies:
        copy.wait()


def on_device(
    mesh_vector,
    cluster_position,
    cluster_sizes,
    block_ranks,
    diag_block,
    top_left,
    top_right,
    low_left,
    low_right,
):
    groups = lax.axis_size("group")
    members = lax.axis_size("member")
    leaves = groups * members
    group_levels = groups.bit_length() - 1
    member_levels = members.bit_length() - 1
    capacity = diag_block.shape[1]
    bucket = capacity // leaves
    padded = (bucket + 16) // 16 * 16
    filled = (bucket + 7) // 8 * 8
    count, columns = mesh_vector.shape
    everyone = ("group", "member")
    low_left = jnp.swapaxes(low_left, 2, 3)
    low_right = jnp.swapaxes(low_right, 2, 3)
    width = low_left.shape[2]
    top_width = top_left.shape[3]
    far_flops = 4 * capacity * columns * (group_levels * top_width + member_levels * width)

    packed, places = call(
        functools.partial(pack_kernel, leaves, bucket),
        [
            jax.ShapeDtypeStruct((leaves, padded, columns), BF16),
            jax.ShapeDtypeStruct((1, count), I32),
        ],
        [HBM] * 3,
        far(cluster_sizes, cluster_position.reshape(1, count), mesh_vector),
        2 * count * count * columns,
        4 << 20,
        16,
        out_specs=[HBM, VMEM],
        scratch=[
            pltpu.SMEM((leaves,), I32),
            pltpu.VMEM((1, count), I32),
            pltpu.VMEM((count, columns), BF16),
            pltpu.VMEM((count + padded, columns), F32),
            pltpu.VMEM((leaves, padded, columns), BF16),
            DMA((3,)),
            DMA((8,)),
        ],
    )
    arrived = lax.all_to_all(packed, everyone, split_axis=0, concat_axis=0, tiled=True)
    ranked = group_levels * top_width + member_levels * width
    right, flags = call(
        near_kernel,
        [
            pltpu.VMEM((2 * ranked * capacity // 256, 256), BF16),
            jax.ShapeDtypeStruct((8, columns), F32),
        ],
        [SMEM, HBM, HBM],
        (block_ranks, *far(top_right, low_right)),
        0,
        6 << 20,
        16,
        scratch=[DMA((2 * group_levels + 2 * member_levels * capacity // 256,))],
    )
    tops = group_levels * columns // 2
    shared = tops + (member_levels - 1) * width // 2
    pair, targets, send, keep = call(
        functools.partial(field_kernel, leaves, bucket, group_levels, member_levels),
        [
            jax.ShapeDtypeStruct((2, capacity, columns), BF16),
            jax.ShapeDtypeStruct((filled // 8, leaves * 8), I32),
            jax.ShapeDtypeStruct((shared + width + 8, columns), F32),
            jax.ShapeDtypeStruct((shared + 8, columns), F32),
        ],
        [VMEM, VMEM],
        (arrived, right),
        far_flops,
        6 << 20,
        24,
        scratch=[pltpu.VMEM((2 * shared + width, columns), F32)],
    )
    unit = capacity // 28
    cuts = [4 * unit, 4 * unit, 3 * unit, 2 * unit, unit]

    def diagonal(first, cuts, after):
        count = sum(cuts)
        return call(
            functools.partial(diag_kernel, first, cuts),
            [jax.ShapeDtypeStruct((count, columns), F32)],
            [HBM, VMEM, pl.BlockSpec(memory_space=pl.ANY)],
            (*far(diag_block), pair, after),
            4 * count * capacity * columns,
            4 * count * capacity,
            24,
            scratch=[pltpu.VMEM((2, count, capacity), BF16), DMA((len(cuts),))],
        )[0]

    received = partner(send, "member", 0)
    slots, order, upper = call(
        way_kernel,
        [
            jax.ShapeDtypeStruct((leaves * filled, leaves * 8), BF16),
            jax.ShapeDtypeStruct((count, capacity // 2), BF16),
            jax.ShapeDtypeStruct((count, 128), I32),
        ],
        [VMEM, VMEM, pl.BlockSpec(memory_space=pl.ANY)],
        (targets, places, send),
        0,
        8 << 20,
        16,
    )
    received, slots, order, upper = lax.optimization_barrier((received, slots, order, upper))
    nearest = received[shared : shared + width]
    running = keep[:shared] + received[:shared]
    power = bound(keep[shared:], received[shared + width :])
    bases = []
    coefs = []
    for bit in range(1, member_levels):
        rest = running.shape[0] - width // 2
        received = partner(narrow(running, power), "member", bit)
        if bit == 1:
            bases.append(diagonal(0, cuts, running))
            received, bases[0] = lax.optimization_barrier((received, bases[0]))
        if bit == member_levels - 1:
            bases.append(diagonal(sum(cuts), cuts, running))
            received, bases[1] = lax.optimization_barrier((received, bases[1]))
        received, other = widen(received)
        power = bound(power, other)
        coefs.insert(0, received[rest:].astype(BF16))
        running = running[:rest] + received[:rest]
    routes = [[], []]
    for low in range(groups):
        for near in range(0, members, 2):
            at = low * members + near
            routes[0] += [(at, (low ^ 2) * members + near), (at + 1, (low ^ 1) * members + near + 1)]
            routes[1] += [(at, (low ^ 3) * members + near), (at + 1, low * members + (near ^ 2) + 1)]
    sums = narrow(running, power)
    heard = [lax.ppermute(sums, everyone, route) for route in routes]
    left_top, left_low = call(
        stage_kernel,
        [
            pltpu.VMEM(top_left.shape, BF16),
            pltpu.VMEM((capacity, member_levels * 2 * width), BF16),
        ],
        [HBM, HBM, pl.BlockSpec(memory_space=pl.ANY)],
        (*far(top_left, low_left), running),
        0,
        8 << 20,
        24,
        scratch=[pltpu.VMEM(low_left.shape, BF16), DMA((2,))],
    )
    own_low = jnp.concatenate(coefs)
    base = call(
        functools.partial(low_kernel, len(bases), group_levels),
        [jax.ShapeDtypeStruct((capacity, columns), F32)],
        [SMEM] + [VMEM] * (len(bases) + 4),
        (block_ranks, *bases, left_low, nearest, own_low, partner(own_low, "member", 0)),
        4 * capacity * columns * member_levels * width,
        3 << 20,
        16,
    )[0]
    heard = [widen(block)[0] for block in heard]
    own = (heard[0] + jnp.where(flags[:1] > 0, heard[1], 0.0)).astype(BF16)
    own, base = lax.optimization_barrier((own, base))
    theirs = partner(own, "member", 0)
    base = call(
        own_kernel,
        [jax.ShapeDtypeStruct((capacity, columns), F32)],
        [VMEM] * 4,
        (flags, base, left_top, own),
        4 * capacity * columns * top_width,
        2 << 20,
        16,
    )[0]
    theirs, base = lax.optimization_barrier((theirs, base))

    leaving = call(
        functools.partial(out_kernel, bucket),
        [jax.ShapeDtypeStruct((capacity, columns), BF16)],
        [VMEM] * 5,
        (flags, base, left_top, theirs, slots),
        4 * capacity * columns * top_width,
        4 << 20,
        24,
        scratch=[
            pltpu.VMEM((leaves * filled, 128), BF16),
            pltpu.VMEM((leaves, filled, 128), F32),
        ],
    )[0]
    returned = lax.all_to_all(
        leaving.reshape(leaves, bucket, columns), everyone, split_axis=0, concat_axis=0, tiled=True
    )
    return call(
        unpack_kernel,
        [jax.ShapeDtypeStruct((count, columns), F32)],
        [VMEM] * 3,
        (order, upper, returned.reshape(capacity, columns)),
        2 * capacity * count * columns,
        4 << 20,
        16,
        out_specs=[HBM],
        scratch=[pltpu.VMEM((count, 128), F32), DMA((count // 256,))],
    )[0]


def solution(mesh):
    return jax.shard_map(
        on_device,
        mesh=mesh,
        in_specs=(
            P(("group", "member"), None),
            P(("group", "member")),
            P(),
            P(),
            P(None, ("group", "member"), None),
            P(None, None, ("group", "member"), None),
            P(None, None, ("group", "member"), None),
            P(None, None, ("group", "member"), None),
            P(None, None, ("group", "member"), None),
        ),
        out_specs=P(("group", "member"), None),
        check_vma=False,
    )
```

```python
import functools

import jax
import jax.numpy as jnp
from jax import lax
from jax.experimental import pallas as pl
from jax.experimental.pallas import tpu as pltpu
from jax.sharding import PartitionSpec as P

F32 = jnp.float32
BF16 = jnp.bfloat16
F16 = jnp.float16
I32 = jnp.int32
VMEM = pl.BlockSpec(memory_space=pltpu.VMEM)
SMEM = pl.BlockSpec(memory_space=pltpu.SMEM)
HBM = pl.BlockSpec(memory_space=pltpu.HBM)
DMA = pltpu.SemaphoreType.DMA


def iota(shape, dim):
    return lax.broadcasted_iota(I32, shape, dim)


def hot(mask):
    return jnp.where(mask, 1.0, 0.0).astype(BF16)


def dot(a, b, over=(1, 0)):
    return lax.dot_general(
        a, b, (((over[0],), (over[1],)), ((), ())), preferred_element_type=F32
    )


def call(kernel, outs, ins, args, flops, moved, limit, scratch=(), **more):
    return pl.pallas_call(
        kernel,
        out_shape=outs,
        in_specs=ins,
        out_specs=more.pop("out_specs", [VMEM] * len(outs)),
        scratch_shapes=scratch,
        cost_estimate=pl.CostEstimate(flops=flops, bytes_accessed=moved, transcendentals=0),
        compiler_params=pltpu.CompilerParams(vmem_limit_bytes=limit << 20),
        **more,
    )(*args)


def partner(block, axis, apart):
    count = lax.axis_size(axis)
    route = []
    for low in range(count):
        high = low | 1 << apart
        if high != low and high < count:
            route += [(low, high), (high, low)]
    return lax.ppermute(block, axis, route)


def far(*arrays):
    return [pltpu.with_memory_space_constraint(array, pltpu.HBM) for array in arrays]


def bound(mine, other):
    return jnp.clip(jnp.maximum(mine, other) + 1.0, -100.0, 126.0)


def narrow(rows, power):
    return jnp.concatenate([rows * jnp.exp2(14.0 - power[:1]), power]).astype(F16)


def widen(sent):
    power = sent[-8:].astype(F32)
    return sent[:-8].astype(F32) * jnp.exp2(power[:1] - 14.0), power


def turn(block):
    half = block.shape[1] // 2
    return jnp.where(iota(block.shape, 1) < half, -1.0, 1.0) * pltpu.roll(block, half, 1)


def rank_of(ranks, level, levels):
    device = lax.axis_index("group") * lax.axis_size("member") + lax.axis_index("member")
    return ranks[(1 << level) - 2 + jnp.right_shift(device, levels - level)]


def pack_kernel(leaves, bucket, sizes_in, position_in, rows_in, packed, places, *scratch):
    sizes, position, rows, ordered, near, sems, out_sems = scratch
    copies = [
        pltpu.make_async_copy(source, target, sems.at[i])
        for i, (source, target) in enumerate(
            [(position_in, position), (rows_in, rows), (sizes_in, sizes)]
        )
    ]
    for copy in copies:
        copy.start()
    copies[0].wait()
    count = rows.shape[0]
    padded = packed.shape[1]
    shift = leaves.bit_length() - 1
    here = position[...]
    window = jnp.right_shift(here, shift)
    copies[1].wait()
    values = rows[...]
    block = 512
    for low in range(0, count, block):
        ordered[low : low + block, :] = dot(hot(iota((block, count), 0) + low == window), values)
    ordered[count:, :] = jnp.zeros((padded, 128), F32)
    copies[2].wait()
    zero = jnp.zeros((1, count), I32)
    owner, first = zero, zero
    starts = [0]
    for c in range(leaves):
        starts.append(starts[-1] + jnp.right_shift(sizes[c], shift))
        beyond = window >= starts[-1]
        owner = owner + beyond.astype(I32)
        first = jnp.where(beyond, starts[-1], first)
    offset = jnp.bitwise_and(here, leaves - 1).astype(F32)
    picked = jnp.where(iota((leaves, count), 0) == owner, offset, 0.0).astype(BF16)
    offsets = dot(picked, hot(iota((128, count), 0) == window - first), (1, 1))
    places[...] = owner * bucket + window - first
    line = iota((padded, 128), 0)
    chunk = leaves // 8
    out = []
    for c in range(leaves):
        data = ordered[pl.ds(starts[c], padded), :]
        data = jnp.where(line < starts[c + 1] - starts[c], data, 0.0)
        data = jnp.where(line == bucket, offsets[c : c + 1, :], data)
        near[c] = data.astype(BF16)
        if c % chunk == chunk - 1:
            part = pl.ds(c + 1 - chunk, chunk)
            out.append(pltpu.make_async_copy(near.at[part], packed.at[part], out_sems.at[c // chunk]))
            out[-1].start()
    for copy in out:
        copy.wait()


def near_kernel(ranks, right_top_in, right_low_in, right, flags, sems):
    tops, parts, capacity, width = right_top_in.shape
    levels, _, rows, _ = right_low_in.shape
    pairs = []
    for level in range(tops):
        for p in range(parts):
            place = (pl.ds(p * capacity, capacity), pl.ds(level * width, width))
            pairs.append((right_top_in.at[level, p], right.at[place]))
    at = parts * capacity
    for low in range(0, capacity, 256):
        for p in range(parts):
            for level in range(levels):
                source = right_low_in.at[level, p, :, pl.ds(low, 256)]
                pairs.append((source, right.at[pl.ds(at, rows), :]))
                at += rows
    copies = [pltpu.make_async_copy(a, b, sems.at[i]) for i, (a, b) in enumerate(pairs)]
    for copy in copies:
        copy.start()
    row, lane = iota(flags.shape, 0), iota(flags.shape, 1)
    marks = jnp.where(row == 0, 1 - jnp.bitwise_and(lax.axis_index("member"), 1), 0)
    for level in range(1, tops + 1):
        counts = (lane < rank_of(ranks, level, tops + levels)).astype(I32)
        marks = jnp.where(row == level, counts, marks)
    flags[...] = marks.astype(F32)
    for copy in copies:
        copy.wait()


def way_kernel(targets, places, after, slots, order, upper):
    groups, part = targets.shape
    lanes = iota((part, 128), 1)
    for g in range(groups):
        target = jnp.transpose(jnp.broadcast_to(targets[g : g + 1, :], (128, part)))
        for low in range(0, part, 128):
            slots[g * part : (g + 1) * part, low : low + 128] = hot(target == lanes + low)
    count, folded = order.shape
    place = jnp.transpose(jnp.broadcast_to(places[...], (128, count)))
    beyond = place >= folded
    upper[...] = beyond.astype(I32)
    place = jnp.where(beyond, place - folded, place)
    block = 256
    lanes = iota((block, 128), 1)
    for low in range(0, count, block):
        for at in range(0, folded, 128):
            order[low : low + block, at : at + 128] = hot(place[low : low + block] == lanes + at)


def stage_kernel(first, left_top_in, left_low_in, block_in, pair, after, *rest):
    left_top, left_low, out, raw, block, sems = rest
    copies = [pltpu.make_async_copy(left_low_in, raw, sems.at[0])]
    count, _, height, _ = block.shape
    for j in range(count):
        rows = pl.ds((first + j) * height, height)
        copies.append(pltpu.make_async_copy(block_in.at[:, rows, :], block.at[j], sems.at[1 + j]))
    copies.append(pltpu.make_async_copy(left_top_in, left_top, sems.at[1 + count]))
    for copy in copies:
        copy.start()
    copies[0].wait()
    levels, parts, width, capacity = raw.shape
    left_low[...] = jnp.transpose(raw[...].reshape(levels * parts * width, capacity))
    for j in range(count):
        copies[1 + j].wait()
        out[j * height : (j + 1) * height, :] = dot(block[j, 0], pair[0]) + dot(block[j, 1], pair[1])
    copies[-1].wait()


def field_kernel(leaves, bucket, tops, levels, arrived, right, *rest):
    pair, targets, send, keep, whole = rest
    capacity = leaves * bucket
    padded = arrived.shape[1]
    part = leaves * 8
    groups = targets.shape[0]
    core = jnp.bitwise_and(lax.axis_index("member"), 1)
    last = arrived[:, padded - 16 :, :].reshape(leaves * 16, 128)
    row = iota((leaves * 16, part), 0)
    spread = jnp.right_shift(iota((leaves * 16, part), 1), 3) * 16 + bucket % 16 == row
    spread_offsets = dot(last, hot(spread), (0, 0))[: groups * 8].reshape(groups, 8, part)
    lane_window = jnp.bitwise_and(iota((8, part), 1), 7)
    own = (lane_window == iota((8, part), 0))[None]
    target = jnp.sum(jnp.where(own, spread_offsets, 0.0), axis=1).astype(I32)
    target = target + lane_window[:1, :] * leaves
    targets[...] = target
    for g in range(groups):
        size = min(part, capacity - g * part)
        if g % 2 == 0:
            both = arrived[:, g * 8 : g * 8 + 16, :].astype(F32)
        chunk = both[:, g % 2 * 8 : g % 2 * 8 + 8, :].reshape(part, 128).astype(BF16)
        placed = dot(hot(iota((part, part), 0) == target[g : g + 1, :]), chunk)
        pair[0, g * part : g * part + size, :] = placed[:size].astype(BF16)
        pair[1, g * part : g * part + size, :] = turn(placed)[:size].astype(BF16)
    plain = jnp.transpose(pair[0])
    turned = jnp.concatenate([-plain[64:], plain[:64]], axis=0)
    upper = dot(plain, right[:capacity, :]) + dot(turned, right[capacity : 2 * capacity, :])
    top_rows = tops * 128
    for level in range(tops):
        whole[level * 128 : (level + 1) * 128, :] = upper[:, level * 128 : (level + 1) * 128]
    rows = whole.shape[0] - top_rows
    width = rows // levels
    lower = jnp.zeros((rows, 128), F32)
    at = 2 * capacity
    for low in range(0, capacity, 256):
        for p in range(2):
            lower += dot(right[at : at + rows, :], pair[p, low : low + 256, :])
            at += rows
    whole[top_rows:, :] = lower
    at = 0
    low = 0
    for half in [tops * 64] + [width // 2] * (levels - 1):
        mine = pl.multiple_of(low + core * half, 8)
        other = pl.multiple_of(low + (1 - core) * half, 8)
        keep[at : at + half, :] = whole[pl.ds(mine, half), :]
        send[at : at + half, :] = whole[pl.ds(other, half), :]
        at += half
        low += 2 * half
    send[at : at + width, :] = lower[(levels - 1) * width :]
    largest = jnp.max(jnp.abs(whole[...]), axis=0, keepdims=True)
    power = jnp.clip(jnp.ceil(jnp.log2(largest + 1e-30)) + 1.0, -100.0, 126.0)
    send[at + width :, :] = jnp.broadcast_to(power, (8, 128))
    keep[at:, :] = jnp.broadcast_to(power, (8, 128))


def diag_kernel(first, block_in, pair, after, out, block, sems):
    count, _, height, _ = block.shape
    copies = []
    for j in range(count):
        rows = pl.ds((first + j) * height, height)
        copies.append(pltpu.make_async_copy(block_in.at[:, rows, :], block.at[j], sems.at[j]))
        copies[j].start()
    for j in range(count):
        copies[j].wait()
        out[j * height : (j + 1) * height, :] = dot(block[j, 0], pair[0]) + dot(block[j, 1], pair[1])


def merged(core, own, theirs, at, half):
    a, b = own[at : at + half, :].astype(F32), theirs[at : at + half, :].astype(F32)
    return jnp.concatenate([jnp.where(core == 0, a, b), jnp.where(core == 0, b, a)], axis=0)


def low_kernel(pieces, tops, ranks, *rest):
    bases = rest[:pieces]
    left_low, nearest, own, theirs, out = rest[pieces:]
    width = nearest.shape[0]
    levels = left_low.shape[1] // (2 * width)
    core = jnp.bitwise_and(lax.axis_index("member"), 1)
    half = width // 2
    stacked = []
    for level in range(levels):
        if level < levels - 1:
            coef = merged(core, own, theirs, level * half, half)
        else:
            coef = nearest[...]
        rank = rank_of(ranks, 1 + tops + level, tops + levels)
        coef = jnp.where(iota(coef.shape, 0) < rank, coef, 0.0)
        stacked += [coef, turn(coef)]
    stacked = jnp.concatenate(stacked, axis=0).astype(BF16)
    low = 0
    for base in bases:
        rows = slice(low, low + base.shape[0])
        out[rows, :] = base[...] + dot(left_low[rows, :], stacked)
        low += base.shape[0]


def out_kernel(bucket, flags, base, left_top, own, theirs, slots, packed, spare, ordered):
    capacity = base.shape[0]
    part = slots.shape[1]
    groups = slots.shape[0] // part
    leaves = part // 8
    first = flags[:1, :] > 0
    levels = left_top.shape[0]
    half = own.shape[0]
    stacked = []
    for level in range(levels):
        pick = (own, theirs) if level == 0 else (theirs, own)
        coef = jnp.where(first, pick[0][...].astype(F32), pick[1][...].astype(F32))
        coef = jnp.where(flags[1 + level : 2 + level, :] > 0, coef, 0.0)
        turned = jnp.concatenate([-coef[half // 2 :], coef[: half // 2]], axis=0)
        stacked += [jnp.transpose(coef), jnp.transpose(turned)]
    stacked = jnp.concatenate(stacked, axis=0).astype(BF16)
    if groups * part > capacity:
        spare[capacity:, :] = jnp.zeros((groups * part - capacity, 128), BF16)
    factors = [left_top[level, p] for level in range(levels) for p in range(2)]
    total = base[...] + dot(jnp.concatenate(factors, axis=1), stacked)
    spare[:capacity, :] = total.astype(BF16)
    for g in range(groups):
        moved = dot(slots[g * part : (g + 1) * part, :], spare[g * part : (g + 1) * part, :])
        ordered[:, g * 8 : g * 8 + 8, :] = moved.reshape(leaves, 8, 128)
    packed[...] = ordered[:, :bucket, :].reshape(capacity, 128).astype(BF16)


def unpack_kernel(order, upper, returned, out, near, sems):
    count, folded = order.shape
    wide = jnp.concatenate([returned[:folded, :], returned[folded:, :]], axis=1)
    block = 256
    copies = []
    for low in range(0, count, block):
        rows = pl.ds(low, block)
        both = dot(order[low : low + block, :], wide)
        near[rows, :] = jnp.where(upper[low : low + block, :] != 0, both[:, 128:], both[:, :128])
        copies.append(pltpu.make_async_copy(near.at[rows, :], out.at[rows, :], sems.at[low // block]))
        copies[-1].start()
    for copy in copies:
        copy.wait()


def on_device(
    mesh_vector,
    cluster_position,
    cluster_sizes,
    block_ranks,
    diag_block,
    top_left,
    top_right,
    low_left,
    low_right,
):
    groups = lax.axis_size("group")
    members = lax.axis_size("member")
    leaves = groups * members
    group_levels = groups.bit_length() - 1
    member_levels = members.bit_length() - 1
    capacity = diag_block.shape[1]
    bucket = capacity // leaves
    padded = (bucket + 16) // 16 * 16
    filled = (bucket + 7) // 8 * 8
    count, columns = mesh_vector.shape
    everyone = ("group", "member")
    low_left = jnp.swapaxes(low_left, 2, 3)
    low_right = jnp.swapaxes(low_right, 2, 3)
    width = low_left.shape[2]
    top_width = top_left.shape[3]
    far_flops = 4 * capacity * columns * (group_levels * top_width + member_levels * width)

    packed, places = call(
        functools.partial(pack_kernel, leaves, bucket),
        [
            jax.ShapeDtypeStruct((leaves, padded, columns), BF16),
            jax.ShapeDtypeStruct((1, count), I32),
        ],
        [HBM] * 3,
        far(cluster_sizes, cluster_position.reshape(1, count), mesh_vector),
        2 * count * count * columns,
        4 << 20,
        16,
        out_specs=[HBM, VMEM],
        scratch=[
            pltpu.SMEM((leaves,), I32),
            pltpu.VMEM((1, count), I32),
            pltpu.VMEM((count, columns), BF16),
            pltpu.VMEM((count + padded, columns), F32),
            pltpu.VMEM((leaves, padded, columns), BF16),
            DMA((3,)),
            DMA((8,)),
        ],
    )
    arrived = lax.all_to_all(packed, everyone, split_axis=0, concat_axis=0, tiled=True)
    ranked = group_levels * top_width + member_levels * width
    right, flags = call(
        near_kernel,
        [
            pltpu.VMEM((2 * ranked * capacity // 256, 256), BF16),
            jax.ShapeDtypeStruct((8, columns), F32),
        ],
        [SMEM, HBM, HBM],
        (block_ranks, *far(top_right, low_right)),
        0,
        6 << 20,
        16,
        scratch=[DMA((2 * group_levels + 2 * member_levels * capacity // 256,))],
    )
    tops = group_levels * columns // 2
    shared = tops + (member_levels - 1) * width // 2
    pair, targets, send, keep = call(
        functools.partial(field_kernel, leaves, bucket, group_levels, member_levels),
        [
            jax.ShapeDtypeStruct((2, capacity, columns), BF16),
            jax.ShapeDtypeStruct((filled // 8, leaves * 8), I32),
            jax.ShapeDtypeStruct((shared + width + 8, columns), F32),
            jax.ShapeDtypeStruct((shared + 8, columns), F32),
        ],
        [VMEM, VMEM],
        (arrived, right),
        far_flops,
        6 << 20,
        24,
        scratch=[pltpu.VMEM((2 * shared + width, columns), F32)],
    )
    height = capacity // 8

    def diagonal(first, chunks, after):
        return call(
            functools.partial(diag_kernel, first),
            [jax.ShapeDtypeStruct((chunks * height, columns), F32)],
            [HBM, VMEM, pl.BlockSpec(memory_space=pl.ANY)],
            (*far(diag_block), pair, after),
            4 * chunks * height * capacity * columns,
            4 * chunks * height * capacity,
            24,
            scratch=[pltpu.VMEM((chunks, 2, height, capacity), BF16), DMA((chunks,))],
        )[0]

    received = partner(send, "member", 0)
    slots, order, upper = call(
        way_kernel,
        [
            jax.ShapeDtypeStruct((leaves * filled, leaves * 8), BF16),
            jax.ShapeDtypeStruct((count, capacity // 2), BF16),
            jax.ShapeDtypeStruct((count, 128), I32),
        ],
        [VMEM, VMEM, pl.BlockSpec(memory_space=pl.ANY)],
        (targets, places, send),
        0,
        8 << 20,
        16,
    )
    received, slots, order, upper = lax.optimization_barrier((received, slots, order, upper))
    nearest = received[shared : shared + width]
    running = keep[:shared] + received[:shared]
    power = bound(keep[shared:], received[shared + width :])
    bases = []
    coefs = []
    for bit in range(1, member_levels):
        rest = running.shape[0] - width // 2
        received = partner(narrow(running, power), "member", bit)
        if bit == 1:
            bases.append(diagonal(0, 3, running))
            received, bases[0] = lax.optimization_barrier((received, bases[0]))
        if bit == member_levels - 1:
            bases.append(diagonal(3, 3, running))
            received, bases[1] = lax.optimization_barrier((received, bases[1]))
        received, other = widen(received)
        power = bound(power, other)
        coefs.insert(0, received[rest:].astype(BF16))
        running = running[:rest] + received[:rest]
    routes = [[], []]
    for low in range(groups):
        for near in range(0, members, 2):
            at = low * members + near
            routes[0] += [(at, (low ^ 2) * members + near), (at + 1, (low ^ 1) * members + near + 1)]
            routes[1] += [(at, (low ^ 3) * members + near), (at + 1, low * members + (near ^ 2) + 1)]
    sums = narrow(running, power)
    heard = [lax.ppermute(sums, everyone, route) for route in routes]
    left_top, left_low, last = call(
        functools.partial(stage_kernel, 6),
        [
            pltpu.VMEM(top_left.shape, BF16),
            pltpu.VMEM((capacity, member_levels * 2 * width), BF16),
            jax.ShapeDtypeStruct((2 * height, columns), F32),
        ],
        [HBM, HBM, HBM, VMEM, pl.BlockSpec(memory_space=pl.ANY)],
        (*far(top_left, low_left, diag_block), pair, running),
        8 * height * capacity * columns,
        12 << 20,
        24,
        scratch=[
            pltpu.VMEM(low_left.shape, BF16),
            pltpu.VMEM((2, 2, height, capacity), BF16),
            DMA((4,)),
        ],
    )
    bases.append(last)
    heard, left_top, left_low = lax.optimization_barrier((heard, left_top, left_low))
    heard = [widen(block)[0] for block in heard]
    own = (heard[0] + jnp.where(flags[:1] > 0, heard[1], 0.0)).astype(BF16)
    own_low = jnp.concatenate(coefs)
    their_low, own = lax.optimization_barrier((partner(own_low, "member", 0), own))
    theirs = partner(own, "member", 0)
    base = call(
        functools.partial(low_kernel, len(bases), group_levels),
        [jax.ShapeDtypeStruct((capacity, columns), F32)],
        [SMEM] + [VMEM] * (len(bases) + 4),
        (block_ranks, *bases, left_low, nearest, own_low, their_low),
        4 * capacity * columns * member_levels * width,
        3 << 20,
        16,
    )[0]

    leaving = call(
        functools.partial(out_kernel, bucket),
        [jax.ShapeDtypeStruct((capacity, columns), BF16)],
        [VMEM] * 6,
        (flags, base, left_top, own, theirs, slots),
        4 * capacity * columns * group_levels * top_width,
        4 << 20,
        24,
        scratch=[
            pltpu.VMEM((leaves * filled, 128), BF16),
            pltpu.VMEM((leaves, filled, 128), F32),
        ],
    )[0]
    returned = lax.all_to_all(
        leaving.reshape(leaves, bucket, columns), everyone, split_axis=0, concat_axis=0, tiled=True
    )
    return call(
        unpack_kernel,
        [jax.ShapeDtypeStruct((count, columns), F32)],
        [VMEM] * 3,
        (order, upper, returned.reshape(capacity, columns)),
        2 * capacity * count * columns,
        4 << 20,
        16,
        out_specs=[HBM],
        scratch=[pltpu.VMEM((count, 128), F32), DMA((count // 256,))],
    )[0]


def solution(mesh):
    return jax.shard_map(
        on_device,
        mesh=mesh,
        in_specs=(
            P(("group", "member"), None),
            P(("group", "member")),
            P(),
            P(),
            P(None, ("group", "member"), None),
            P(None, None, ("group", "member"), None),
            P(None, None, ("group", "member"), None),
            P(None, None, ("group", "member"), None),
            P(None, None, ("group", "member"), None),
        ),
        out_specs=P(("group", "member"), None),
        check_vma=False,
    )
```

```python
import functools

import jax
import jax.numpy as jnp
from jax import lax
from jax.experimental import pallas as pl
from jax.experimental.pallas import tpu as pltpu
from jax.sharding import PartitionSpec as P

F32 = jnp.float32
BF16 = jnp.bfloat16
F16 = jnp.float16
I32 = jnp.int32
VMEM = pl.BlockSpec(memory_space=pltpu.VMEM)
SMEM = pl.BlockSpec(memory_space=pltpu.SMEM)
HBM = pl.BlockSpec(memory_space=pltpu.HBM)
DMA = pltpu.SemaphoreType.DMA


def iota(shape, dim):
    return lax.broadcasted_iota(I32, shape, dim)


def hot(mask):
    return jnp.where(mask, 1.0, 0.0).astype(BF16)


def dot(a, b, over=(1, 0)):
    return lax.dot_general(
        a, b, (((over[0],), (over[1],)), ((), ())), preferred_element_type=F32
    )


def call(kernel, outs, ins, args, flops, moved, limit, scratch=(), **more):
    return pl.pallas_call(
        kernel,
        out_shape=outs,
        in_specs=ins,
        out_specs=more.pop("out_specs", [VMEM] * len(outs)),
        scratch_shapes=scratch,
        cost_estimate=pl.CostEstimate(flops=flops, bytes_accessed=moved, transcendentals=0),
        compiler_params=pltpu.CompilerParams(vmem_limit_bytes=limit << 20),
        **more,
    )(*args)


def partner(block, axis, apart):
    count = lax.axis_size(axis)
    route = []
    for low in range(count):
        high = low | 1 << apart
        if high != low and high < count:
            route += [(low, high), (high, low)]
    return lax.ppermute(block, axis, route)


def far(*arrays):
    return [pltpu.with_memory_space_constraint(array, pltpu.HBM) for array in arrays]


def bound(mine, other):
    return jnp.clip(jnp.maximum(mine, other) + 1.0, -100.0, 126.0)


def narrow(rows, power):
    return jnp.concatenate([rows * jnp.exp2(14.0 - power[:1]), power]).astype(F16)


def widen(sent):
    power = sent[-8:].astype(F32)
    return sent[:-8].astype(F32) * jnp.exp2(power[:1] - 14.0), power


def turn(block):
    half = block.shape[1] // 2
    return jnp.where(iota(block.shape, 1) < half, -1.0, 1.0) * pltpu.roll(block, half, 1)


def rank_of(ranks, level, levels):
    device = lax.axis_index("group") * lax.axis_size("member") + lax.axis_index("member")
    return ranks[(1 << level) - 2 + jnp.right_shift(device, levels - level)]


def pack_kernel(leaves, bucket, sizes_in, position_in, rows_in, packed, places, *scratch):
    sizes, position, rows, ordered, near, sems, out_sems = scratch
    copies = [
        pltpu.make_async_copy(source, target, sems.at[i])
        for i, (source, target) in enumerate(
            [(position_in, position), (rows_in, rows), (sizes_in, sizes)]
        )
    ]
    for copy in copies:
        copy.start()
    copies[0].wait()
    count = rows.shape[0]
    padded = packed.shape[1]
    shift = leaves.bit_length() - 1
    here = position[...]
    window = jnp.right_shift(here, shift)
    copies[1].wait()
    values = rows[...]
    block = 512
    for low in range(0, count, block):
        ordered[low : low + block, :] = dot(hot(iota((block, count), 0) + low == window), values)
    ordered[count:, :] = jnp.zeros((padded, 128), F32)
    copies[2].wait()
    zero = jnp.zeros((1, count), I32)
    owner, first = zero, zero
    starts = [0]
    for c in range(leaves):
        starts.append(starts[-1] + jnp.right_shift(sizes[c], shift))
        beyond = window >= starts[-1]
        owner = owner + beyond.astype(I32)
        first = jnp.where(beyond, starts[-1], first)
    offset = jnp.bitwise_and(here, leaves - 1).astype(F32)
    picked = jnp.where(iota((leaves, count), 0) == owner, offset, 0.0).astype(BF16)
    offsets = dot(picked, hot(iota((128, count), 0) == window - first), (1, 1))
    places[...] = owner * bucket + window - first
    line = iota((padded, 128), 0)
    chunk = leaves // 8
    out = []
    for c in range(leaves):
        data = ordered[pl.ds(starts[c], padded), :]
        data = jnp.where(line < starts[c + 1] - starts[c], data, 0.0)
        data = jnp.where(line == bucket, offsets[c : c + 1, :], data)
        near[c] = data.astype(BF16)
        if c % chunk == chunk - 1:
            part = pl.ds(c + 1 - chunk, chunk)
            out.append(pltpu.make_async_copy(near.at[part], packed.at[part], out_sems.at[c // chunk]))
            out[-1].start()
    for copy in out:
        copy.wait()


def near_kernel(ranks, right_top_in, right_low_in, right, flags, sems):
    tops, parts, capacity, width = right_top_in.shape
    levels, _, rows, _ = right_low_in.shape
    pairs = []
    for level in range(tops):
        for p in range(parts):
            place = (pl.ds(p * capacity, capacity), pl.ds(level * width, width))
            pairs.append((right_top_in.at[level, p], right.at[place]))
    at = parts * capacity
    for low in range(0, capacity, 256):
        for p in range(parts):
            for level in range(levels):
                source = right_low_in.at[level, p, :, pl.ds(low, 256)]
                pairs.append((source, right.at[pl.ds(at, rows), :]))
                at += rows
    copies = [pltpu.make_async_copy(a, b, sems.at[i]) for i, (a, b) in enumerate(pairs)]
    for copy in copies:
        copy.start()
    row, lane = iota(flags.shape, 0), iota(flags.shape, 1)
    marks = jnp.where(row == 0, 1 - jnp.bitwise_and(lax.axis_index("member"), 1), 0)
    for level in range(1, tops + 1):
        counts = (lane < rank_of(ranks, level, tops + levels)).astype(I32)
        marks = jnp.where(row == level, counts, marks)
    flags[...] = marks.astype(F32)
    for copy in copies:
        copy.wait()


def way_kernel(targets, places, after, slots, order, upper):
    groups, part = targets.shape
    lanes = iota((part, 128), 1)
    for g in range(groups):
        target = jnp.transpose(jnp.broadcast_to(targets[g : g + 1, :], (128, part)))
        for low in range(0, part, 128):
            slots[g * part : (g + 1) * part, low : low + 128] = hot(target == lanes + low)
    count, folded = order.shape
    place = jnp.transpose(jnp.broadcast_to(places[...], (128, count)))
    beyond = place >= folded
    upper[...] = beyond.astype(I32)
    place = jnp.where(beyond, place - folded, place)
    block = 256
    lanes = iota((block, 128), 1)
    for low in range(0, count, block):
        for at in range(0, folded, 128):
            order[low : low + block, at : at + 128] = hot(place[low : low + block] == lanes + at)


def stage_kernel(first, left_top_in, left_low_in, block_in, pair, after, *rest):
    left_top, left_low, out, raw, block, sems = rest
    copies = [pltpu.make_async_copy(left_low_in, raw, sems.at[0])]
    count, _, height, _ = block.shape
    for j in range(count):
        rows = pl.ds((first + j) * height, height)
        copies.append(pltpu.make_async_copy(block_in.at[:, rows, :], block.at[j], sems.at[1 + j]))
    copies.append(pltpu.make_async_copy(left_top_in, left_top, sems.at[1 + count]))
    for copy in copies:
        copy.start()
    copies[0].wait()
    levels, parts, width, capacity = raw.shape
    left_low[...] = jnp.transpose(raw[...].reshape(levels * parts * width, capacity))
    for j in range(count):
        copies[1 + j].wait()
        out[j * height : (j + 1) * height, :] = dot(block[j, 0], pair[0]) + dot(block[j, 1], pair[1])
    copies[-1].wait()


def field_kernel(leaves, bucket, tops, levels, arrived, right, *rest):
    pair, targets, send, keep, whole = rest
    capacity = leaves * bucket
    padded = arrived.shape[1]
    part = leaves * 8
    groups = targets.shape[0]
    core = jnp.bitwise_and(lax.axis_index("member"), 1)
    last = arrived[:, padded - 16 :, :].reshape(leaves * 16, 128)
    row = iota((leaves * 16, part), 0)
    spread = jnp.right_shift(iota((leaves * 16, part), 1), 3) * 16 + bucket % 16 == row
    spread_offsets = dot(last, hot(spread), (0, 0))[: groups * 8].reshape(groups, 8, part)
    lane_window = jnp.bitwise_and(iota((8, part), 1), 7)
    own = (lane_window == iota((8, part), 0))[None]
    target = jnp.sum(jnp.where(own, spread_offsets, 0.0), axis=1).astype(I32)
    target = target + lane_window[:1, :] * leaves
    targets[...] = target
    for g in range(groups):
        size = min(part, capacity - g * part)
        if g % 2 == 0:
            both = arrived[:, g * 8 : g * 8 + 16, :].astype(F32)
        chunk = both[:, g % 2 * 8 : g % 2 * 8 + 8, :].reshape(part, 128).astype(BF16)
        placed = dot(hot(iota((part, part), 0) == target[g : g + 1, :]), chunk)
        pair[0, g * part : g * part + size, :] = placed[:size].astype(BF16)
        pair[1, g * part : g * part + size, :] = turn(placed)[:size].astype(BF16)
    plain = jnp.transpose(pair[0])
    turned = jnp.concatenate([-plain[64:], plain[:64]], axis=0)
    upper = dot(plain, right[:capacity, :]) + dot(turned, right[capacity : 2 * capacity, :])
    top_rows = tops * 128
    for level in range(tops):
        whole[level * 128 : (level + 1) * 128, :] = upper[:, level * 128 : (level + 1) * 128]
    rows = whole.shape[0] - top_rows
    width = rows // levels
    lower = jnp.zeros((rows, 128), F32)
    at = 2 * capacity
    for low in range(0, capacity, 256):
        for p in range(2):
            lower += dot(right[at : at + rows, :], pair[p, low : low + 256, :])
            at += rows
    whole[top_rows:, :] = lower
    at = 0
    low = 0
    for half in [tops * 64] + [width // 2] * (levels - 1):
        mine = pl.multiple_of(low + core * half, 8)
        other = pl.multiple_of(low + (1 - core) * half, 8)
        keep[at : at + half, :] = whole[pl.ds(mine, half), :]
        send[at : at + half, :] = whole[pl.ds(other, half), :]
        at += half
        low += 2 * half
    send[at : at + width, :] = lower[(levels - 1) * width :]
    largest = jnp.max(jnp.abs(whole[...]), axis=0, keepdims=True)
    power = jnp.clip(jnp.ceil(jnp.log2(largest + 1e-30)) + 1.0, -100.0, 126.0)
    send[at + width :, :] = jnp.broadcast_to(power, (8, 128))
    keep[at:, :] = jnp.broadcast_to(power, (8, 128))


def diag_kernel(first, block_in, pair, after, out, block, sems):
    count, _, height, _ = block.shape
    copies = []
    for j in range(count):
        rows = pl.ds((first + j) * height, height)
        copies.append(pltpu.make_async_copy(block_in.at[:, rows, :], block.at[j], sems.at[j]))
        copies[j].start()
    for j in range(count):
        copies[j].wait()
        out[j * height : (j + 1) * height, :] = dot(block[j, 0], pair[0]) + dot(block[j, 1], pair[1])


def merged(core, own, theirs, at, half):
    a, b = own[at : at + half, :].astype(F32), theirs[at : at + half, :].astype(F32)
    return jnp.concatenate([jnp.where(core == 0, a, b), jnp.where(core == 0, b, a)], axis=0)


def low_kernel(pieces, tops, ranks, *rest):
    bases = rest[:pieces]
    left_low, nearest, own, theirs, out = rest[pieces:]
    width = nearest.shape[0]
    levels = left_low.shape[1] // (2 * width)
    core = jnp.bitwise_and(lax.axis_index("member"), 1)
    half = width // 2
    stacked = []
    for level in range(levels):
        if level < levels - 1:
            coef = merged(core, own, theirs, level * half, half)
        else:
            coef = nearest[...]
        rank = rank_of(ranks, 1 + tops + level, tops + levels)
        coef = jnp.where(iota(coef.shape, 0) < rank, coef, 0.0)
        stacked += [coef, turn(coef)]
    stacked = jnp.concatenate(stacked, axis=0).astype(BF16)
    low = 0
    for base in bases:
        rows = slice(low, low + base.shape[0])
        out[rows, :] = base[...] + dot(left_low[rows, :], stacked)
        low += base.shape[0]


def out_kernel(bucket, flags, base, left_top, own, theirs, slots, packed, spare, ordered):
    capacity = base.shape[0]
    part = slots.shape[1]
    groups = slots.shape[0] // part
    leaves = part // 8
    first = flags[:1, :] > 0
    levels = left_top.shape[0]
    half = own.shape[0]
    stacked = []
    for level in range(levels):
        pick = (own, theirs) if level == 0 else (theirs, own)
        coef = jnp.where(first, pick[0][...].astype(F32), pick[1][...].astype(F32))
        coef = jnp.where(flags[1 + level : 2 + level, :] > 0, coef, 0.0)
        turned = jnp.concatenate([-coef[half // 2 :], coef[: half // 2]], axis=0)
        stacked += [jnp.transpose(coef), jnp.transpose(turned)]
    stacked = jnp.concatenate(stacked, axis=0).astype(BF16)
    if groups * part > capacity:
        spare[capacity:, :] = jnp.zeros((groups * part - capacity, 128), BF16)
    factors = [left_top[level, p] for level in range(levels) for p in range(2)]
    total = base[...] + dot(jnp.concatenate(factors, axis=1), stacked)
    spare[:capacity, :] = total.astype(BF16)
    for g in range(groups):
        moved = dot(slots[g * part : (g + 1) * part, :], spare[g * part : (g + 1) * part, :])
        ordered[:, g * 8 : g * 8 + 8, :] = moved.reshape(leaves, 8, 128)
    packed[...] = ordered[:, :bucket, :].reshape(capacity, 128).astype(BF16)


def unpack_kernel(order, upper, returned, out, near, sems):
    count, folded = order.shape
    wide = jnp.concatenate([returned[:folded, :], returned[folded:, :]], axis=1)
    block = 256
    copies = []
    for low in range(0, count, block):
        rows = pl.ds(low, block)
        both = dot(order[low : low + block, :], wide)
        near[rows, :] = jnp.where(upper[low : low + block, :] != 0, both[:, 128:], both[:, :128])
        copies.append(pltpu.make_async_copy(near.at[rows, :], out.at[rows, :], sems.at[low // block]))
        copies[-1].start()
    for copy in copies:
        copy.wait()


def on_device(
    mesh_vector,
    cluster_position,
    cluster_sizes,
    block_ranks,
    diag_block,
    top_left,
    top_right,
    low_left,
    low_right,
):
    groups = lax.axis_size("group")
    members = lax.axis_size("member")
    leaves = groups * members
    group_levels = groups.bit_length() - 1
    member_levels = members.bit_length() - 1
    capacity = diag_block.shape[1]
    bucket = capacity // leaves
    padded = (bucket + 16) // 16 * 16
    filled = (bucket + 7) // 8 * 8
    count, columns = mesh_vector.shape
    everyone = ("group", "member")
    low_left = jnp.swapaxes(low_left, 2, 3)
    low_right = jnp.swapaxes(low_right, 2, 3)
    width = low_left.shape[2]
    top_width = top_left.shape[3]
    far_flops = 4 * capacity * columns * (group_levels * top_width + member_levels * width)

    packed, places = call(
        functools.partial(pack_kernel, leaves, bucket),
        [
            jax.ShapeDtypeStruct((leaves, padded, columns), BF16),
            jax.ShapeDtypeStruct((1, count), I32),
        ],
        [HBM] * 3,
        far(cluster_sizes, cluster_position.reshape(1, count), mesh_vector),
        2 * count * count * columns,
        4 << 20,
        16,
        out_specs=[HBM, VMEM],
        scratch=[
            pltpu.SMEM((leaves,), I32),
            pltpu.VMEM((1, count), I32),
            pltpu.VMEM((count, columns), BF16),
            pltpu.VMEM((count + padded, columns), F32),
            pltpu.VMEM((leaves, padded, columns), BF16),
            DMA((3,)),
            DMA((8,)),
        ],
    )
    arrived = lax.all_to_all(packed, everyone, split_axis=0, concat_axis=0, tiled=True)
    ranked = group_levels * top_width + member_levels * width
    right, flags = call(
        near_kernel,
        [
            pltpu.VMEM((2 * ranked * capacity // 256, 256), BF16),
            jax.ShapeDtypeStruct((8, columns), F32),
        ],
        [SMEM, HBM, HBM],
        (block_ranks, *far(top_right, low_right)),
        0,
        6 << 20,
        16,
        scratch=[DMA((2 * group_levels + 2 * member_levels * capacity // 256,))],
    )
    tops = group_levels * columns // 2
    shared = tops + (member_levels - 1) * width // 2
    pair, targets, send, keep = call(
        functools.partial(field_kernel, leaves, bucket, group_levels, member_levels),
        [
            jax.ShapeDtypeStruct((2, capacity, columns), BF16),
            jax.ShapeDtypeStruct((filled // 8, leaves * 8), I32),
            jax.ShapeDtypeStruct((shared + width + 8, columns), F32),
            jax.ShapeDtypeStruct((shared + 8, columns), F32),
        ],
        [VMEM, VMEM],
        (arrived, right),
        far_flops,
        6 << 20,
        24,
        scratch=[pltpu.VMEM((2 * shared + width, columns), F32)],
    )
    height = capacity // 8

    def diagonal(first, chunks, after):
        return call(
            functools.partial(diag_kernel, first),
            [jax.ShapeDtypeStruct((chunks * height, columns), F32)],
            [HBM, VMEM, pl.BlockSpec(memory_space=pl.ANY)],
            (*far(diag_block), pair, after),
            4 * chunks * height * capacity * columns,
            4 * chunks * height * capacity,
            24,
            scratch=[pltpu.VMEM((chunks, 2, height, capacity), BF16), DMA((chunks,))],
        )[0]

    received = partner(send, "member", 0)
    slots, order, upper = call(
        way_kernel,
        [
            jax.ShapeDtypeStruct((leaves * filled, leaves * 8), BF16),
            jax.ShapeDtypeStruct((count, capacity // 2), BF16),
            jax.ShapeDtypeStruct((count, 128), I32),
        ],
        [VMEM, VMEM, pl.BlockSpec(memory_space=pl.ANY)],
        (targets, places, send),
        0,
        8 << 20,
        16,
    )
    received, slots, order, upper = lax.optimization_barrier((received, slots, order, upper))
    nearest = received[shared : shared + width]
    running = keep[:shared] + received[:shared]
    power = bound(keep[shared:], received[shared + width :])
    bases = []
    coefs = []
    for bit in range(1, member_levels):
        rest = running.shape[0] - width // 2
        received = partner(narrow(running, power), "member", bit)
        if bit == 1:
            bases.append(diagonal(0, 3, running))
            received, bases[0] = lax.optimization_barrier((received, bases[0]))
        if bit == member_levels - 1:
            bases.append(diagonal(3, 4, running))
            received, bases[1] = lax.optimization_barrier((received, bases[1]))
        received, other = widen(received)
        power = bound(power, other)
        coefs.insert(0, received[rest:].astype(BF16))
        running = running[:rest] + received[:rest]
    routes = [[], []]
    for low in range(groups):
        for near in range(0, members, 2):
            at = low * members + near
            routes[0] += [(at, (low ^ 2) * members + near), (at + 1, (low ^ 1) * members + near + 1)]
            routes[1] += [(at, (low ^ 3) * members + near), (at + 1, low * members + (near ^ 2) + 1)]
    sums = narrow(running, power)
    heard = [lax.ppermute(sums, everyone, route) for route in routes]
    left_top, left_low, last = call(
        functools.partial(stage_kernel, 7),
        [
            pltpu.VMEM(top_left.shape, BF16),
            pltpu.VMEM((capacity, member_levels * 2 * width), BF16),
            jax.ShapeDtypeStruct((height, columns), F32),
        ],
        [HBM, HBM, HBM, VMEM, pl.BlockSpec(memory_space=pl.ANY)],
        (*far(top_left, low_left, diag_block), pair, running),
        4 * height * capacity * columns,
        10 << 20,
        24,
        scratch=[
            pltpu.VMEM(low_left.shape, BF16),
            pltpu.VMEM((1, 2, height, capacity), BF16),
            DMA((3,)),
        ],
    )
    bases.append(last)
    heard, left_top, left_low = lax.optimization_barrier((heard, left_top, left_low))
    heard = [widen(block)[0] for block in heard]
    own = (heard[0] + jnp.where(flags[:1] > 0, heard[1], 0.0)).astype(BF16)
    own_low = jnp.concatenate(coefs)
    their_low, own = lax.optimization_barrier((partner(own_low, "member", 0), own))
    theirs = partner(own, "member", 0)
    base = call(
        functools.partial(low_kernel, len(bases), group_levels),
        [jax.ShapeDtypeStruct((capacity, columns), F32)],
        [SMEM] + [VMEM] * (len(bases) + 4),
        (block_ranks, *bases, left_low, nearest, own_low, their_low),
        4 * capacity * columns * member_levels * width,
        3 << 20,
        16,
    )[0]

    leaving = call(
        functools.partial(out_kernel, bucket),
        [jax.ShapeDtypeStruct((capacity, columns), BF16)],
        [VMEM] * 6,
        (flags, base, left_top, own, theirs, slots),
        4 * capacity * columns * group_levels * top_width,
        4 << 20,
        24,
        scratch=[
            pltpu.VMEM((leaves * filled, 128), BF16),
            pltpu.VMEM((leaves, filled, 128), F32),
        ],
    )[0]
    returned = lax.all_to_all(
        leaving.reshape(leaves, bucket, columns), everyone, split_axis=0, concat_axis=0, tiled=True
    )
    return call(
        unpack_kernel,
        [jax.ShapeDtypeStruct((count, columns), F32)],
        [VMEM] * 3,
        (order, upper, returned.reshape(capacity, columns)),
        2 * capacity * count * columns,
        4 << 20,
        16,
        out_specs=[HBM],
        scratch=[pltpu.VMEM((count, 128), F32), DMA((count // 256,))],
    )[0]


def solution(mesh):
    return jax.shard_map(
        on_device,
        mesh=mesh,
        in_specs=(
            P(("group", "member"), None),
            P(("group", "member")),
            P(),
            P(),
            P(None, ("group", "member"), None),
            P(None, None, ("group", "member"), None),
            P(None, None, ("group", "member"), None),
            P(None, None, ("group", "member"), None),
            P(None, None, ("group", "member"), None),
        ),
        out_specs=P(("group", "member"), None),
        check_vma=False,
    )
```

```python
import functools

import jax
import jax.numpy as jnp
from jax import lax
from jax.experimental import pallas as pl
from jax.experimental.pallas import tpu as pltpu
from jax.sharding import PartitionSpec as P

F32 = jnp.float32
BF16 = jnp.bfloat16
F16 = jnp.float16
I32 = jnp.int32
VMEM = pl.BlockSpec(memory_space=pltpu.VMEM)
SMEM = pl.BlockSpec(memory_space=pltpu.SMEM)
HBM = pl.BlockSpec(memory_space=pltpu.HBM)
DMA = pltpu.SemaphoreType.DMA


def iota(shape, dim):
    return lax.broadcasted_iota(I32, shape, dim)


def hot(mask):
    return jnp.where(mask, 1.0, 0.0).astype(BF16)


def dot(a, b, over=(1, 0)):
    return lax.dot_general(
        a, b, (((over[0],), (over[1],)), ((), ())), preferred_element_type=F32
    )


def call(kernel, outs, ins, args, flops, moved, limit, scratch=(), **more):
    return pl.pallas_call(
        kernel,
        out_shape=outs,
        in_specs=ins,
        out_specs=more.pop("out_specs", [VMEM] * len(outs)),
        scratch_shapes=scratch,
        cost_estimate=pl.CostEstimate(flops=flops, bytes_accessed=moved, transcendentals=0),
        compiler_params=pltpu.CompilerParams(vmem_limit_bytes=limit << 20),
        **more,
    )(*args)


def partner(block, axis, apart):
    count = lax.axis_size(axis)
    route = []
    for low in range(count):
        high = low | 1 << apart
        if high != low and high < count:
            route += [(low, high), (high, low)]
    return lax.ppermute(block, axis, route)


def far(*arrays):
    return [pltpu.with_memory_space_constraint(array, pltpu.HBM) for array in arrays]


def bound(mine, other):
    return jnp.clip(jnp.maximum(mine, other) + 1.0, -100.0, 126.0)


def narrow(rows, power):
    return jnp.concatenate([rows * jnp.exp2(14.0 - power[:1]), power]).astype(F16)


def widen(sent):
    power = sent[-8:].astype(F32)
    return sent[:-8].astype(F32) * jnp.exp2(power[:1] - 14.0), power


def turn(block):
    half = block.shape[1] // 2
    return jnp.where(iota(block.shape, 1) < half, -1.0, 1.0) * pltpu.roll(block, half, 1)


def rank_of(ranks, level, levels):
    device = lax.axis_index("group") * lax.axis_size("member") + lax.axis_index("member")
    return ranks[(1 << level) - 2 + jnp.right_shift(device, levels - level)]


def pack_kernel(leaves, groups, bucket, sizes_in, position_in, rows_in, packed, places, *scratch):
    sizes, position, rows, ordered, near, sems, out_sems = scratch
    copies = [
        pltpu.make_async_copy(source, target, sems.at[i])
        for i, (source, target) in enumerate(
            [(position_in, position), (rows_in, rows), (sizes_in, sizes)]
        )
    ]
    for copy in copies:
        copy.start()
    copies[0].wait()
    count = rows.shape[0]
    padded = packed.shape[1]
    shift = leaves.bit_length() - 1
    here = position[...]
    window = jnp.right_shift(here, shift)
    copies[1].wait()
    values = rows[...]
    block = 512
    for low in range(0, count, block):
        ordered[low : low + block, :] = dot(hot(iota((block, count), 0) + low == window), values)
    ordered[count:, :] = jnp.zeros((padded, 128), F32)
    copies[2].wait()
    zero = jnp.zeros((1, count), I32)
    owner, first = zero, zero
    starts = [0]
    for c in range(leaves):
        starts.append(starts[-1] + jnp.right_shift(sizes[c], shift))
        beyond = window >= starts[-1]
        owner = owner + beyond.astype(I32)
        first = jnp.where(beyond, starts[-1], first)
    offset = jnp.bitwise_and(here, leaves - 1).astype(F32)
    picked = jnp.where(iota((leaves, count), 0) == owner, offset, 0.0).astype(BF16)
    offsets = dot(picked, hot(iota((128, count), 0) == window - first), (1, 1))
    members = leaves // groups
    places[...] = (owner % members * groups + owner // members) * bucket + window - first
    line = iota((padded, 128), 0)
    chunk = leaves // 8
    out = []
    for at in range(leaves):
        c = at % groups * members + at // groups
        data = ordered[pl.ds(starts[c], padded), :]
        data = jnp.where(line < starts[c + 1] - starts[c], data, 0.0)
        data = jnp.where(line == bucket, offsets[c : c + 1, :], data)
        near[at] = data.astype(BF16)
        if at % chunk == chunk - 1:
            part = pl.ds(at + 1 - chunk, chunk)
            out.append(pltpu.make_async_copy(near.at[part], packed.at[part], out_sems.at[at // chunk]))
            out[-1].start()
    for copy in out:
        copy.wait()


def near_kernel(ranks, right_top_in, right_low_in, right, flags, sems):
    tops, parts, capacity, width = right_top_in.shape
    levels, _, rows, _ = right_low_in.shape
    pairs = []
    for level in range(tops):
        for p in range(parts):
            place = (pl.ds(p * capacity, capacity), pl.ds(level * width, width))
            pairs.append((right_top_in.at[level, p], right.at[place]))
    at = parts * capacity
    for low in range(0, capacity, 256):
        for p in range(parts):
            for level in range(levels):
                source = right_low_in.at[level, p, :, pl.ds(low, 256)]
                pairs.append((source, right.at[pl.ds(at, rows), :]))
                at += rows
    copies = [pltpu.make_async_copy(a, b, sems.at[i]) for i, (a, b) in enumerate(pairs)]
    for copy in copies:
        copy.start()
    row, lane = iota(flags.shape, 0), iota(flags.shape, 1)
    marks = jnp.where(row == 0, 1 - jnp.bitwise_and(lax.axis_index("member"), 1), 0)
    for level in range(1, tops + 1):
        counts = (lane < rank_of(ranks, level, tops + levels)).astype(I32)
        marks = jnp.where(row == level, counts, marks)
    flags[...] = marks.astype(F32)
    for copy in copies:
        copy.wait()


def way_kernel(targets, places, after, slots, order, upper):
    groups, part = targets.shape
    lanes = iota((part, 128), 1)
    for g in range(groups):
        target = jnp.transpose(jnp.broadcast_to(targets[g : g + 1, :], (128, part)))
        for low in range(0, part, 128):
            slots[g * part : (g + 1) * part, low : low + 128] = hot(target == lanes + low)
    count, folded = order.shape
    place = jnp.transpose(jnp.broadcast_to(places[...], (128, count)))
    beyond = place >= folded
    upper[...] = beyond.astype(I32)
    place = jnp.where(beyond, place - folded, place)
    block = 256
    lanes = iota((block, 128), 1)
    for low in range(0, count, block):
        for at in range(0, folded, 128):
            order[low : low + block, at : at + 128] = hot(place[low : low + block] == lanes + at)


def stage_kernel(first, left_top_in, left_low_in, block_in, pair, after, *rest):
    left_top, left_low, out, raw, block, sems = rest
    copies = [pltpu.make_async_copy(left_low_in, raw, sems.at[0])]
    count, _, height, _ = block.shape
    for j in range(count):
        rows = pl.ds((first + j) * height, height)
        copies.append(pltpu.make_async_copy(block_in.at[:, rows, :], block.at[j], sems.at[1 + j]))
    copies.append(pltpu.make_async_copy(left_top_in, left_top, sems.at[1 + count]))
    for copy in copies:
        copy.start()
    copies[0].wait()
    levels, parts, width, capacity = raw.shape
    left_low[...] = jnp.transpose(raw[...].reshape(levels * parts * width, capacity))
    for j in range(count):
        copies[1 + j].wait()
        out[j * height : (j + 1) * height, :] = dot(block[j, 0], pair[0]) + dot(block[j, 1], pair[1])
    copies[-1].wait()


def field_kernel(leaves, bucket, tops, levels, arrived, right, *rest):
    pair, targets, send, keep, whole = rest
    capacity = leaves * bucket
    padded = arrived.shape[1]
    part = leaves * 8
    groups = targets.shape[0]
    core = jnp.bitwise_and(lax.axis_index("member"), 1)
    last = arrived[:, padded - 16 :, :].reshape(leaves * 16, 128)
    row = iota((leaves * 16, part), 0)
    spread = jnp.right_shift(iota((leaves * 16, part), 1), 3) * 16 + bucket % 16 == row
    spread_offsets = dot(last, hot(spread), (0, 0))[: groups * 8].reshape(groups, 8, part)
    lane_window = jnp.bitwise_and(iota((8, part), 1), 7)
    own = (lane_window == iota((8, part), 0))[None]
    target = jnp.sum(jnp.where(own, spread_offsets, 0.0), axis=1).astype(I32)
    target = target + lane_window[:1, :] * leaves
    targets[...] = target
    for g in range(groups):
        size = min(part, capacity - g * part)
        if g % 2 == 0:
            both = arrived[:, g * 8 : g * 8 + 16, :].astype(F32)
        chunk = both[:, g % 2 * 8 : g % 2 * 8 + 8, :].reshape(part, 128).astype(BF16)
        placed = dot(hot(iota((part, part), 0) == target[g : g + 1, :]), chunk)
        pair[0, g * part : g * part + size, :] = placed[:size].astype(BF16)
        pair[1, g * part : g * part + size, :] = turn(placed)[:size].astype(BF16)
    plain = jnp.transpose(pair[0])
    turned = jnp.concatenate([-plain[64:], plain[:64]], axis=0)
    upper = dot(plain, right[:capacity, :]) + dot(turned, right[capacity : 2 * capacity, :])
    top_rows = tops * 128
    for level in range(tops):
        whole[level * 128 : (level + 1) * 128, :] = upper[:, level * 128 : (level + 1) * 128]
    rows = whole.shape[0] - top_rows
    width = rows // levels
    lower = jnp.zeros((rows, 128), F32)
    at = 2 * capacity
    for low in range(0, capacity, 256):
        for p in range(2):
            lower += dot(right[at : at + rows, :], pair[p, low : low + 256, :])
            at += rows
    whole[top_rows:, :] = lower
    at = 0
    low = 0
    for half in [tops * 64] + [width // 2] * (levels - 1):
        mine = pl.multiple_of(low + core * half, 8)
        other = pl.multiple_of(low + (1 - core) * half, 8)
        keep[at : at + half, :] = whole[pl.ds(mine, half), :]
        send[at : at + half, :] = whole[pl.ds(other, half), :]
        at += half
        low += 2 * half
    send[at : at + width, :] = lower[(levels - 1) * width :]
    largest = jnp.max(jnp.abs(whole[...]), axis=0, keepdims=True)
    power = jnp.clip(jnp.ceil(jnp.log2(largest + 1e-30)) + 1.0, -100.0, 126.0)
    send[at + width :, :] = jnp.broadcast_to(power, (8, 128))
    keep[at:, :] = jnp.broadcast_to(power, (8, 128))


def diag_kernel(first, block_in, pair, after, out, block, sems):
    count, _, height, _ = block.shape
    copies = []
    for j in range(count):
        rows = pl.ds((first + j) * height, height)
        copies.append(pltpu.make_async_copy(block_in.at[:, rows, :], block.at[j], sems.at[j]))
        copies[j].start()
    for j in range(count):
        copies[j].wait()
        out[j * height : (j + 1) * height, :] = dot(block[j, 0], pair[0]) + dot(block[j, 1], pair[1])


def merged(core, own, theirs, at, half):
    a, b = own[at : at + half, :].astype(F32), theirs[at : at + half, :].astype(F32)
    return jnp.concatenate([jnp.where(core == 0, a, b), jnp.where(core == 0, b, a)], axis=0)


def low_kernel(pieces, tops, ranks, *rest):
    bases = rest[:pieces]
    left_low, nearest, own, theirs, out = rest[pieces:]
    width = nearest.shape[0]
    levels = left_low.shape[1] // (2 * width)
    core = jnp.bitwise_and(lax.axis_index("member"), 1)
    half = width // 2
    stacked = []
    for level in range(levels):
        if level < levels - 1:
            coef = merged(core, own, theirs, level * half, half)
        else:
            coef = nearest[...]
        rank = rank_of(ranks, 1 + tops + level, tops + levels)
        coef = jnp.where(iota(coef.shape, 0) < rank, coef, 0.0)
        stacked += [coef, turn(coef)]
    stacked = jnp.concatenate(stacked, axis=0).astype(BF16)
    low = 0
    for base in bases:
        rows = slice(low, low + base.shape[0])
        out[rows, :] = base[...] + dot(left_low[rows, :], stacked)
        low += base.shape[0]


def out_kernel(bucket, flags, base, left_top, own, theirs, slots, packed, spare, ordered):
    capacity = base.shape[0]
    part = slots.shape[1]
    groups = slots.shape[0] // part
    leaves = part // 8
    first = flags[:1, :] > 0
    levels = left_top.shape[0]
    half = own.shape[0]
    stacked = []
    for level in range(levels):
        pick = (own, theirs) if level == 0 else (theirs, own)
        coef = jnp.where(first, pick[0][...].astype(F32), pick[1][...].astype(F32))
        coef = jnp.where(flags[1 + level : 2 + level, :] > 0, coef, 0.0)
        turned = jnp.concatenate([-coef[half // 2 :], coef[: half // 2]], axis=0)
        stacked += [jnp.transpose(coef), jnp.transpose(turned)]
    stacked = jnp.concatenate(stacked, axis=0).astype(BF16)
    if groups * part > capacity:
        spare[capacity:, :] = jnp.zeros((groups * part - capacity, 128), BF16)
    factors = [left_top[level, p] for level in range(levels) for p in range(2)]
    total = base[...] + dot(jnp.concatenate(factors, axis=1), stacked)
    spare[:capacity, :] = total.astype(BF16)
    for g in range(groups):
        moved = dot(slots[g * part : (g + 1) * part, :], spare[g * part : (g + 1) * part, :])
        ordered[:, g * 8 : g * 8 + 8, :] = moved.reshape(leaves, 8, 128)
    packed[...] = ordered[:, :bucket, :].reshape(capacity, 128).astype(BF16)


def unpack_kernel(order, upper, returned, out, near, sems):
    count, folded = order.shape
    wide = jnp.concatenate([returned[:folded, :], returned[folded:, :]], axis=1)
    block = 256
    copies = []
    for low in range(0, count, block):
        rows = pl.ds(low, block)
        both = dot(order[low : low + block, :], wide)
        near[rows, :] = jnp.where(upper[low : low + block, :] != 0, both[:, 128:], both[:, :128])
        copies.append(pltpu.make_async_copy(near.at[rows, :], out.at[rows, :], sems.at[low // block]))
        copies[-1].start()
    for copy in copies:
        copy.wait()


def on_device(
    mesh_vector,
    cluster_position,
    cluster_sizes,
    block_ranks,
    diag_block,
    top_left,
    top_right,
    low_left,
    low_right,
):
    groups = lax.axis_size("group")
    members = lax.axis_size("member")
    leaves = groups * members
    group_levels = groups.bit_length() - 1
    member_levels = members.bit_length() - 1
    capacity = diag_block.shape[1]
    bucket = capacity // leaves
    padded = (bucket + 16) // 16 * 16
    filled = (bucket + 7) // 8 * 8
    count, columns = mesh_vector.shape
    everyone = ("group", "member")
    low_left = jnp.swapaxes(low_left, 2, 3)
    low_right = jnp.swapaxes(low_right, 2, 3)
    width = low_left.shape[2]
    top_width = top_left.shape[3]
    far_flops = 4 * capacity * columns * (group_levels * top_width + member_levels * width)

    packed, places = call(
        functools.partial(pack_kernel, leaves, groups, bucket),
        [
            jax.ShapeDtypeStruct((leaves, padded, columns), BF16),
            jax.ShapeDtypeStruct((1, count), I32),
        ],
        [HBM] * 3,
        far(cluster_sizes, cluster_position.reshape(1, count), mesh_vector),
        2 * count * count * columns,
        4 << 20,
        16,
        out_specs=[HBM, VMEM],
        scratch=[
            pltpu.SMEM((leaves,), I32),
            pltpu.VMEM((1, count), I32),
            pltpu.VMEM((count, columns), BF16),
            pltpu.VMEM((count + padded, columns), F32),
            pltpu.VMEM((leaves, padded, columns), BF16),
            DMA((3,)),
            DMA((8,)),
        ],
    )
    arrived = lax.all_to_all(packed, ("member", "group"), split_axis=0, concat_axis=0, tiled=True)
    ranked = group_levels * top_width + member_levels * width
    right, flags = call(
        near_kernel,
        [
            pltpu.VMEM((2 * ranked * capacity // 256, 256), BF16),
            jax.ShapeDtypeStruct((8, columns), F32),
        ],
        [SMEM, HBM, HBM],
        (block_ranks, *far(top_right, low_right)),
        0,
        6 << 20,
        16,
        scratch=[DMA((2 * group_levels + 2 * member_levels * capacity // 256,))],
    )
    tops = group_levels * columns // 2
    shared = tops + (member_levels - 1) * width // 2
    pair, targets, send, keep = call(
        functools.partial(field_kernel, leaves, bucket, group_levels, member_levels),
        [
            jax.ShapeDtypeStruct((2, capacity, columns), BF16),
            jax.ShapeDtypeStruct((filled // 8, leaves * 8), I32),
            jax.ShapeDtypeStruct((shared + width + 8, columns), F32),
            jax.ShapeDtypeStruct((shared + 8, columns), F32),
        ],
        [VMEM, VMEM],
        (arrived, right),
        far_flops,
        6 << 20,
        24,
        scratch=[pltpu.VMEM((2 * shared + width, columns), F32)],
    )
    height = capacity // 8

    def diagonal(first, chunks, after):
        return call(
            functools.partial(diag_kernel, first),
            [jax.ShapeDtypeStruct((chunks * height, columns), F32)],
            [HBM, VMEM, pl.BlockSpec(memory_space=pl.ANY)],
            (*far(diag_block), pair, after),
            4 * chunks * height * capacity * columns,
            4 * chunks * height * capacity,
            24,
            scratch=[pltpu.VMEM((chunks, 2, height, capacity), BF16), DMA((chunks,))],
        )[0]

    received = partner(send, "member", 0)
    slots, order, upper = call(
        way_kernel,
        [
            jax.ShapeDtypeStruct((leaves * filled, leaves * 8), BF16),
            jax.ShapeDtypeStruct((count, capacity // 2), BF16),
            jax.ShapeDtypeStruct((count, 128), I32),
        ],
        [VMEM, VMEM, pl.BlockSpec(memory_space=pl.ANY)],
        (targets, places, send),
        0,
        8 << 20,
        16,
    )
    received, slots, order, upper = lax.optimization_barrier((received, slots, order, upper))
    nearest = received[shared : shared + width]
    running = keep[:shared] + received[:shared]
    power = bound(keep[shared:], received[shared + width :])
    bases = []
    coefs = []
    for bit in range(1, member_levels):
        rest = running.shape[0] - width // 2
        received = partner(narrow(running, power), "member", bit)
        if bit == 1:
            bases.append(diagonal(0, 3, running))
            received, bases[0] = lax.optimization_barrier((received, bases[0]))
        if bit == member_levels - 1:
            bases.append(diagonal(3, 3, running))
            received, bases[1] = lax.optimization_barrier((received, bases[1]))
        received, other = widen(received)
        power = bound(power, other)
        coefs.insert(0, received[rest:].astype(BF16))
        running = running[:rest] + received[:rest]
    routes = [[], []]
    for low in range(groups):
        for near in range(0, members, 2):
            at = low * members + near
            routes[0] += [(at, (low ^ 2) * members + near), (at + 1, (low ^ 1) * members + near + 1)]
            routes[1] += [(at, (low ^ 3) * members + near), (at + 1, low * members + (near ^ 2) + 1)]
    sums = narrow(running, power)
    heard = [lax.ppermute(sums, everyone, route) for route in routes]
    left_top, left_low, last = call(
        functools.partial(stage_kernel, 6),
        [
            pltpu.VMEM(top_left.shape, BF16),
            pltpu.VMEM((capacity, member_levels * 2 * width), BF16),
            jax.ShapeDtypeStruct((2 * height, columns), F32),
        ],
        [HBM, HBM, HBM, VMEM, pl.BlockSpec(memory_space=pl.ANY)],
        (*far(top_left, low_left, diag_block), pair, running),
        8 * height * capacity * columns,
        12 << 20,
        24,
        scratch=[
            pltpu.VMEM(low_left.shape, BF16),
            pltpu.VMEM((2, 2, height, capacity), BF16),
            DMA((4,)),
        ],
    )
    bases.append(last)
    heard, left_top, left_low = lax.optimization_barrier((heard, left_top, left_low))
    heard = [widen(block)[0] for block in heard]
    own = (heard[0] + jnp.where(flags[:1] > 0, heard[1], 0.0)).astype(BF16)
    own_low = jnp.concatenate(coefs)
    their_low, own = lax.optimization_barrier((partner(own_low, "member", 0), own))
    theirs = partner(own, "member", 0)
    base = call(
        functools.partial(low_kernel, len(bases), group_levels),
        [jax.ShapeDtypeStruct((capacity, columns), F32)],
        [SMEM] + [VMEM] * (len(bases) + 4),
        (block_ranks, *bases, left_low, nearest, own_low, their_low),
        4 * capacity * columns * member_levels * width,
        3 << 20,
        16,
    )[0]

    leaving = call(
        functools.partial(out_kernel, bucket),
        [jax.ShapeDtypeStruct((capacity, columns), BF16)],
        [VMEM] * 6,
        (flags, base, left_top, own, theirs, slots),
        4 * capacity * columns * group_levels * top_width,
        4 << 20,
        24,
        scratch=[
            pltpu.VMEM((leaves * filled, 128), BF16),
            pltpu.VMEM((leaves, filled, 128), F32),
        ],
    )[0]
    returned = lax.all_to_all(
        leaving.reshape(leaves, bucket, columns), ("member", "group"), split_axis=0, concat_axis=0, tiled=True
    )
    return call(
        unpack_kernel,
        [jax.ShapeDtypeStruct((count, columns), F32)],
        [VMEM] * 3,
        (order, upper, returned.reshape(capacity, columns)),
        2 * capacity * count * columns,
        4 << 20,
        16,
        out_specs=[HBM],
        scratch=[pltpu.VMEM((count, 128), F32), DMA((count // 256,))],
    )[0]


def solution(mesh):
    return jax.shard_map(
        on_device,
        mesh=mesh,
        in_specs=(
            P(("group", "member"), None),
            P(("group", "member")),
            P(),
            P(),
            P(None, ("group", "member"), None),
            P(None, None, ("group", "member"), None),
            P(None, None, ("group", "member"), None),
            P(None, None, ("group", "member"), None),
            P(None, None, ("group", "member"), None),
        ),
        out_specs=P(("group", "member"), None),
        check_vma=False,
    )
```

```python
import functools

import jax
import jax.numpy as jnp
from jax import lax
from jax.experimental import pallas as pl
from jax.experimental.pallas import tpu as pltpu
from jax.sharding import PartitionSpec as P

F32 = jnp.float32
BF16 = jnp.bfloat16
F16 = jnp.float16
I32 = jnp.int32
VMEM = pl.BlockSpec(memory_space=pltpu.VMEM)
SMEM = pl.BlockSpec(memory_space=pltpu.SMEM)
HBM = pl.BlockSpec(memory_space=pltpu.HBM)
DMA = pltpu.SemaphoreType.DMA


def iota(shape, dim):
    return lax.broadcasted_iota(I32, shape, dim)


def hot(mask):
    return jnp.where(mask, 1.0, 0.0).astype(BF16)


def dot(a, b, over=(1, 0)):
    return lax.dot_general(
        a, b, (((over[0],), (over[1],)), ((), ())), preferred_element_type=F32
    )


def call(kernel, outs, ins, args, flops, moved, limit, scratch=(), **more):
    return pl.pallas_call(
        kernel,
        out_shape=outs,
        in_specs=ins,
        out_specs=more.pop("out_specs", [VMEM] * len(outs)),
        scratch_shapes=scratch,
        cost_estimate=pl.CostEstimate(flops=flops, bytes_accessed=moved, transcendentals=0),
        compiler_params=pltpu.CompilerParams(vmem_limit_bytes=limit << 20),
        **more,
    )(*args)


def partner(block, axis, apart):
    count = lax.axis_size(axis)
    route = []
    for low in range(count):
        high = low | 1 << apart
        if high != low and high < count:
            route += [(low, high), (high, low)]
    return lax.ppermute(block, axis, route)


def far(*arrays):
    return [pltpu.with_memory_space_constraint(array, pltpu.HBM) for array in arrays]


def bound(mine, other):
    return jnp.clip(jnp.maximum(mine, other) + 1.0, -100.0, 126.0)


def narrow(rows, power):
    return jnp.concatenate([rows * jnp.exp2(14.0 - power[:1]), power]).astype(F16)


def widen(sent):
    power = sent[-8:].astype(F32)
    return sent[:-8].astype(F32) * jnp.exp2(power[:1] - 14.0), power


def turn(block):
    half = block.shape[1] // 2
    return jnp.where(iota(block.shape, 1) < half, -1.0, 1.0) * pltpu.roll(block, half, 1)


def rank_of(ranks, level, levels):
    device = lax.axis_index("group") * lax.axis_size("member") + lax.axis_index("member")
    return ranks[(1 << level) - 2 + jnp.right_shift(device, levels - level)]


def pack_kernel(leaves, bucket, sizes_in, position_in, rows_in, packed, places, *scratch):
    sizes, position, rows, ordered, near, sems, out_sems = scratch
    copies = [
        pltpu.make_async_copy(source, target, sems.at[i])
        for i, (source, target) in enumerate(
            [(position_in, position), (rows_in, rows), (sizes_in, sizes)]
        )
    ]
    for copy in copies:
        copy.start()
    copies[0].wait()
    count = rows.shape[0]
    padded = packed.shape[1]
    shift = leaves.bit_length() - 1
    here = position[...]
    window = jnp.right_shift(here, shift)
    copies[1].wait()
    values = rows[...]
    block = 256
    for low in range(0, count, block):
        ordered[low : low + block, :] = dot(hot(iota((block, count), 0) + low == window), values)
    ordered[count:, :] = jnp.zeros((padded, 128), F32)
    copies[2].wait()
    zero = jnp.zeros((1, count), I32)
    owner, first = zero, zero
    starts = [0]
    for c in range(leaves):
        starts.append(starts[-1] + jnp.right_shift(sizes[c], shift))
        beyond = window >= starts[-1]
        owner = owner + beyond.astype(I32)
        first = jnp.where(beyond, starts[-1], first)
    offset = jnp.bitwise_and(here, leaves - 1).astype(F32)
    picked = jnp.where(iota((leaves, count), 0) == owner, offset, 0.0).astype(BF16)
    offsets = dot(picked, hot(iota((128, count), 0) == window - first), (1, 1))
    places[...] = owner * bucket + window - first
    line = iota((padded, 128), 0)
    chunk = leaves // 8
    out = []
    for c in range(leaves):
        data = ordered[pl.ds(starts[c], padded), :]
        data = jnp.where(line < starts[c + 1] - starts[c], data, 0.0)
        data = jnp.where(line == bucket, offsets[c : c + 1, :], data)
        near[c] = data.astype(BF16)
        if c % chunk == chunk - 1:
            part = pl.ds(c + 1 - chunk, chunk)
            out.append(pltpu.make_async_copy(near.at[part], packed.at[part], out_sems.at[c // chunk]))
            out[-1].start()
    for copy in out:
        copy.wait()


def near_kernel(ranks, right_top_in, right_low_in, right, flags, sems):
    tops, parts, capacity, width = right_top_in.shape
    levels, _, rows, _ = right_low_in.shape
    pairs = []
    for level in range(tops):
        for p in range(parts):
            place = (pl.ds(p * capacity, capacity), pl.ds(level * width, width))
            pairs.append((right_top_in.at[level, p], right.at[place]))
    at = parts * capacity
    for low in range(0, capacity, 256):
        for p in range(parts):
            for level in range(levels):
                source = right_low_in.at[level, p, :, pl.ds(low, 256)]
                pairs.append((source, right.at[pl.ds(at, rows), :]))
                at += rows
    copies = [pltpu.make_async_copy(a, b, sems.at[i]) for i, (a, b) in enumerate(pairs)]
    for copy in copies:
        copy.start()
    row, lane = iota(flags.shape, 0), iota(flags.shape, 1)
    marks = jnp.where(row == 0, 1 - jnp.bitwise_and(lax.axis_index("member"), 1), 0)
    for level in range(1, tops + 1):
        counts = (lane < rank_of(ranks, level, tops + levels)).astype(I32)
        marks = jnp.where(row == level, counts, marks)
    last = rank_of(ranks, tops + levels, tops + levels)
    flags[...] = jnp.where(row < 8, marks, (row - 8 < last).astype(I32)).astype(F32)
    for copy in copies:
        copy.wait()


def way_kernel(targets, places, left_low_in, after, slots, order, upper, left_last, raw, sem):
    copy = pltpu.make_async_copy(left_low_in.at[left_low_in.shape[0] - 1], raw, sem)
    copy.start()
    groups, part = targets.shape
    lanes = iota((part, 128), 1)
    for g in range(groups):
        target = jnp.transpose(jnp.broadcast_to(targets[g : g + 1, :], (128, part)))
        for low in range(0, part, 128):
            slots[g * part : (g + 1) * part, low : low + 128] = hot(target == lanes + low)
    count, folded = order.shape
    place = jnp.transpose(jnp.broadcast_to(places[...], (128, count)))
    beyond = place >= folded
    upper[...] = beyond.astype(I32)
    place = jnp.where(beyond, place - folded, place)
    block = 256
    lanes = iota((block, 128), 1)
    for low in range(0, count, block):
        for at in range(0, folded, 128):
            order[low : low + block, at : at + 128] = hot(place[low : low + block] == lanes + at)
    copy.wait()
    left_last[...] = jnp.transpose(raw[...].reshape(-1, raw.shape[2]))


def last_level(flags, nearest):
    coef = jnp.where(flags[8:, :] > 0, nearest[...], 0.0)
    return jnp.concatenate([coef, turn(coef)], axis=0).astype(BF16)


def stage_kernel(first, left_top_in, left_low_in, block_in, pair, flags, nearest, left_last, after, *rest):
    left_top, left_low, out, raw, block, sems = rest
    copies = [pltpu.make_async_copy(left_low_in.at[pl.ds(0, raw.shape[0])], raw, sems.at[0])]
    count, _, height, _ = block.shape
    for j in range(count):
        rows = pl.ds((first + j) * height, height)
        copies.append(pltpu.make_async_copy(block_in.at[:, rows, :], block.at[j], sems.at[1 + j]))
    copies.append(pltpu.make_async_copy(left_top_in, left_top, sems.at[1 + count]))
    for copy in copies:
        copy.start()
    copies[0].wait()
    levels, parts, width, capacity = raw.shape
    left_low[...] = jnp.transpose(raw[...].reshape(levels * parts * width, capacity))
    stacked = last_level(flags, nearest)
    for j in range(count):
        copies[1 + j].wait()
        far_part = dot(left_last[(first + j) * height : (first + j + 1) * height, :], stacked)
        near_part = dot(block[j, 0], pair[0]) + dot(block[j, 1], pair[1])
        out[j * height : (j + 1) * height, :] = near_part + far_part
    copies[-1].wait()


def field_kernel(leaves, bucket, tops, levels, arrived, right, *rest):
    pair, targets, send, keep, whole = rest
    capacity = leaves * bucket
    padded = arrived.shape[1]
    part = leaves * 8
    groups = targets.shape[0]
    core = jnp.bitwise_and(lax.axis_index("member"), 1)
    last = arrived[:, padded - 16 :, :].reshape(leaves * 16, 128)
    row = iota((leaves * 16, part), 0)
    spread = jnp.right_shift(iota((leaves * 16, part), 1), 3) * 16 + bucket % 16 == row
    spread_offsets = dot(last, hot(spread), (0, 0))[: groups * 8].reshape(groups, 8, part)
    lane_window = jnp.bitwise_and(iota((8, part), 1), 7)
    own = (lane_window == iota((8, part), 0))[None]
    target = jnp.sum(jnp.where(own, spread_offsets, 0.0), axis=1).astype(I32)
    target = target + lane_window[:1, :] * leaves
    targets[...] = target
    for g in range(groups):
        size = min(part, capacity - g * part)
        if g % 2 == 0:
            both = arrived[:, g * 8 : g * 8 + 16, :].astype(F32)
        chunk = both[:, g % 2 * 8 : g % 2 * 8 + 8, :].reshape(part, 128).astype(BF16)
        placed = dot(hot(iota((part, part), 0) == target[g : g + 1, :]), chunk)
        pair[0, g * part : g * part + size, :] = placed[:size].astype(BF16)
        pair[1, g * part : g * part + size, :] = turn(placed)[:size].astype(BF16)
    plain = jnp.transpose(pair[0])
    turned = jnp.concatenate([-plain[64:], plain[:64]], axis=0)
    upper = dot(plain, right[:capacity, :]) + dot(turned, right[capacity : 2 * capacity, :])
    top_rows = tops * 128
    for level in range(tops):
        whole[level * 128 : (level + 1) * 128, :] = upper[:, level * 128 : (level + 1) * 128]
    rows = whole.shape[0] - top_rows
    width = rows // levels
    lower = jnp.zeros((rows, 128), F32)
    at = 2 * capacity
    for low in range(0, capacity, 256):
        for p in range(2):
            lower += dot(right[at : at + rows, :], pair[p, low : low + 256, :])
            at += rows
    whole[top_rows:, :] = lower
    at = 0
    low = 0
    for half in [tops * 64] + [width // 2] * (levels - 1):
        mine = pl.multiple_of(low + core * half, 8)
        other = pl.multiple_of(low + (1 - core) * half, 8)
        keep[at : at + half, :] = whole[pl.ds(mine, half), :]
        send[at : at + half, :] = whole[pl.ds(other, half), :]
        at += half
        low += 2 * half
    send[at : at + width, :] = lower[(levels - 1) * width :]
    largest = jnp.max(jnp.abs(whole[...]), axis=0, keepdims=True)
    power = jnp.clip(jnp.ceil(jnp.log2(largest + 1e-30)) + 1.0, -100.0, 126.0)
    send[at + width :, :] = jnp.broadcast_to(power, (8, 128))
    keep[at:, :] = jnp.broadcast_to(power, (8, 128))


def diag_kernel(first, block_in, pair, flags, nearest, left_last, after, out, block, sems):
    count, _, height, _ = block.shape
    copies = []
    for j in range(count):
        rows = pl.ds((first + j) * height, height)
        copies.append(pltpu.make_async_copy(block_in.at[:, rows, :], block.at[j], sems.at[j]))
        copies[j].start()
    stacked = last_level(flags, nearest)
    for j in range(count):
        far_part = dot(left_last[(first + j) * height : (first + j + 1) * height, :], stacked)
        copies[j].wait()
        near_part = dot(block[j, 0], pair[0]) + dot(block[j, 1], pair[1])
        out[j * height : (j + 1) * height, :] = near_part + far_part


def merged(core, own, theirs, at, half):
    a, b = own[at : at + half, :].astype(F32), theirs[at : at + half, :].astype(F32)
    return jnp.concatenate([jnp.where(core == 0, a, b), jnp.where(core == 0, b, a)], axis=0)


def low_kernel(pieces, tops, ranks, *rest):
    bases = rest[:pieces]
    left_low, own, theirs, out = rest[pieces:]
    core = jnp.bitwise_and(lax.axis_index("member"), 1)
    half = own.shape[0] // (left_low.shape[1] // 128)
    levels = own.shape[0] // half
    stacked = []
    for level in range(levels):
        coef = merged(core, own, theirs, level * half, half)
        rank = rank_of(ranks, 1 + tops + level, tops + levels + 1)
        coef = jnp.where(iota(coef.shape, 0) < rank, coef, 0.0)
        stacked += [coef, turn(coef)]
    stacked = jnp.concatenate(stacked, axis=0).astype(BF16)
    low = 0
    for base in bases:
        rows = slice(low, low + base.shape[0])
        out[rows, :] = base[...] + dot(left_low[rows, :], stacked)
        low += base.shape[0]


def out_kernel(bucket, flags, base, left_top, own, theirs, slots, packed, spare, ordered):
    capacity = base.shape[0]
    part = slots.shape[1]
    groups = slots.shape[0] // part
    leaves = part // 8
    first = flags[:1, :] > 0
    levels = left_top.shape[0]
    half = own.shape[0]
    stacked = []
    for level in range(levels):
        pick = (own, theirs) if level == 0 else (theirs, own)
        coef = jnp.where(first, pick[0][...].astype(F32), pick[1][...].astype(F32))
        coef = jnp.where(flags[1 + level : 2 + level, :] > 0, coef, 0.0)
        turned = jnp.concatenate([-coef[half // 2 :], coef[: half // 2]], axis=0)
        stacked += [jnp.transpose(coef), jnp.transpose(turned)]
    stacked = jnp.concatenate(stacked, axis=0).astype(BF16)
    if groups * part > capacity:
        spare[capacity:, :] = jnp.zeros((groups * part - capacity, 128), BF16)
    factors = [left_top[level, p] for level in range(levels) for p in range(2)]
    total = base[...] + dot(jnp.concatenate(factors, axis=1), stacked)
    spare[:capacity, :] = total.astype(BF16)
    for g in range(groups):
        moved = dot(slots[g * part : (g + 1) * part, :], spare[g * part : (g + 1) * part, :])
        ordered[:, g * 8 : g * 8 + 8, :] = moved.reshape(leaves, 8, 128)
    packed[...] = ordered[:, :bucket, :].reshape(capacity, 128).astype(BF16)


def unpack_kernel(order, upper, returned, out, near, sems):
    count, folded = order.shape
    wide = jnp.concatenate([returned[:folded, :], returned[folded:, :]], axis=1)
    block = 256
    copies = []
    for low in range(0, count, block):
        rows = pl.ds(low, block)
        both = dot(order[low : low + block, :], wide)
        near[rows, :] = jnp.where(upper[low : low + block, :] != 0, both[:, 128:], both[:, :128])
        copies.append(pltpu.make_async_copy(near.at[rows, :], out.at[rows, :], sems.at[low // block]))
        copies[-1].start()
    for copy in copies:
        copy.wait()


def on_device(
    mesh_vector,
    cluster_position,
    cluster_sizes,
    block_ranks,
    diag_block,
    top_left,
    top_right,
    low_left,
    low_right,
):
    groups = lax.axis_size("group")
    members = lax.axis_size("member")
    leaves = groups * members
    group_levels = groups.bit_length() - 1
    member_levels = members.bit_length() - 1
    capacity = diag_block.shape[1]
    bucket = capacity // leaves
    padded = (bucket + 16) // 16 * 16
    filled = (bucket + 7) // 8 * 8
    count, columns = mesh_vector.shape
    everyone = ("group", "member")
    low_left = jnp.swapaxes(low_left, 2, 3)
    low_right = jnp.swapaxes(low_right, 2, 3)
    width = low_left.shape[2]
    top_width = top_left.shape[3]
    far_flops = 4 * capacity * columns * (group_levels * top_width + member_levels * width)

    packed, places = call(
        functools.partial(pack_kernel, leaves, bucket),
        [
            jax.ShapeDtypeStruct((leaves, padded, columns), BF16),
            jax.ShapeDtypeStruct((1, count), I32),
        ],
        [HBM] * 3,
        far(cluster_sizes, cluster_position.reshape(1, count), mesh_vector),
        2 * count * count * columns,
        4 << 20,
        16,
        out_specs=[HBM, VMEM],
        scratch=[
            pltpu.SMEM((leaves,), I32),
            pltpu.VMEM((1, count), I32),
            pltpu.VMEM((count, columns), BF16),
            pltpu.VMEM((count + padded, columns), F32),
            pltpu.VMEM((leaves, padded, columns), BF16),
            DMA((3,)),
            DMA((8,)),
        ],
    )
    arrived = lax.all_to_all(packed, everyone, split_axis=0, concat_axis=0, tiled=True)
    ranked = group_levels * top_width + member_levels * width
    right, flags = call(
        near_kernel,
        [
            pltpu.VMEM((2 * ranked * capacity // 256, 256), BF16),
            jax.ShapeDtypeStruct((8 + width, columns), F32),
        ],
        [SMEM, HBM, HBM],
        (block_ranks, *far(top_right, low_right)),
        0,
        6 << 20,
        16,
        scratch=[DMA((2 * group_levels + 2 * member_levels * capacity // 256,))],
    )
    tops = group_levels * columns // 2
    shared = tops + (member_levels - 1) * width // 2
    pair, targets, send, keep = call(
        functools.partial(field_kernel, leaves, bucket, group_levels, member_levels),
        [
            jax.ShapeDtypeStruct((2, capacity, columns), BF16),
            jax.ShapeDtypeStruct((filled // 8, leaves * 8), I32),
            jax.ShapeDtypeStruct((shared + width + 8, columns), F32),
            jax.ShapeDtypeStruct((shared + 8, columns), F32),
        ],
        [VMEM, VMEM],
        (arrived, right),
        far_flops,
        6 << 20,
        24,
        scratch=[pltpu.VMEM((2 * shared + width, columns), F32)],
    )
    height = capacity // 8

    def diagonal(first, chunks, after):
        return call(
            functools.partial(diag_kernel, first),
            [jax.ShapeDtypeStruct((chunks * height, columns), F32)],
            [HBM] + [VMEM] * 4 + [pl.BlockSpec(memory_space=pl.ANY)],
            (*far(diag_block), pair, flags, nearest, left_last, after),
            4 * chunks * height * capacity * columns,
            4 * chunks * height * capacity,
            24,
            scratch=[pltpu.VMEM((chunks, 2, height, capacity), BF16), DMA((chunks,))],
        )[0]

    received = partner(send, "member", 0)
    slots, order, upper, left_last = call(
        way_kernel,
        [
            jax.ShapeDtypeStruct((leaves * filled, leaves * 8), BF16),
            jax.ShapeDtypeStruct((count, capacity // 2), BF16),
            jax.ShapeDtypeStruct((count, 128), I32),
            jax.ShapeDtypeStruct((capacity, 2 * width), BF16),
        ],
        [VMEM, VMEM, HBM, pl.BlockSpec(memory_space=pl.ANY)],
        (targets, places, *far(low_left), send),
        0,
        8 << 20,
        16,
        scratch=[pltpu.VMEM(low_left.shape[1:], BF16), DMA],
    )
    received, slots, order, upper, left_last = lax.optimization_barrier(
        (received, slots, order, upper, left_last)
    )
    nearest = received[shared : shared + width]
    running = keep[:shared] + received[:shared]
    power = bound(keep[shared:], received[shared + width :])
    bases = []
    coefs = []
    for bit in range(1, member_levels):
        rest = running.shape[0] - width // 2
        received = partner(narrow(running, power), "member", bit)
        if bit == 1:
            bases.append(diagonal(0, 3, running))
            received, bases[0] = lax.optimization_barrier((received, bases[0]))
        if bit == member_levels - 1:
            bases.append(diagonal(3, 3, running))
            received, bases[1] = lax.optimization_barrier((received, bases[1]))
        received, other = widen(received)
        power = bound(power, other)
        coefs.insert(0, received[rest:].astype(BF16))
        running = running[:rest] + received[:rest]
    routes = [[], []]
    for low in range(groups):
        for near in range(0, members, 2):
            at = low * members + near
            routes[0] += [(at, (low ^ 2) * members + near), (at + 1, (low ^ 1) * members + near + 1)]
            routes[1] += [(at, (low ^ 3) * members + near), (at + 1, low * members + (near ^ 2) + 1)]
    sums = narrow(running, power)
    heard = [lax.ppermute(sums, everyone, route) for route in routes]
    left_top, left_low, last = call(
        functools.partial(stage_kernel, 6),
        [
            pltpu.VMEM(top_left.shape, BF16),
            pltpu.VMEM((capacity, (member_levels - 1) * 2 * width), BF16),
            jax.ShapeDtypeStruct((2 * height, columns), F32),
        ],
        [HBM] * 3 + [VMEM] * 4 + [pl.BlockSpec(memory_space=pl.ANY)],
        (*far(top_left, low_left, diag_block), pair, flags, nearest, left_last, running),
        8 * height * capacity * columns,
        12 << 20,
        24,
        scratch=[
            pltpu.VMEM((member_levels - 1,) + low_left.shape[1:], BF16),
            pltpu.VMEM((2, 2, height, capacity), BF16),
            DMA((4,)),
        ],
    )
    bases.append(last)
    heard, left_top, left_low = lax.optimization_barrier((heard, left_top, left_low))
    heard = [widen(block)[0] for block in heard]
    own = (heard[0] + jnp.where(flags[:1] > 0, heard[1], 0.0)).astype(BF16)
    own_low = jnp.concatenate(coefs)
    their_low, own = lax.optimization_barrier((partner(own_low, "member", 0), own))
    theirs = partner(own, "member", 0)
    base = call(
        functools.partial(low_kernel, len(bases), group_levels),
        [jax.ShapeDtypeStruct((capacity, columns), F32)],
        [SMEM] + [VMEM] * (len(bases) + 3),
        (block_ranks, *bases, left_low, own_low, their_low),
        4 * capacity * columns * member_levels * width,
        3 << 20,
        16,
    )[0]

    leaving = call(
        functools.partial(out_kernel, bucket),
        [jax.ShapeDtypeStruct((capacity, columns), BF16)],
        [VMEM] * 6,
        (flags, base, left_top, own, theirs, slots),
        4 * capacity * columns * group_levels * top_width,
        4 << 20,
        24,
        scratch=[
            pltpu.VMEM((leaves * filled, 128), BF16),
            pltpu.VMEM((leaves, filled, 128), F32),
        ],
    )[0]
    returned = lax.all_to_all(
        leaving.reshape(leaves, bucket, columns), everyone, split_axis=0, concat_axis=0, tiled=True
    )
    return call(
        unpack_kernel,
        [jax.ShapeDtypeStruct((count, columns), F32)],
        [VMEM] * 3,
        (order, upper, returned.reshape(capacity, columns)),
        2 * capacity * count * columns,
        4 << 20,
        16,
        out_specs=[HBM],
        scratch=[pltpu.VMEM((count, 128), F32), DMA((count // 256,))],
    )[0]


def solution(mesh):
    return jax.shard_map(
        on_device,
        mesh=mesh,
        in_specs=(
            P(("group", "member"), None),
            P(("group", "member")),
            P(),
            P(),
            P(None, ("group", "member"), None),
            P(None, None, ("group", "member"), None),
            P(None, None, ("group", "member"), None),
            P(None, None, ("group", "member"), None),
            P(None, None, ("group", "member"), None),
        ),
        out_specs=P(("group", "member"), None),
        check_vma=False,
    )
```

```python
import functools

import jax
import jax.numpy as jnp
from jax import lax
from jax.experimental import pallas as pl
from jax.experimental.pallas import tpu as pltpu
from jax.sharding import PartitionSpec as P

F32 = jnp.float32
BF16 = jnp.bfloat16
F16 = jnp.float16
I32 = jnp.int32
VMEM = pl.BlockSpec(memory_space=pltpu.VMEM)
SMEM = pl.BlockSpec(memory_space=pltpu.SMEM)
HBM = pl.BlockSpec(memory_space=pltpu.HBM)
DMA = pltpu.SemaphoreType.DMA


def iota(shape, dim):
    return lax.broadcasted_iota(I32, shape, dim)


def hot(mask):
    return jnp.where(mask, 1.0, 0.0).astype(BF16)


def dot(a, b, over=(1, 0)):
    return lax.dot_general(
        a, b, (((over[0],), (over[1],)), ((), ())), preferred_element_type=F32
    )


def call(kernel, outs, ins, args, flops, moved, limit, scratch=(), **more):
    return pl.pallas_call(
        kernel,
        out_shape=outs,
        in_specs=ins,
        out_specs=more.pop("out_specs", [VMEM] * len(outs)),
        scratch_shapes=scratch,
        cost_estimate=pl.CostEstimate(flops=flops, bytes_accessed=moved, transcendentals=0),
        compiler_params=pltpu.CompilerParams(vmem_limit_bytes=limit << 20),
        **more,
    )(*args)


def partner(block, axis, apart):
    count = lax.axis_size(axis)
    route = []
    for low in range(count):
        high = low | 1 << apart
        if high != low and high < count:
            route += [(low, high), (high, low)]
    return lax.ppermute(block, axis, route)


def far(*arrays):
    return [pltpu.with_memory_space_constraint(array, pltpu.HBM) for array in arrays]


def bound(mine, other):
    return jnp.clip(jnp.maximum(mine, other) + 1.0, -100.0, 126.0)


def narrow(rows, power):
    return jnp.concatenate([rows * jnp.exp2(14.0 - power[:1]), power]).astype(F16)


def widen(sent):
    power = sent[-8:].astype(F32)
    return sent[:-8].astype(F32) * jnp.exp2(power[:1] - 14.0), power


def turn(block):
    half = block.shape[1] // 2
    return jnp.where(iota(block.shape, 1) < half, -1.0, 1.0) * pltpu.roll(block, half, 1)


def rank_of(ranks, level, levels):
    device = lax.axis_index("group") * lax.axis_size("member") + lax.axis_index("member")
    return ranks[(1 << level) - 2 + jnp.right_shift(device, levels - level)]


def pack_kernel(leaves, bucket, sizes_in, position_in, rows_in, packed, places, *scratch):
    sizes, position, rows, ordered, near, sems, out_sems = scratch
    copies = [
        pltpu.make_async_copy(source, target, sems.at[i])
        for i, (source, target) in enumerate(
            [(position_in, position), (rows_in, rows), (sizes_in, sizes)]
        )
    ]
    for copy in copies:
        copy.start()
    copies[0].wait()
    count = rows.shape[0]
    padded = packed.shape[1]
    shift = leaves.bit_length() - 1
    here = position[...]
    window = jnp.right_shift(here, shift)
    copies[1].wait()
    values = rows[...]
    block = 256
    for low in range(0, count, block):
        ordered[low : low + block, :] = dot(hot(iota((block, count), 0) + low == window), values)
    ordered[count:, :] = jnp.zeros((padded, 128), F32)
    copies[2].wait()
    zero = jnp.zeros((1, count), I32)
    owner, first = zero, zero
    starts = [0]
    for c in range(leaves):
        starts.append(starts[-1] + jnp.right_shift(sizes[c], shift))
        beyond = window >= starts[-1]
        owner = owner + beyond.astype(I32)
        first = jnp.where(beyond, starts[-1], first)
    offset = jnp.bitwise_and(here, leaves - 1).astype(F32)
    picked = jnp.where(iota((leaves, count), 0) == owner, offset, 0.0).astype(BF16)
    offsets = dot(picked, hot(iota((128, count), 0) == window - first), (1, 1))
    places[...] = owner * bucket + window - first
    line = iota((padded, 128), 0)
    chunk = leaves // 8
    out = []
    for c in range(leaves):
        data = ordered[pl.ds(starts[c], padded), :]
        data = jnp.where(line < starts[c + 1] - starts[c], data, 0.0)
        data = jnp.where(line == bucket, offsets[c : c + 1, :], data)
        near[c] = data.astype(BF16)
        if c % chunk == chunk - 1:
            part = pl.ds(c + 1 - chunk, chunk)
            out.append(pltpu.make_async_copy(near.at[part], packed.at[part], out_sems.at[c // chunk]))
            out[-1].start()
    for copy in out:
        copy.wait()


def near_kernel(ranks, right_top_in, right_low_in, right, flags, sems):
    tops, parts, capacity, width = right_top_in.shape
    levels, _, rows, _ = right_low_in.shape
    pairs = []
    for level in range(tops):
        for p in range(parts):
            place = (pl.ds(p * capacity, capacity), pl.ds(level * width, width))
            pairs.append((right_top_in.at[level, p], right.at[place]))
    at = parts * capacity
    for low in range(0, capacity, 256):
        for p in range(parts):
            for level in range(levels):
                source = right_low_in.at[level, p, :, pl.ds(low, 256)]
                pairs.append((source, right.at[pl.ds(at, rows), :]))
                at += rows
    copies = [pltpu.make_async_copy(a, b, sems.at[i]) for i, (a, b) in enumerate(pairs)]
    for copy in copies:
        copy.start()
    row, lane = iota(flags.shape, 0), iota(flags.shape, 1)
    marks = jnp.where(row == 0, 1 - jnp.bitwise_and(lax.axis_index("member"), 1), 0)
    for level in range(1, tops + 1):
        counts = (lane < rank_of(ranks, level, tops + levels)).astype(I32)
        marks = jnp.where(row == level, counts, marks)
    for level in range(levels):
        inside = row - 8 - level * rows
        counts = (inside < rank_of(ranks, 1 + tops + level, tops + levels)).astype(I32)
        marks = jnp.where(inside >= 0, counts, marks)
    flags[...] = marks.astype(F32)
    for copy in copies:
        copy.wait()


def way_kernel(targets, places, after, slots, order, upper):
    groups, part = targets.shape
    lanes = iota((part, 128), 1)
    for g in range(groups):
        target = jnp.transpose(jnp.broadcast_to(targets[g : g + 1, :], (128, part)))
        for low in range(0, part, 128):
            slots[g * part : (g + 1) * part, low : low + 128] = hot(target == lanes + low)
    count, folded = order.shape
    place = jnp.transpose(jnp.broadcast_to(places[...], (128, count)))
    beyond = place >= folded
    upper[...] = beyond.astype(I32)
    place = jnp.where(beyond, place - folded, place)
    block = 256
    lanes = iota((block, 128), 1)
    for low in range(0, count, block):
        for at in range(0, folded, 128):
            order[low : low + block, at : at + 128] = hot(place[low : low + block] == lanes + at)


def stage_kernel(first, left_top_in, left_low_in, block_in, pair, after, *rest):
    left_top, left_low, out, raw, block, sems = rest
    copies = [pltpu.make_async_copy(left_low_in, raw, sems.at[0])]
    count, _, height, _ = block.shape
    for j in range(count):
        rows = pl.ds((first + j) * height, height)
        copies.append(pltpu.make_async_copy(block_in.at[:, rows, :], block.at[j], sems.at[1 + j]))
    copies.append(pltpu.make_async_copy(left_top_in, left_top, sems.at[1 + count]))
    for copy in copies:
        copy.start()
    copies[0].wait()
    levels, parts, width, capacity = raw.shape
    left_low[...] = jnp.transpose(raw[...].reshape(levels * parts * width, capacity))
    for j in range(count):
        copies[1 + j].wait()
        out[j * height : (j + 1) * height, :] = dot(block[j, 0], pair[0]) + dot(block[j, 1], pair[1])
    copies[-1].wait()


def field_kernel(leaves, bucket, tops, levels, arrived, right, *rest):
    pair, targets, send, keep, whole = rest
    capacity = leaves * bucket
    padded = arrived.shape[1]
    part = leaves * 8
    groups = targets.shape[0]
    core = jnp.bitwise_and(lax.axis_index("member"), 1)
    last = arrived[:, padded - 16 :, :].reshape(leaves * 16, 128)
    row = iota((leaves * 16, part), 0)
    spread = jnp.right_shift(iota((leaves * 16, part), 1), 3) * 16 + bucket % 16 == row
    spread_offsets = dot(last, hot(spread), (0, 0))[: groups * 8].reshape(groups, 8, part)
    lane_window = jnp.bitwise_and(iota((8, part), 1), 7)
    own = (lane_window == iota((8, part), 0))[None]
    target = jnp.sum(jnp.where(own, spread_offsets, 0.0), axis=1).astype(I32)
    target = target + lane_window[:1, :] * leaves
    targets[...] = target
    for g in range(groups):
        size = min(part, capacity - g * part)
        if g % 2 == 0:
            both = arrived[:, g * 8 : g * 8 + 16, :].astype(F32)
        chunk = both[:, g % 2 * 8 : g % 2 * 8 + 8, :].reshape(part, 128).astype(BF16)
        placed = dot(hot(iota((part, part), 0) == target[g : g + 1, :]), chunk)
        pair[0, g * part : g * part + size, :] = placed[:size].astype(BF16)
        pair[1, g * part : g * part + size, :] = turn(placed)[:size].astype(BF16)
    plain = jnp.transpose(pair[0])
    turned = jnp.concatenate([-plain[64:], plain[:64]], axis=0)
    upper = dot(plain, right[:capacity, :]) + dot(turned, right[capacity : 2 * capacity, :])
    top_rows = tops * 128
    for level in range(tops):
        whole[level * 128 : (level + 1) * 128, :] = upper[:, level * 128 : (level + 1) * 128]
    rows = whole.shape[0] - top_rows
    width = rows // levels
    lower = jnp.zeros((rows, 128), F32)
    at = 2 * capacity
    for low in range(0, capacity, 256):
        for p in range(2):
            lower += dot(right[at : at + rows, :], pair[p, low : low + 256, :])
            at += rows
    whole[top_rows:, :] = lower
    at = 0
    low = 0
    for half in [tops * 64] + [width // 2] * (levels - 1):
        mine = pl.multiple_of(low + core * half, 8)
        other = pl.multiple_of(low + (1 - core) * half, 8)
        keep[at : at + half, :] = whole[pl.ds(mine, half), :]
        send[at : at + half, :] = whole[pl.ds(other, half), :]
        at += half
        low += 2 * half
    send[at : at + width, :] = lower[(levels - 1) * width :]
    largest = jnp.max(jnp.abs(whole[...]), axis=0, keepdims=True)
    power = jnp.clip(jnp.ceil(jnp.log2(largest + 1e-30)) + 1.0, -100.0, 126.0)
    send[at + width :, :] = jnp.broadcast_to(power, (8, 128))
    keep[at:, :] = jnp.broadcast_to(power, (8, 128))


def diag_kernel(first, block_in, pair, after, out, block, sems):
    count, _, height, _ = block.shape
    copies = []
    for j in range(count):
        rows = pl.ds((first + j) * height, height)
        copies.append(pltpu.make_async_copy(block_in.at[:, rows, :], block.at[j], sems.at[j]))
        copies[j].start()
    for j in range(count):
        copies[j].wait()
        out[j * height : (j + 1) * height, :] = dot(block[j, 0], pair[0]) + dot(block[j, 1], pair[1])


def merged(core, own, theirs, at, half):
    a, b = own[at : at + half, :].astype(F32), theirs[at : at + half, :].astype(F32)
    return jnp.concatenate([jnp.where(core == 0, a, b), jnp.where(core == 0, b, a)], axis=0)


def low_kernel(pieces, flags, *rest):
    bases = rest[:pieces]
    left_low, nearest, own, theirs, out = rest[pieces:]
    width = nearest.shape[0]
    levels = left_low.shape[1] // (2 * width)
    core = jnp.bitwise_and(lax.axis_index("member"), 1)
    half = width // 2
    stacked = []
    for level in range(levels):
        if level < levels - 1:
            coef = merged(core, own, theirs, level * half, half)
        else:
            coef = nearest[...]
        coef = jnp.where(flags[8 + level * width : 8 + (level + 1) * width, :] > 0, coef, 0.0)
        stacked += [coef, turn(coef)]
    stacked = jnp.concatenate(stacked, axis=0).astype(BF16)
    low = 0
    for base in bases:
        rows = slice(low, low + base.shape[0])
        out[rows, :] = base[...] + dot(left_low[rows, :], stacked)
        low += base.shape[0]


def out_kernel(bucket, flags, base, left_top, own, theirs, slots, packed, spare, ordered):
    capacity = base.shape[0]
    part = slots.shape[1]
    groups = slots.shape[0] // part
    leaves = part // 8
    first = flags[:1, :] > 0
    levels = left_top.shape[0]
    half = own.shape[0]
    stacked = []
    for level in range(levels):
        pick = (own, theirs) if level == 0 else (theirs, own)
        coef = jnp.where(first, pick[0][...].astype(F32), pick[1][...].astype(F32))
        coef = jnp.where(flags[1 + level : 2 + level, :] > 0, coef, 0.0)
        turned = jnp.concatenate([-coef[half // 2 :], coef[: half // 2]], axis=0)
        stacked += [jnp.transpose(coef), jnp.transpose(turned)]
    stacked = jnp.concatenate(stacked, axis=0).astype(BF16)
    if groups * part > capacity:
        spare[capacity:, :] = jnp.zeros((groups * part - capacity, 128), BF16)
    factors = [left_top[level, p] for level in range(levels) for p in range(2)]
    total = base[...] + dot(jnp.concatenate(factors, axis=1), stacked)
    spare[:capacity, :] = total.astype(BF16)
    for g in range(groups):
        moved = dot(slots[g * part : (g + 1) * part, :], spare[g * part : (g + 1) * part, :])
        ordered[:, g * 8 : g * 8 + 8, :] = moved.reshape(leaves, 8, 128)
    packed[...] = ordered[:, :bucket, :].reshape(capacity, 128).astype(BF16)


def unpack_kernel(order, upper, returned, out, near, sems):
    count, folded = order.shape
    wide = jnp.concatenate([returned[:folded, :], returned[folded:, :]], axis=1)
    block = 256
    copies = []
    for low in range(0, count, block):
        rows = pl.ds(low, block)
        both = dot(order[low : low + block, :], wide)
        near[rows, :] = jnp.where(upper[low : low + block, :] != 0, both[:, 128:], both[:, :128])
        copies.append(pltpu.make_async_copy(near.at[rows, :], out.at[rows, :], sems.at[low // block]))
        copies[-1].start()
    for copy in copies:
        copy.wait()


def on_device(
    mesh_vector,
    cluster_position,
    cluster_sizes,
    block_ranks,
    diag_block,
    top_left,
    top_right,
    low_left,
    low_right,
):
    groups = lax.axis_size("group")
    members = lax.axis_size("member")
    leaves = groups * members
    group_levels = groups.bit_length() - 1
    member_levels = members.bit_length() - 1
    capacity = diag_block.shape[1]
    bucket = capacity // leaves
    padded = (bucket + 16) // 16 * 16
    filled = (bucket + 7) // 8 * 8
    count, columns = mesh_vector.shape
    everyone = ("group", "member")
    low_left = jnp.swapaxes(low_left, 2, 3)
    low_right = jnp.swapaxes(low_right, 2, 3)
    width = low_left.shape[2]
    top_width = top_left.shape[3]
    far_flops = 4 * capacity * columns * (group_levels * top_width + member_levels * width)

    packed, places = call(
        functools.partial(pack_kernel, leaves, bucket),
        [
            jax.ShapeDtypeStruct((leaves, padded, columns), BF16),
            jax.ShapeDtypeStruct((1, count), I32),
        ],
        [HBM] * 3,
        far(cluster_sizes, cluster_position.reshape(1, count), mesh_vector),
        2 * count * count * columns,
        4 << 20,
        16,
        out_specs=[HBM, VMEM],
        scratch=[
            pltpu.SMEM((leaves,), I32),
            pltpu.VMEM((1, count), I32),
            pltpu.VMEM((count, columns), BF16),
            pltpu.VMEM((count + padded, columns), F32),
            pltpu.VMEM((leaves, padded, columns), BF16),
            DMA((3,)),
            DMA((8,)),
        ],
    )
    arrived = lax.all_to_all(packed, everyone, split_axis=0, concat_axis=0, tiled=True)
    ranked = group_levels * top_width + member_levels * width
    right, flags = call(
        near_kernel,
        [
            pltpu.VMEM((2 * ranked * capacity // 256, 256), BF16),
            jax.ShapeDtypeStruct((8 + member_levels * width, columns), F32),
        ],
        [SMEM, HBM, HBM],
        (block_ranks, *far(top_right, low_right)),
        0,
        6 << 20,
        16,
        scratch=[DMA((2 * group_levels + 2 * member_levels * capacity // 256,))],
    )
    tops = group_levels * columns // 2
    shared = tops + (member_levels - 1) * width // 2
    pair, targets, send, keep = call(
        functools.partial(field_kernel, leaves, bucket, group_levels, member_levels),
        [
            jax.ShapeDtypeStruct((2, capacity, columns), BF16),
            jax.ShapeDtypeStruct((filled // 8, leaves * 8), I32),
            jax.ShapeDtypeStruct((shared + width + 8, columns), F32),
            jax.ShapeDtypeStruct((shared + 8, columns), F32),
        ],
        [VMEM, VMEM],
        (arrived, right),
        far_flops,
        6 << 20,
        24,
        scratch=[pltpu.VMEM((2 * shared + width, columns), F32)],
    )
    height = capacity // 8

    def diagonal(first, chunks, after):
        return call(
            functools.partial(diag_kernel, first),
            [jax.ShapeDtypeStruct((chunks * height, columns), F32)],
            [HBM, VMEM, pl.BlockSpec(memory_space=pl.ANY)],
            (*far(diag_block), pair, after),
            4 * chunks * height * capacity * columns,
            4 * chunks * height * capacity,
            24,
            scratch=[pltpu.VMEM((chunks, 2, height, capacity), BF16), DMA((chunks,))],
        )[0]

    received = partner(send, "member", 0)
    slots, order, upper = call(
        way_kernel,
        [
            jax.ShapeDtypeStruct((leaves * filled, leaves * 8), BF16),
            jax.ShapeDtypeStruct((count, capacity // 2), BF16),
            jax.ShapeDtypeStruct((count, 128), I32),
        ],
        [VMEM, VMEM, pl.BlockSpec(memory_space=pl.ANY)],
        (targets, places, send),
        0,
        8 << 20,
        16,
    )
    received, slots, order, upper = lax.optimization_barrier((received, slots, order, upper))
    nearest = received[shared : shared + width]
    running = keep[:shared] + received[:shared]
    power = bound(keep[shared:], received[shared + width :])
    bases = []
    coefs = []
    for bit in range(1, member_levels):
        rest = running.shape[0] - width // 2
        received = partner(narrow(running, power), "member", bit)
        if bit == 1:
            bases.append(diagonal(0, 3, running))
            received, bases[0] = lax.optimization_barrier((received, bases[0]))
        if bit == member_levels - 1:
            bases.append(diagonal(3, 3, running))
            received, bases[1] = lax.optimization_barrier((received, bases[1]))
        received, other = widen(received)
        power = bound(power, other)
        coefs.insert(0, received[rest:].astype(BF16))
        running = running[:rest] + received[:rest]
    routes = [[], []]
    for low in range(groups):
        for near in range(0, members, 2):
            at = low * members + near
            routes[0] += [(at, (low ^ 2) * members + near), (at + 1, (low ^ 1) * members + near + 1)]
            routes[1] += [(at, (low ^ 3) * members + near), (at + 1, low * members + (near ^ 2) + 1)]
    sums = narrow(running, power)
    heard = [lax.ppermute(sums, everyone, route) for route in routes]
    left_top, left_low, last = call(
        functools.partial(stage_kernel, 6),
        [
            pltpu.VMEM(top_left.shape, BF16),
            pltpu.VMEM((capacity, member_levels * 2 * width), BF16),
            jax.ShapeDtypeStruct((2 * height, columns), F32),
        ],
        [HBM, HBM, HBM, VMEM, pl.BlockSpec(memory_space=pl.ANY)],
        (*far(top_left, low_left, diag_block), pair, running),
        8 * height * capacity * columns,
        12 << 20,
        24,
        scratch=[
            pltpu.VMEM(low_left.shape, BF16),
            pltpu.VMEM((2, 2, height, capacity), BF16),
            DMA((4,)),
        ],
    )
    bases.append(last)
    heard, left_top, left_low = lax.optimization_barrier((heard, left_top, left_low))
    heard = [widen(block)[0] for block in heard]
    own = (heard[0] + jnp.where(flags[:1] > 0, heard[1], 0.0)).astype(BF16)
    own_low = jnp.concatenate(coefs)
    their_low, own = lax.optimization_barrier((partner(own_low, "member", 0), own))
    theirs = partner(own, "member", 0)
    base = call(
        functools.partial(low_kernel, len(bases)),
        [jax.ShapeDtypeStruct((capacity, columns), F32)],
        [VMEM] * (len(bases) + 5),
        (flags, *bases, left_low, nearest, own_low, their_low),
        4 * capacity * columns * member_levels * width,
        3 << 20,
        16,
    )[0]

    leaving = call(
        functools.partial(out_kernel, bucket),
        [jax.ShapeDtypeStruct((capacity, columns), BF16)],
        [VMEM] * 6,
        (flags, base, left_top, own, theirs, slots),
        4 * capacity * columns * group_levels * top_width,
        4 << 20,
        24,
        scratch=[
            pltpu.VMEM((leaves * filled, 128), BF16),
            pltpu.VMEM((leaves, filled, 128), F32),
        ],
    )[0]
    returned = lax.all_to_all(
        leaving.reshape(leaves, bucket, columns), everyone, split_axis=0, concat_axis=0, tiled=True
    )
    return call(
        unpack_kernel,
        [jax.ShapeDtypeStruct((count, columns), F32)],
        [VMEM] * 3,
        (order, upper, returned.reshape(capacity, columns)),
        2 * capacity * count * columns,
        4 << 20,
        16,
        out_specs=[HBM],
        scratch=[pltpu.VMEM((count, 128), F32), DMA((count // 256,))],
    )[0]


def solution(mesh):
    return jax.shard_map(
        on_device,
        mesh=mesh,
        in_specs=(
            P(("group", "member"), None),
            P(("group", "member")),
            P(),
            P(),
            P(None, ("group", "member"), None),
            P(None, None, ("group", "member"), None),
            P(None, None, ("group", "member"), None),
            P(None, None, ("group", "member"), None),
            P(None, None, ("group", "member"), None),
        ),
        out_specs=P(("group", "member"), None),
        check_vma=False,
    )
```

```python
import functools

import jax
import jax.numpy as jnp
from jax import lax
from jax.experimental import pallas as pl
from jax.experimental.pallas import tpu as pltpu
from jax.sharding import PartitionSpec as P

F32 = jnp.float32
BF16 = jnp.bfloat16
F16 = jnp.float16
I32 = jnp.int32
VMEM = pl.BlockSpec(memory_space=pltpu.VMEM)
SMEM = pl.BlockSpec(memory_space=pltpu.SMEM)
HBM = pl.BlockSpec(memory_space=pltpu.HBM)
DMA = pltpu.SemaphoreType.DMA


def iota(shape, dim):
    return lax.broadcasted_iota(I32, shape, dim)


def hot(mask):
    return jnp.where(mask, 1.0, 0.0).astype(BF16)


def dot(a, b, over=(1, 0)):
    return lax.dot_general(
        a, b, (((over[0],), (over[1],)), ((), ())), preferred_element_type=F32
    )


def call(kernel, outs, ins, args, flops, moved, limit, scratch=(), **more):
    return pl.pallas_call(
        kernel,
        out_shape=outs,
        in_specs=ins,
        out_specs=more.pop("out_specs", [VMEM] * len(outs)),
        scratch_shapes=scratch,
        cost_estimate=pl.CostEstimate(flops=flops, bytes_accessed=moved, transcendentals=0),
        compiler_params=pltpu.CompilerParams(vmem_limit_bytes=limit << 20),
        **more,
    )(*args)


def partner(block, axis, apart):
    count = lax.axis_size(axis)
    route = []
    for low in range(count):
        high = low | 1 << apart
        if high != low and high < count:
            route += [(low, high), (high, low)]
    return lax.ppermute(block, axis, route)


def far(*arrays):
    return [pltpu.with_memory_space_constraint(array, pltpu.HBM) for array in arrays]


def bound(mine, other):
    return jnp.clip(jnp.maximum(mine, other) + 1.0, -100.0, 126.0)


def stretch(power, heights):
    parts = [jnp.broadcast_to(power[i : i + 1], (h, power.shape[1])) for i, h in enumerate(heights)]
    return jnp.concatenate(parts)


def narrow(rows, power, heights):
    return jnp.concatenate([rows * jnp.exp2(14.0 - stretch(power, heights)), power]).astype(F16)


def widen(sent, heights):
    power = sent[-8:].astype(F32)
    return sent[:-8].astype(F32) * jnp.exp2(stretch(power, heights) - 14.0), power


def turn(block):
    half = block.shape[1] // 2
    return jnp.where(iota(block.shape, 1) < half, -1.0, 1.0) * pltpu.roll(block, half, 1)


def rank_of(ranks, level, levels, other=0):
    device = lax.axis_index("group") * lax.axis_size("member") + lax.axis_index("member")
    node = jnp.bitwise_xor(jnp.right_shift(device, levels - level), other)
    return ranks[(1 << level) - 2 + node]


def pack_kernel(leaves, bucket, sizes_in, position_in, rows_in, packed, places, *scratch):
    sizes, position, rows, ordered, near, sems, out_sems = scratch
    copies = [
        pltpu.make_async_copy(source, target, sems.at[i])
        for i, (source, target) in enumerate(
            [(position_in, position), (rows_in, rows), (sizes_in, sizes)]
        )
    ]
    for copy in copies:
        copy.start()
    copies[0].wait()
    count = rows.shape[0]
    padded = packed.shape[1]
    shift = leaves.bit_length() - 1
    here = position[...]
    window = jnp.right_shift(here, shift)
    copies[1].wait()
    values = rows[...]
    block = 256
    for low in range(0, count, block):
        ordered[low : low + block, :] = dot(hot(iota((block, count), 0) + low == window), values)
    ordered[count:, :] = jnp.zeros((padded, 128), F32)
    copies[2].wait()
    zero = jnp.zeros((1, count), I32)
    owner, first = zero, zero
    starts = [0]
    for c in range(leaves):
        starts.append(starts[-1] + jnp.right_shift(sizes[c], shift))
        beyond = window >= starts[-1]
        owner = owner + beyond.astype(I32)
        first = jnp.where(beyond, starts[-1], first)
    offset = jnp.bitwise_and(here, leaves - 1).astype(F32)
    picked = jnp.where(iota((leaves, count), 0) == owner, offset, 0.0).astype(BF16)
    offsets = dot(picked, hot(iota((128, count), 0) == window - first), (1, 1))
    places[...] = owner * bucket + window - first
    line = iota((padded, 128), 0)
    chunk = leaves // 8
    out = []
    for c in range(leaves):
        data = ordered[pl.ds(starts[c], padded), :]
        data = jnp.where(line < starts[c + 1] - starts[c], data, 0.0)
        data = jnp.where(line == bucket, offsets[c : c + 1, :], data)
        near[c] = data.astype(BF16)
        if c % chunk == chunk - 1:
            part = pl.ds(c + 1 - chunk, chunk)
            out.append(pltpu.make_async_copy(near.at[part], packed.at[part], out_sems.at[c // chunk]))
            out[-1].start()
    for copy in out:
        copy.wait()


def near_kernel(ranks, right_top_in, right_low_in, right, flags, sems):
    tops, parts, capacity, width = right_top_in.shape
    levels, _, rows, _ = right_low_in.shape
    pairs = []
    for level in range(tops):
        for p in range(parts):
            place = (pl.ds(p * capacity, capacity), pl.ds(level * width, width))
            pairs.append((right_top_in.at[level, p], right.at[place]))
    at = parts * capacity
    for low in range(0, capacity, 256):
        for p in range(parts):
            for level in range(levels):
                source = right_low_in.at[level, p, :, pl.ds(low, 256)]
                pairs.append((source, right.at[pl.ds(at, rows), :]))
                at += rows
    copies = [pltpu.make_async_copy(a, b, sems.at[i]) for i, (a, b) in enumerate(pairs)]
    for copy in copies:
        copy.start()
    row, lane = iota(flags.shape, 0), iota(flags.shape, 1)
    marks = jnp.where(row == 0, 1 - jnp.bitwise_and(lax.axis_index("member"), 1), 0)
    for level in range(1, tops + 1):
        counts = (lane < rank_of(ranks, level, tops + levels)).astype(I32)
        marks = jnp.where(row == level, counts, marks)
    for level in range(levels):
        inside = row - 8 - level * rows
        counts = (inside < rank_of(ranks, 1 + tops + level, tops + levels, 1)).astype(I32)
        marks = jnp.where(inside >= 0, counts, marks)
    flags[...] = marks.astype(F32)
    for copy in copies:
        copy.wait()


def way_kernel(targets, places, after, slots, order, upper):
    groups, part = targets.shape
    lanes = iota((part, 128), 1)
    for g in range(groups):
        target = jnp.transpose(jnp.broadcast_to(targets[g : g + 1, :], (128, part)))
        for low in range(0, part, 128):
            slots[g * part : (g + 1) * part, low : low + 128] = hot(target == lanes + low)
    count, folded = order.shape
    place = jnp.transpose(jnp.broadcast_to(places[...], (128, count)))
    beyond = place >= folded
    upper[...] = beyond.astype(I32)
    place = jnp.where(beyond, place - folded, place)
    block = 256
    lanes = iota((block, 128), 1)
    for low in range(0, count, block):
        for at in range(0, folded, 128):
            order[low : low + block, at : at + 128] = hot(place[low : low + block] == lanes + at)


def stage_kernel(first, left_top_in, left_low_in, block_in, pair, after, *rest):
    left_top, left_low, out, raw, block, sems = rest
    copies = [pltpu.make_async_copy(left_low_in, raw, sems.at[0])]
    count, _, height, _ = block.shape
    for j in range(count):
        rows = pl.ds((first + j) * height, height)
        copies.append(pltpu.make_async_copy(block_in.at[:, rows, :], block.at[j], sems.at[1 + j]))
    copies.append(pltpu.make_async_copy(left_top_in, left_top, sems.at[1 + count]))
    for copy in copies:
        copy.start()
    copies[0].wait()
    levels, parts, width, capacity = raw.shape
    left_low[...] = jnp.transpose(raw[...].reshape(levels * parts * width, capacity))
    for j in range(count):
        copies[1 + j].wait()
        out[j * height : (j + 1) * height, :] = dot(block[j, 0], pair[0]) + dot(block[j, 1], pair[1])
    copies[-1].wait()


def field_kernel(leaves, bucket, tops, levels, arrived, right, flags, *rest):
    pair, targets, send, keep, whole = rest
    capacity = leaves * bucket
    padded = arrived.shape[1]
    part = leaves * 8
    groups = targets.shape[0]
    core = jnp.bitwise_and(lax.axis_index("member"), 1)
    last = arrived[:, padded - 16 :, :].reshape(leaves * 16, 128)
    row = iota((leaves * 16, part), 0)
    spread = jnp.right_shift(iota((leaves * 16, part), 1), 3) * 16 + bucket % 16 == row
    spread_offsets = dot(last, hot(spread), (0, 0))[: groups * 8].reshape(groups, 8, part)
    lane_window = jnp.bitwise_and(iota((8, part), 1), 7)
    own = (lane_window == iota((8, part), 0))[None]
    target = jnp.sum(jnp.where(own, spread_offsets, 0.0), axis=1).astype(I32)
    target = target + lane_window[:1, :] * leaves
    targets[...] = target
    for g in range(groups):
        size = min(part, capacity - g * part)
        if g % 2 == 0:
            both = arrived[:, g * 8 : g * 8 + 16, :].astype(F32)
        chunk = both[:, g % 2 * 8 : g % 2 * 8 + 8, :].reshape(part, 128).astype(BF16)
        placed = dot(hot(iota((part, part), 0) == target[g : g + 1, :]), chunk)
        pair[0, g * part : g * part + size, :] = placed[:size].astype(BF16)
        pair[1, g * part : g * part + size, :] = turn(placed)[:size].astype(BF16)
    plain = jnp.transpose(pair[0])
    turned = jnp.concatenate([-plain[64:], plain[:64]], axis=0)
    upper = dot(plain, right[:capacity, :]) + dot(turned, right[capacity : 2 * capacity, :])
    top_rows = tops * 128
    for level in range(tops):
        whole[level * 128 : (level + 1) * 128, :] = upper[:, level * 128 : (level + 1) * 128]
    rows = whole.shape[0] - top_rows
    width = rows // levels
    lower = jnp.zeros((rows, 128), F32)
    at = 2 * capacity
    for low in range(0, capacity, 256):
        for p in range(2):
            lower += dot(right[at : at + rows, :], pair[p, low : low + 256, :])
            at += rows
    whole[top_rows:, :] = jnp.where(flags[8:, :] > 0, lower, 0.0)
    at = 0
    low = 0
    for half in [tops * 64] + [width // 2] * (levels - 1):
        mine = pl.multiple_of(low + core * half, 8)
        other = pl.multiple_of(low + (1 - core) * half, 8)
        keep[at : at + half, :] = whole[pl.ds(mine, half), :]
        send[at : at + half, :] = whole[pl.ds(other, half), :]
        at += half
        low += 2 * half
    send[at : at + width, :] = whole[whole.shape[0] - width :, :]
    power = []
    for low, high in [(level * 128, level * 128 + 128) for level in range(tops)] + [
        (top_rows + level * width, top_rows + (level + 1) * width) for level in range(levels - 1)
    ]:
        largest = jnp.max(jnp.abs(whole[low:high, :]), axis=0, keepdims=True)
        power.append(jnp.clip(jnp.ceil(jnp.log2(largest + 1e-30)) + 1.0, -100.0, 126.0))
    line = iota((8, 128), 0)
    shared = jnp.zeros((8, 128), F32)
    for i, row in enumerate(power[tops:]):
        shared = jnp.where(line == 1 + i, row, shared)
    send[at + width :, :] = jnp.where(line == 0, jnp.where(core == 0, power[1], power[0]), shared)
    keep[at:, :] = jnp.where(line == 0, jnp.where(core == 0, power[0], power[1]), shared)


def diag_kernel(first, block_in, pair, after, out, block, sems):
    count, _, height, _ = block.shape
    copies = []
    for j in range(count):
        rows = pl.ds((first + j) * height, height)
        copies.append(pltpu.make_async_copy(block_in.at[:, rows, :], block.at[j], sems.at[j]))
        copies[j].start()
    for j in range(count):
        copies[j].wait()
        out[j * height : (j + 1) * height, :] = dot(block[j, 0], pair[0]) + dot(block[j, 1], pair[1])


def merged(core, own, theirs, at, half):
    a, b = own[at : at + half, :].astype(F32), theirs[at : at + half, :].astype(F32)
    return jnp.concatenate([jnp.where(core == 0, a, b), jnp.where(core == 0, b, a)], axis=0)


def low_kernel(pieces, *rest):
    bases = rest[:pieces]
    left_low, nearest, own, theirs, out = rest[pieces:]
    width = nearest.shape[0]
    levels = left_low.shape[1] // (2 * width)
    core = jnp.bitwise_and(lax.axis_index("member"), 1)
    half = width // 2
    stacked = []
    for level in range(levels):
        if level < levels - 1:
            coef = merged(core, own, theirs, level * half, half)
        else:
            coef = nearest[...]
        stacked += [coef, turn(coef)]
    stacked = jnp.concatenate(stacked, axis=0).astype(BF16)
    low = 0
    for base in bases:
        rows = slice(low, low + base.shape[0])
        out[rows, :] = base[...] + dot(left_low[rows, :], stacked)
        low += base.shape[0]


def out_kernel(bucket, flags, base, left_top, own, theirs, slots, packed, spare, ordered):
    capacity = base.shape[0]
    part = slots.shape[1]
    groups = slots.shape[0] // part
    leaves = part // 8
    first = flags[:1, :] > 0
    levels = left_top.shape[0]
    half = own.shape[0]
    stacked = []
    for level in range(levels):
        pick = (own, theirs) if level == 0 else (theirs, own)
        coef = jnp.where(first, pick[0][...].astype(F32), pick[1][...].astype(F32))
        coef = jnp.where(flags[1 + level : 2 + level, :] > 0, coef, 0.0)
        turned = jnp.concatenate([-coef[half // 2 :], coef[: half // 2]], axis=0)
        stacked += [jnp.transpose(coef), jnp.transpose(turned)]
    stacked = jnp.concatenate(stacked, axis=0).astype(BF16)
    if groups * part > capacity:
        spare[capacity:, :] = jnp.zeros((groups * part - capacity, 128), BF16)
    factors = [left_top[level, p] for level in range(levels) for p in range(2)]
    total = base[...] + dot(jnp.concatenate(factors, axis=1), stacked)
    spare[:capacity, :] = total.astype(BF16)
    for g in range(groups):
        moved = dot(slots[g * part : (g + 1) * part, :], spare[g * part : (g + 1) * part, :])
        ordered[:, g * 8 : g * 8 + 8, :] = moved.reshape(leaves, 8, 128)
    packed[...] = ordered[:, :bucket, :].reshape(capacity, 128).astype(BF16)


def unpack_kernel(order, upper, returned, out, near, sems):
    count, folded = order.shape
    wide = jnp.concatenate([returned[:folded, :], returned[folded:, :]], axis=1)
    block = 256
    copies = []
    for low in range(0, count, block):
        rows = pl.ds(low, block)
        both = dot(order[low : low + block, :], wide)
        near[rows, :] = jnp.where(upper[low : low + block, :] != 0, both[:, 128:], both[:, :128])
        copies.append(pltpu.make_async_copy(near.at[rows, :], out.at[rows, :], sems.at[low // block]))
        copies[-1].start()
    for copy in copies:
        copy.wait()


def on_device(
    mesh_vector,
    cluster_position,
    cluster_sizes,
    block_ranks,
    diag_block,
    top_left,
    top_right,
    low_left,
    low_right,
):
    groups = lax.axis_size("group")
    members = lax.axis_size("member")
    leaves = groups * members
    group_levels = groups.bit_length() - 1
    member_levels = members.bit_length() - 1
    capacity = diag_block.shape[1]
    bucket = capacity // leaves
    padded = (bucket + 16) // 16 * 16
    filled = (bucket + 7) // 8 * 8
    count, columns = mesh_vector.shape
    everyone = ("group", "member")
    low_left = jnp.swapaxes(low_left, 2, 3)
    low_right = jnp.swapaxes(low_right, 2, 3)
    width = low_left.shape[2]
    top_width = top_left.shape[3]
    far_flops = 4 * capacity * columns * (group_levels * top_width + member_levels * width)

    packed, places = call(
        functools.partial(pack_kernel, leaves, bucket),
        [
            jax.ShapeDtypeStruct((leaves, padded, columns), BF16),
            jax.ShapeDtypeStruct((1, count), I32),
        ],
        [HBM] * 3,
        far(cluster_sizes, cluster_position.reshape(1, count), mesh_vector),
        2 * count * count * columns,
        4 << 20,
        16,
        out_specs=[HBM, VMEM],
        scratch=[
            pltpu.SMEM((leaves,), I32),
            pltpu.VMEM((1, count), I32),
            pltpu.VMEM((count, columns), BF16),
            pltpu.VMEM((count + padded, columns), F32),
            pltpu.VMEM((leaves, padded, columns), BF16),
            DMA((3,)),
            DMA((8,)),
        ],
    )
    arrived = lax.all_to_all(packed, everyone, split_axis=0, concat_axis=0, tiled=True)
    ranked = group_levels * top_width + member_levels * width
    right, flags = call(
        near_kernel,
        [
            pltpu.VMEM((2 * ranked * capacity // 256, 256), BF16),
            jax.ShapeDtypeStruct((8 + member_levels * width, columns), F32),
        ],
        [SMEM, HBM, HBM],
        (block_ranks, *far(top_right, low_right)),
        0,
        6 << 20,
        16,
        scratch=[DMA((2 * group_levels + 2 * member_levels * capacity // 256,))],
    )
    tops = group_levels * columns // 2
    shared = tops + (member_levels - 1) * width // 2
    pair, targets, send, keep = call(
        functools.partial(field_kernel, leaves, bucket, group_levels, member_levels),
        [
            jax.ShapeDtypeStruct((2, capacity, columns), BF16),
            jax.ShapeDtypeStruct((filled // 8, leaves * 8), I32),
            jax.ShapeDtypeStruct((shared + width + 8, columns), F32),
            jax.ShapeDtypeStruct((shared + 8, columns), F32),
        ],
        [VMEM] * 3,
        (arrived, right, flags),
        far_flops,
        6 << 20,
        24,
        scratch=[pltpu.VMEM((2 * shared + width, columns), F32)],
    )
    height = capacity // 8

    def diagonal(first, chunks, after):
        return call(
            functools.partial(diag_kernel, first),
            [jax.ShapeDtypeStruct((chunks * height, columns), F32)],
            [HBM, VMEM, pl.BlockSpec(memory_space=pl.ANY)],
            (*far(diag_block), pair, after),
            4 * chunks * height * capacity * columns,
            4 * chunks * height * capacity,
            24,
            scratch=[pltpu.VMEM((chunks, 2, height, capacity), BF16), DMA((chunks,))],
        )[0]

    received = partner(send, "member", 0)
    slots, order, upper = call(
        way_kernel,
        [
            jax.ShapeDtypeStruct((leaves * filled, leaves * 8), BF16),
            jax.ShapeDtypeStruct((count, capacity // 2), BF16),
            jax.ShapeDtypeStruct((count, 128), I32),
        ],
        [VMEM, VMEM, pl.BlockSpec(memory_space=pl.ANY)],
        (targets, places, send),
        0,
        8 << 20,
        16,
    )
    received, slots, order, upper = lax.optimization_barrier((received, slots, order, upper))
    nearest = received[shared : shared + width]
    running = keep[:shared] + received[:shared]
    power = bound(keep[shared:], received[shared + width :])
    heights = [columns] + [width // 2] * (member_levels - 1)
    bases = []
    coefs = []
    for bit in range(1, member_levels):
        rest = running.shape[0] - width // 2
        received = partner(narrow(running, power, heights), "member", bit)
        if bit == 1:
            bases.append(diagonal(0, 3, running))
            received, bases[0] = lax.optimization_barrier((received, bases[0]))
        if bit == member_levels - 1:
            bases.append(diagonal(3, 3, running))
            received, bases[1] = lax.optimization_barrier((received, bases[1]))
        received, other = widen(received, heights)
        power = bound(power, other)
        heights = heights[:-1]
        coefs.insert(0, received[rest:].astype(BF16))
        running = running[:rest] + received[:rest]
    routes = [[], []]
    for low in range(groups):
        for near in range(0, members, 2):
            at = low * members + near
            routes[0] += [(at, (low ^ 2) * members + near), (at + 1, (low ^ 1) * members + near + 1)]
            routes[1] += [(at, (low ^ 3) * members + near), (at + 1, low * members + (near ^ 2) + 1)]
    sums = narrow(running, power, heights)
    heard = [lax.ppermute(sums, everyone, route) for route in routes]
    left_top, left_low, last = call(
        functools.partial(stage_kernel, 6),
        [
            pltpu.VMEM(top_left.shape, BF16),
            pltpu.VMEM((capacity, member_levels * 2 * width), BF16),
            jax.ShapeDtypeStruct((2 * height, columns), F32),
        ],
        [HBM, HBM, HBM, VMEM, pl.BlockSpec(memory_space=pl.ANY)],
        (*far(top_left, low_left, diag_block), pair, running),
        8 * height * capacity * columns,
        12 << 20,
        24,
        scratch=[
            pltpu.VMEM(low_left.shape, BF16),
            pltpu.VMEM((2, 2, height, capacity), BF16),
            DMA((4,)),
        ],
    )
    bases.append(last)
    heard, left_top, left_low = lax.optimization_barrier((heard, left_top, left_low))
    heard = [widen(block, heights)[0] for block in heard]
    own = (heard[0] + jnp.where(flags[:1] > 0, heard[1], 0.0)).astype(BF16)
    own_low = jnp.concatenate(coefs)
    their_low, own = lax.optimization_barrier((partner(own_low, "member", 0), own))
    theirs = partner(own, "member", 0)
    base = call(
        functools.partial(low_kernel, len(bases)),
        [jax.ShapeDtypeStruct((capacity, columns), F32)],
        [VMEM] * (len(bases) + 4),
        (*bases, left_low, nearest, own_low, their_low),
        4 * capacity * columns * member_levels * width,
        3 << 20,
        16,
    )[0]

    leaving = call(
        functools.partial(out_kernel, bucket),
        [jax.ShapeDtypeStruct((capacity, columns), BF16)],
        [VMEM] * 6,
        (flags, base, left_top, own, theirs, slots),
        4 * capacity * columns * group_levels * top_width,
        4 << 20,
        24,
        scratch=[
            pltpu.VMEM((leaves * filled, 128), BF16),
            pltpu.VMEM((leaves, filled, 128), F32),
        ],
    )[0]
    returned = lax.all_to_all(
        leaving.reshape(leaves, bucket, columns), everyone, split_axis=0, concat_axis=0, tiled=True
    )
    return call(
        unpack_kernel,
        [jax.ShapeDtypeStruct((count, columns), F32)],
        [VMEM] * 3,
        (order, upper, returned.reshape(capacity, columns)),
        2 * capacity * count * columns,
        4 << 20,
        16,
        out_specs=[HBM],
        scratch=[pltpu.VMEM((count, 128), F32), DMA((count // 256,))],
    )[0]


def solution(mesh):
    return jax.shard_map(
        on_device,
        mesh=mesh,
        in_specs=(
            P(("group", "member"), None),
            P(("group", "member")),
            P(),
            P(),
            P(None, ("group", "member"), None),
            P(None, None, ("group", "member"), None),
            P(None, None, ("group", "member"), None),
            P(None, None, ("group", "member"), None),
            P(None, None, ("group", "member"), None),
        ),
        out_specs=P(("group", "member"), None),
        check_vma=False,
    )
```

```python
import functools

import jax
import jax.numpy as jnp
from jax import lax
from jax.experimental import pallas as pl
from jax.experimental.pallas import tpu as pltpu
from jax.sharding import PartitionSpec as P

F32 = jnp.float32
BF16 = jnp.bfloat16
F16 = jnp.float16
I32 = jnp.int32
VMEM = pl.BlockSpec(memory_space=pltpu.VMEM)
SMEM = pl.BlockSpec(memory_space=pltpu.SMEM)
HBM = pl.BlockSpec(memory_space=pltpu.HBM)
DMA = pltpu.SemaphoreType.DMA


def iota(shape, dim):
    return lax.broadcasted_iota(I32, shape, dim)


def hot(mask):
    return jnp.where(mask, 1.0, 0.0).astype(BF16)


def dot(a, b, over=(1, 0)):
    return lax.dot_general(
        a, b, (((over[0],), (over[1],)), ((), ())), preferred_element_type=F32
    )


def call(kernel, outs, ins, args, flops, moved, limit, scratch=(), **more):
    return pl.pallas_call(
        kernel,
        out_shape=outs,
        in_specs=ins,
        out_specs=more.pop("out_specs", [VMEM] * len(outs)),
        scratch_shapes=scratch,
        cost_estimate=pl.CostEstimate(flops=flops, bytes_accessed=moved, transcendentals=0),
        compiler_params=pltpu.CompilerParams(vmem_limit_bytes=limit << 20),
        **more,
    )(*args)


def partner(block, axis, apart):
    count = lax.axis_size(axis)
    route = []
    for low in range(count):
        high = low | 1 << apart
        if high != low and high < count:
            route += [(low, high), (high, low)]
    return lax.ppermute(block, axis, route)


def far(*arrays):
    return [pltpu.with_memory_space_constraint(array, pltpu.HBM) for array in arrays]


def bound(mine, other):
    return jnp.clip(jnp.maximum(mine, other) + 1.0, -100.0, 126.0)


def stretch(power, heights):
    parts = [jnp.broadcast_to(power[i : i + 1], (h, power.shape[1])) for i, h in enumerate(heights)]
    return jnp.concatenate(parts)


def narrow(rows, power, heights):
    return jnp.concatenate([rows * jnp.exp2(14.0 - stretch(power, heights)), power]).astype(F16)


def widen(sent, heights):
    power = sent[-8:].astype(F32)
    return sent[:-8].astype(F32) * jnp.exp2(stretch(power, heights) - 14.0), power


def turn(block):
    half = block.shape[1] // 2
    return jnp.where(iota(block.shape, 1) < half, -1.0, 1.0) * pltpu.roll(block, half, 1)


def rank_of(ranks, level, levels, other=0):
    device = lax.axis_index("group") * lax.axis_size("member") + lax.axis_index("member")
    node = jnp.bitwise_xor(jnp.right_shift(device, levels - level), other)
    return ranks[(1 << level) - 2 + node]


def pack_kernel(leaves, bucket, sizes_in, position_in, rows_in, packed, places, *scratch):
    sizes, position, rows, ordered, near, sems, out_sems = scratch
    copies = [
        pltpu.make_async_copy(source, target, sems.at[i])
        for i, (source, target) in enumerate(
            [(position_in, position), (rows_in, rows), (sizes_in, sizes)]
        )
    ]
    for copy in copies:
        copy.start()
    copies[0].wait()
    count = rows.shape[0]
    padded = packed.shape[1]
    shift = leaves.bit_length() - 1
    here = position[...]
    window = jnp.right_shift(here, shift)
    copies[1].wait()
    values = rows[...]
    block = 256
    for low in range(0, count, block):
        ordered[low : low + block, :] = dot(hot(iota((block, count), 0) + low == window), values)
    ordered[count:, :] = jnp.zeros((padded, 128), F32)
    copies[2].wait()
    zero = jnp.zeros((1, count), I32)
    owner, first = zero, zero
    starts = [0]
    for c in range(leaves):
        starts.append(starts[-1] + jnp.right_shift(sizes[c], shift))
        beyond = window >= starts[-1]
        owner = owner + beyond.astype(I32)
        first = jnp.where(beyond, starts[-1], first)
    offset = jnp.bitwise_and(here, leaves - 1).astype(F32)
    picked = jnp.where(iota((leaves, count), 0) == owner, offset, 0.0).astype(BF16)
    offsets = dot(picked, hot(iota((128, count), 0) == window - first), (1, 1))
    places[...] = owner * bucket + window - first
    line = iota((padded, 128), 0)
    chunk = leaves // 8
    out = []
    for c in range(leaves):
        data = ordered[pl.ds(starts[c], padded), :]
        data = jnp.where(line < starts[c + 1] - starts[c], data, 0.0)
        data = jnp.where(line == bucket, offsets[c : c + 1, :], data)
        near[c] = data.astype(BF16)
        if c % chunk == chunk - 1:
            part = pl.ds(c + 1 - chunk, chunk)
            out.append(pltpu.make_async_copy(near.at[part], packed.at[part], out_sems.at[c // chunk]))
            out[-1].start()
    for copy in out:
        copy.wait()


def near_kernel(ranks, right_top_in, right_low_in, right, flags, sems):
    tops, parts, capacity, width = right_top_in.shape
    levels, _, rows, _ = right_low_in.shape
    pairs = []
    for level in range(tops):
        for p in range(parts):
            place = (pl.ds(p * capacity, capacity), pl.ds(level * width, width))
            pairs.append((right_top_in.at[level, p], right.at[place]))
    at = parts * capacity
    for low in range(0, capacity, 256):
        for p in range(parts):
            for level in range(levels):
                source = right_low_in.at[level, p, :, pl.ds(low, 256)]
                pairs.append((source, right.at[pl.ds(at, rows), :]))
                at += rows
    copies = [pltpu.make_async_copy(a, b, sems.at[i]) for i, (a, b) in enumerate(pairs)]
    for copy in copies:
        copy.start()
    row, lane = iota(flags.shape, 0), iota(flags.shape, 1)
    marks = jnp.where(row == 0, 1 - jnp.bitwise_and(lax.axis_index("member"), 1), 0)
    for level in range(1, tops + 1):
        counts = (lane < rank_of(ranks, level, tops + levels)).astype(I32)
        marks = jnp.where(row == level, counts, marks)
    for level in range(levels):
        inside = row - 8 - level * rows
        counts = (inside < rank_of(ranks, 1 + tops + level, tops + levels, 1)).astype(I32)
        marks = jnp.where(inside >= 0, counts, marks)
    flags[...] = marks.astype(F32)
    for copy in copies:
        copy.wait()


def way_kernel(targets, places, after, slots, order, upper):
    groups, part = targets.shape
    lanes = iota((part, 128), 1)
    for g in range(groups):
        target = jnp.transpose(jnp.broadcast_to(targets[g : g + 1, :], (128, part)))
        for low in range(0, part, 128):
            slots[g * part : (g + 1) * part, low : low + 128] = hot(target == lanes + low)
    count, folded = order.shape
    place = jnp.transpose(jnp.broadcast_to(places[...], (128, count)))
    beyond = place >= folded
    upper[...] = beyond.astype(I32)
    place = jnp.where(beyond, place - folded, place)
    block = 256
    lanes = iota((block, 128), 1)
    for low in range(0, count, block):
        for at in range(0, folded, 128):
            order[low : low + block, at : at + 128] = hot(place[low : low + block] == lanes + at)


def stage_kernel(first, left_top_in, left_low_in, block_in, pair, after, *rest):
    left_top, left_low, out, raw, block, sems = rest
    copies = [pltpu.make_async_copy(left_low_in, raw, sems.at[0])]
    count, _, height, _ = block.shape
    for j in range(count):
        rows = pl.ds((first + j) * height, height)
        copies.append(pltpu.make_async_copy(block_in.at[:, rows, :], block.at[j], sems.at[1 + j]))
    copies.append(pltpu.make_async_copy(left_top_in, left_top, sems.at[1 + count]))
    for copy in copies:
        copy.start()
    copies[0].wait()
    levels, parts, width, capacity = raw.shape
    left_low[...] = jnp.transpose(raw[...].reshape(levels * parts * width, capacity))
    for j in range(count):
        copies[1 + j].wait()
        out[j * height : (j + 1) * height, :] = dot(block[j, 0], pair[0]) + dot(block[j, 1], pair[1])
    copies[-1].wait()


def field_kernel(leaves, bucket, tops, levels, arrived, right, flags, *rest):
    pair, targets, send, keep, whole = rest
    capacity = leaves * bucket
    padded = arrived.shape[1]
    part = leaves * 8
    groups = targets.shape[0]
    core = jnp.bitwise_and(lax.axis_index("member"), 1)
    last = arrived[:, padded - 16 :, :].reshape(leaves * 16, 128)
    row = iota((leaves * 16, part), 0)
    spread = jnp.right_shift(iota((leaves * 16, part), 1), 3) * 16 + bucket % 16 == row
    spread_offsets = dot(last, hot(spread), (0, 0))[: groups * 8].reshape(groups, 8, part)
    lane_window = jnp.bitwise_and(iota((8, part), 1), 7)
    own = (lane_window == iota((8, part), 0))[None]
    target = jnp.sum(jnp.where(own, spread_offsets, 0.0), axis=1).astype(I32)
    target = target + lane_window[:1, :] * leaves
    targets[...] = target
    for g in range(groups):
        size = min(part, capacity - g * part)
        if g % 2 == 0:
            both = arrived[:, g * 8 : g * 8 + 16, :].astype(F32)
        chunk = both[:, g % 2 * 8 : g % 2 * 8 + 8, :].reshape(part, 128).astype(BF16)
        placed = dot(hot(iota((part, part), 0) == target[g : g + 1, :]), chunk)
        pair[0, g * part : g * part + size, :] = placed[:size].astype(BF16)
        pair[1, g * part : g * part + size, :] = turn(placed)[:size].astype(BF16)
    plain = jnp.transpose(pair[0])
    turned = jnp.concatenate([-plain[64:], plain[:64]], axis=0)
    upper = dot(plain, right[:capacity, :]) + dot(turned, right[capacity : 2 * capacity, :])
    top_rows = tops * 128
    for level in range(tops):
        whole[level * 128 : (level + 1) * 128, :] = upper[:, level * 128 : (level + 1) * 128]
    rows = whole.shape[0] - top_rows
    width = rows // levels
    lower = jnp.zeros((rows, 128), F32)
    at = 2 * capacity
    for low in range(0, capacity, 256):
        for p in range(2):
            lower += dot(right[at : at + rows, :], pair[p, low : low + 256, :])
            at += rows
    whole[top_rows:, :] = jnp.where(flags[8:, :] > 0, lower, 0.0)
    at = 0
    low = 0
    for half in [tops * 64] + [width // 2] * (levels - 1):
        mine = pl.multiple_of(low + core * half, 8)
        other = pl.multiple_of(low + (1 - core) * half, 8)
        keep[at : at + half, :] = whole[pl.ds(mine, half), :]
        send[at : at + half, :] = whole[pl.ds(other, half), :]
        at += half
        low += 2 * half
    send[at : at + width, :] = whole[whole.shape[0] - width :, :]
    power = []
    for low, high in [(level * 128, level * 128 + 128) for level in range(tops)] + [
        (top_rows + level * width, top_rows + (level + 1) * width) for level in range(levels - 1)
    ]:
        largest = jnp.max(jnp.abs(whole[low:high, :]), axis=0, keepdims=True)
        power.append(jnp.clip(jnp.ceil(jnp.log2(largest + 1e-30)) + 1.0, -100.0, 126.0))
    line = iota((8, 128), 0)
    shared = jnp.zeros((8, 128), F32)
    for i, row in enumerate(power[tops:]):
        shared = jnp.where(line == 1 + i, row, shared)
    send[at + width :, :] = jnp.where(line == 0, jnp.where(core == 0, power[1], power[0]), shared)
    keep[at:, :] = jnp.where(line == 0, jnp.where(core == 0, power[0], power[1]), shared)


def diag_kernel(first, block_in, pair, after, out, block, sems):
    count, _, height, _ = block.shape
    copies = []
    for j in range(count):
        rows = pl.ds((first + j) * height, height)
        copies.append(pltpu.make_async_copy(block_in.at[:, rows, :], block.at[j], sems.at[j]))
        copies[j].start()
    for j in range(count):
        copies[j].wait()
        out[j * height : (j + 1) * height, :] = dot(block[j, 0], pair[0]) + dot(block[j, 1], pair[1])


def merged(core, own, theirs, at, half):
    a, b = own[at : at + half, :].astype(F32), theirs[at : at + half, :].astype(F32)
    return jnp.concatenate([jnp.where(core == 0, a, b), jnp.where(core == 0, b, a)], axis=0)


def low_kernel(pieces, *rest):
    bases = rest[:pieces]
    left_low, nearest, own, theirs, out = rest[pieces:]
    width = nearest.shape[0]
    levels = left_low.shape[1] // (2 * width)
    core = jnp.bitwise_and(lax.axis_index("member"), 1)
    half = width // 2
    stacked = []
    for level in range(levels):
        if level < levels - 1:
            coef = merged(core, own, theirs, level * half, half)
        else:
            coef = nearest[...]
        stacked += [coef, turn(coef)]
    stacked = jnp.concatenate(stacked, axis=0).astype(BF16)
    low = 0
    for base in bases:
        rows = slice(low, low + base.shape[0])
        out[rows, :] = base[...] + dot(left_low[rows, :], stacked)
        low += base.shape[0]


def out_kernel(bucket, flags, base, left_top, own, theirs, slots, packed, spare, ordered):
    capacity = base.shape[0]
    part = slots.shape[1]
    groups = slots.shape[0] // part
    leaves = part // 8
    first = flags[:1, :] > 0
    levels = left_top.shape[0]
    half = own.shape[0]
    stacked = []
    for level in range(levels):
        pick = (own, theirs) if level == 0 else (theirs, own)
        coef = jnp.where(first, pick[0][...].astype(F32), pick[1][...].astype(F32))
        coef = jnp.where(flags[1 + level : 2 + level, :] > 0, coef, 0.0)
        turned = jnp.concatenate([-coef[half // 2 :], coef[: half // 2]], axis=0)
        stacked += [jnp.transpose(coef), jnp.transpose(turned)]
    stacked = jnp.concatenate(stacked, axis=0).astype(BF16)
    if groups * part > capacity:
        spare[capacity:, :] = jnp.zeros((groups * part - capacity, 128), BF16)
    factors = [left_top[level, p] for level in range(levels) for p in range(2)]
    total = base[...] + dot(jnp.concatenate(factors, axis=1), stacked)
    spare[:capacity, :] = total.astype(BF16)
    for g in range(groups):
        moved = dot(slots[g * part : (g + 1) * part, :], spare[g * part : (g + 1) * part, :])
        ordered[:, g * 8 : g * 8 + 8, :] = moved.reshape(leaves, 8, 128)
    packed[...] = ordered[:, :bucket, :].reshape(capacity, 128).astype(BF16)


def unpack_kernel(order, upper, returned, out, near, sems):
    count, folded = order.shape
    wide = jnp.concatenate([returned[:folded, :], returned[folded:, :]], axis=1)
    block = 256
    copies = []
    for low in range(0, count, block):
        rows = pl.ds(low, block)
        both = dot(order[low : low + block, :], wide)
        near[rows, :] = jnp.where(upper[low : low + block, :] != 0, both[:, 128:], both[:, :128])
        copies.append(pltpu.make_async_copy(near.at[rows, :], out.at[rows, :], sems.at[low // block]))
        copies[-1].start()
    for copy in copies:
        copy.wait()


def on_device(
    mesh_vector,
    cluster_position,
    cluster_sizes,
    block_ranks,
    diag_block,
    top_left,
    top_right,
    low_left,
    low_right,
):
    groups = lax.axis_size("group")
    members = lax.axis_size("member")
    leaves = groups * members
    group_levels = groups.bit_length() - 1
    member_levels = members.bit_length() - 1
    capacity = diag_block.shape[1]
    bucket = capacity // leaves
    padded = (bucket + 16) // 16 * 16
    filled = (bucket + 7) // 8 * 8
    count, columns = mesh_vector.shape
    everyone = ("group", "member")
    low_left = jnp.swapaxes(low_left, 2, 3)
    low_right = jnp.swapaxes(low_right, 2, 3)
    width = low_left.shape[2]
    top_width = top_left.shape[3]
    far_flops = 4 * capacity * columns * (group_levels * top_width + member_levels * width)

    packed, places = call(
        functools.partial(pack_kernel, leaves, bucket),
        [
            jax.ShapeDtypeStruct((leaves, padded, columns), BF16),
            jax.ShapeDtypeStruct((1, count), I32),
        ],
        [HBM] * 3,
        far(cluster_sizes, cluster_position.reshape(1, count), mesh_vector),
        2 * count * count * columns,
        4 << 20,
        16,
        out_specs=[HBM, VMEM],
        scratch=[
            pltpu.SMEM((leaves,), I32),
            pltpu.VMEM((1, count), I32),
            pltpu.VMEM((count, columns), BF16),
            pltpu.VMEM((count + padded, columns), F32),
            pltpu.VMEM((leaves, padded, columns), BF16),
            DMA((3,)),
            DMA((8,)),
        ],
    )
    arrived = lax.all_to_all(packed, everyone, split_axis=0, concat_axis=0, tiled=True)
    ranked = group_levels * top_width + member_levels * width
    right, flags = call(
        near_kernel,
        [
            pltpu.VMEM((2 * ranked * capacity // 256, 256), BF16),
            jax.ShapeDtypeStruct((8 + member_levels * width, columns), F32),
        ],
        [SMEM, HBM, HBM],
        (block_ranks, *far(top_right, low_right)),
        0,
        6 << 20,
        16,
        scratch=[DMA((2 * group_levels + 2 * member_levels * capacity // 256,))],
    )
    tops = group_levels * columns // 2
    shared = tops + (member_levels - 1) * width // 2
    pair, targets, send, keep = call(
        functools.partial(field_kernel, leaves, bucket, group_levels, member_levels),
        [
            jax.ShapeDtypeStruct((2, capacity, columns), BF16),
            jax.ShapeDtypeStruct((filled // 8, leaves * 8), I32),
            jax.ShapeDtypeStruct((shared + width + 8, columns), F32),
            jax.ShapeDtypeStruct((shared + 8, columns), F32),
        ],
        [VMEM] * 3,
        (arrived, right, flags),
        far_flops,
        6 << 20,
        24,
        scratch=[pltpu.VMEM((2 * shared + width, columns), F32)],
    )
    height = capacity // 8

    def diagonal(first, chunks, after):
        return call(
            functools.partial(diag_kernel, first),
            [jax.ShapeDtypeStruct((chunks * height, columns), F32)],
            [HBM, VMEM, pl.BlockSpec(memory_space=pl.ANY)],
            (*far(diag_block), pair, after),
            4 * chunks * height * capacity * columns,
            4 * chunks * height * capacity,
            24,
            scratch=[pltpu.VMEM((chunks, 2, height, capacity), BF16), DMA((chunks,))],
        )[0]

    received = partner(send, "member", 0)
    slots, order, upper = call(
        way_kernel,
        [
            jax.ShapeDtypeStruct((leaves * filled, leaves * 8), BF16),
            jax.ShapeDtypeStruct((count, capacity // 2), BF16),
            jax.ShapeDtypeStruct((count, 128), I32),
        ],
        [VMEM, VMEM, pl.BlockSpec(memory_space=pl.ANY)],
        (targets, places, send),
        0,
        8 << 20,
        16,
    )
    received, slots, order, upper = lax.optimization_barrier((received, slots, order, upper))
    nearest = received[shared : shared + width]
    running = keep[:shared] + received[:shared]
    power = bound(keep[shared:], received[shared + width :])
    heights = [columns] + [width // 2] * (member_levels - 1)
    bases = []
    coefs = []
    for bit in range(1, member_levels):
        rest = running.shape[0] - width // 2
        received = partner(narrow(running, power, heights), "member", bit)
        if bit == 1:
            bases.append(diagonal(0, 3, running))
            received, bases[0] = lax.optimization_barrier((received, bases[0]))
        if bit == member_levels - 1:
            bases.append(diagonal(3, 3, running))
            received, bases[1] = lax.optimization_barrier((received, bases[1]))
        received, other = widen(received, heights)
        power = bound(power, other)
        heights = heights[:-1]
        coefs.insert(0, received[rest:].astype(BF16))
        running = running[:rest] + received[:rest]
    own_low = jnp.concatenate(coefs)
    their_low = partner(own_low, "member", 0)
    routes = [[], []]
    for low in range(groups):
        for near in range(0, members, 2):
            at = low * members + near
            routes[0] += [(at, (low ^ 2) * members + near), (at + 1, (low ^ 1) * members + near + 1)]
            routes[1] += [(at, (low ^ 3) * members + near), (at + 1, low * members + (near ^ 2) + 1)]
    sums = narrow(running, power, heights)
    heard = [lax.ppermute(sums, everyone, route) for route in routes]
    left_top, left_low, last = call(
        functools.partial(stage_kernel, 6),
        [
            pltpu.VMEM(top_left.shape, BF16),
            pltpu.VMEM((capacity, member_levels * 2 * width), BF16),
            jax.ShapeDtypeStruct((2 * height, columns), F32),
        ],
        [HBM, HBM, HBM, VMEM, pl.BlockSpec(memory_space=pl.ANY)],
        (*far(top_left, low_left, diag_block), pair, their_low),
        8 * height * capacity * columns,
        12 << 20,
        24,
        scratch=[
            pltpu.VMEM(low_left.shape, BF16),
            pltpu.VMEM((2, 2, height, capacity), BF16),
            DMA((4,)),
        ],
    )
    bases.append(last)
    heard, left_top, left_low = lax.optimization_barrier((heard, left_top, left_low))
    heard = [widen(block, heights)[0] for block in heard]
    own = (heard[0] + jnp.where(flags[:1] > 0, heard[1], 0.0)).astype(BF16)
    their_low, own = lax.optimization_barrier((their_low, own))
    theirs = partner(own, "member", 0)
    base = call(
        functools.partial(low_kernel, len(bases)),
        [jax.ShapeDtypeStruct((capacity, columns), F32)],
        [VMEM] * (len(bases) + 4),
        (*bases, left_low, nearest, own_low, their_low),
        4 * capacity * columns * member_levels * width,
        3 << 20,
        16,
    )[0]

    leaving = call(
        functools.partial(out_kernel, bucket),
        [jax.ShapeDtypeStruct((capacity, columns), BF16)],
        [VMEM] * 6,
        (flags, base, left_top, own, theirs, slots),
        4 * capacity * columns * group_levels * top_width,
        4 << 20,
        24,
        scratch=[
            pltpu.VMEM((leaves * filled, 128), BF16),
            pltpu.VMEM((leaves, filled, 128), F32),
        ],
    )[0]
    returned = lax.all_to_all(
        leaving.reshape(leaves, bucket, columns), everyone, split_axis=0, concat_axis=0, tiled=True
    )
    return call(
        unpack_kernel,
        [jax.ShapeDtypeStruct((count, columns), F32)],
        [VMEM] * 3,
        (order, upper, returned.reshape(capacity, columns)),
        2 * capacity * count * columns,
        4 << 20,
        16,
        out_specs=[HBM],
        scratch=[pltpu.VMEM((count, 128), F32), DMA((count // 256,))],
    )[0]


def solution(mesh):
    return jax.shard_map(
        on_device,
        mesh=mesh,
        in_specs=(
            P(("group", "member"), None),
            P(("group", "member")),
            P(),
            P(),
            P(None, ("group", "member"), None),
            P(None, None, ("group", "member"), None),
            P(None, None, ("group", "member"), None),
            P(None, None, ("group", "member"), None),
            P(None, None, ("group", "member"), None),
        ),
        out_specs=P(("group", "member"), None),
        check_vma=False,
    )
```

```python
import functools

import jax
import jax.numpy as jnp
from jax import lax
from jax.experimental import pallas as pl
from jax.experimental.pallas import tpu as pltpu
from jax.sharding import PartitionSpec as P

F32 = jnp.float32
BF16 = jnp.bfloat16
F16 = jnp.float16
I32 = jnp.int32
VMEM = pl.BlockSpec(memory_space=pltpu.VMEM)
SMEM = pl.BlockSpec(memory_space=pltpu.SMEM)
HBM = pl.BlockSpec(memory_space=pltpu.HBM)
DMA = pltpu.SemaphoreType.DMA


def iota(shape, dim):
    return lax.broadcasted_iota(I32, shape, dim)


def hot(mask):
    return jnp.where(mask, 1.0, 0.0).astype(BF16)


def dot(a, b, over=(1, 0)):
    return lax.dot_general(
        a, b, (((over[0],), (over[1],)), ((), ())), preferred_element_type=F32
    )


def call(kernel, outs, ins, args, flops, moved, limit, scratch=(), **more):
    return pl.pallas_call(
        kernel,
        out_shape=outs,
        in_specs=ins,
        out_specs=more.pop("out_specs", [VMEM] * len(outs)),
        scratch_shapes=scratch,
        cost_estimate=pl.CostEstimate(flops=flops, bytes_accessed=moved, transcendentals=0),
        compiler_params=pltpu.CompilerParams(vmem_limit_bytes=limit << 20),
        **more,
    )(*args)


def partner(block, axis, apart):
    count = lax.axis_size(axis)
    route = []
    for low in range(count):
        high = low | 1 << apart
        if high != low and high < count:
            route += [(low, high), (high, low)]
    return lax.ppermute(block, axis, route)


def far(*arrays):
    return [pltpu.with_memory_space_constraint(array, pltpu.HBM) for array in arrays]


def bound(mine, other):
    return jnp.clip(jnp.maximum(mine, other) + 1.0, -100.0, 126.0)


def stretch(power, heights):
    parts = [jnp.broadcast_to(power[i : i + 1], (h, power.shape[1])) for i, h in enumerate(heights)]
    return jnp.concatenate(parts)


def narrow(rows, power, heights):
    return jnp.concatenate([rows * jnp.exp2(14.0 - stretch(power, heights)), power]).astype(F16)


def widen(sent, heights):
    power = sent[-8:].astype(F32)
    return sent[:-8].astype(F32) * jnp.exp2(stretch(power, heights) - 14.0), power


def turn(block):
    half = block.shape[1] // 2
    return jnp.where(iota(block.shape, 1) < half, -1.0, 1.0) * pltpu.roll(block, half, 1)


def rank_of(ranks, level, levels, other=0):
    device = lax.axis_index("group") * lax.axis_size("member") + lax.axis_index("member")
    node = jnp.bitwise_xor(jnp.right_shift(device, levels - level), other)
    return ranks[(1 << level) - 2 + node]


def pack_kernel(leaves, bucket, sizes_in, position_in, rows_in, packed, places, *scratch):
    sizes, position, rows, ordered, near, sems, out_sems = scratch
    copies = [
        pltpu.make_async_copy(source, target, sems.at[i])
        for i, (source, target) in enumerate(
            [(position_in, position), (rows_in, rows), (sizes_in, sizes)]
        )
    ]
    for copy in copies:
        copy.start()
    copies[0].wait()
    count = rows.shape[0]
    padded = packed.shape[1]
    shift = leaves.bit_length() - 1
    here = position[...]
    window = jnp.right_shift(here, shift)
    copies[1].wait()
    values = rows[...]
    block = 256
    for low in range(0, count, block):
        ordered[low : low + block, :] = dot(hot(iota((block, count), 0) + low == window), values)
    ordered[count:, :] = jnp.zeros((padded, 128), F32)
    copies[2].wait()
    zero = jnp.zeros((1, count), I32)
    owner, first = zero, zero
    starts = [0]
    for c in range(leaves):
        starts.append(starts[-1] + jnp.right_shift(sizes[c], shift))
        beyond = window >= starts[-1]
        owner = owner + beyond.astype(I32)
        first = jnp.where(beyond, starts[-1], first)
    offset = jnp.bitwise_and(here, leaves - 1).astype(F32)
    picked = jnp.where(iota((leaves, count), 0) == owner, offset, 0.0).astype(BF16)
    offsets = dot(picked, hot(iota((128, count), 0) == window - first), (1, 1))
    places[...] = owner * bucket + window - first
    line = iota((padded, 128), 0)
    chunk = leaves // 8
    out = []
    for c in range(leaves):
        data = ordered[pl.ds(starts[c], padded), :]
        data = jnp.where(line < starts[c + 1] - starts[c], data, 0.0)
        data = jnp.where(line == bucket, offsets[c : c + 1, :], data)
        near[c] = data.astype(BF16)
        if c % chunk == chunk - 1:
            part = pl.ds(c + 1 - chunk, chunk)
            out.append(pltpu.make_async_copy(near.at[part], packed.at[part], out_sems.at[c // chunk]))
            out[-1].start()
    for copy in out:
        copy.wait()


def near_kernel(ranks, right_top_in, right_low_in, right, flags, sems):
    tops, parts, capacity, width = right_top_in.shape
    levels, _, rows, _ = right_low_in.shape
    pairs = []
    for level in range(tops):
        for p in range(parts):
            place = (pl.ds(p * capacity, capacity), pl.ds(level * width, width))
            pairs.append((right_top_in.at[level, p], right.at[place]))
    at = parts * capacity
    for low in range(0, capacity, 256):
        for p in range(parts):
            for level in range(levels):
                source = right_low_in.at[level, p, :, pl.ds(low, 256)]
                pairs.append((source, right.at[pl.ds(at, rows), :]))
                at += rows
    copies = [pltpu.make_async_copy(a, b, sems.at[i]) for i, (a, b) in enumerate(pairs)]
    for copy in copies:
        copy.start()
    row, lane = iota(flags.shape, 0), iota(flags.shape, 1)
    marks = jnp.where(row == 0, 1 - jnp.bitwise_and(lax.axis_index("member"), 1), 0)
    for level in range(1, tops + 1):
        counts = (lane < rank_of(ranks, level, tops + levels)).astype(I32)
        marks = jnp.where(row == level, counts, marks)
    for level in range(levels):
        inside = row - 8 - level * rows
        counts = (inside < rank_of(ranks, 1 + tops + level, tops + levels, 1)).astype(I32)
        marks = jnp.where(inside >= 0, counts, marks)
    flags[...] = marks.astype(F32)
    for copy in copies:
        copy.wait()


def way_kernel(targets, places, after, slots, order, upper):
    groups, part = targets.shape
    lanes = iota((part, 128), 1)
    for g in range(groups):
        target = jnp.transpose(jnp.broadcast_to(targets[g : g + 1, :], (128, part)))
        for low in range(0, part, 128):
            slots[g * part : (g + 1) * part, low : low + 128] = hot(target == lanes + low)
    count, folded = order.shape
    place = jnp.transpose(jnp.broadcast_to(places[...], (128, count)))
    beyond = place >= folded
    upper[...] = beyond.astype(I32)
    place = jnp.where(beyond, place - folded, place)
    block = 256
    lanes = iota((block, 128), 1)
    for low in range(0, count, block):
        for at in range(0, folded, 128):
            order[low : low + block, at : at + 128] = hot(place[low : low + block] == lanes + at)


def stage_kernel(first, left_top_in, left_low_in, block_in, pair, after, *rest):
    left_top, left_low, out, raw, block, sems = rest
    copies = [pltpu.make_async_copy(left_low_in, raw, sems.at[0])]
    count, _, height, _ = block.shape
    for j in range(count):
        rows = pl.ds((first + j) * height, height)
        copies.append(pltpu.make_async_copy(block_in.at[:, rows, :], block.at[j], sems.at[1 + j]))
    copies.append(pltpu.make_async_copy(left_top_in, left_top, sems.at[1 + count]))
    for copy in copies:
        copy.start()
    copies[0].wait()
    levels, parts, width, capacity = raw.shape
    left_low[...] = jnp.transpose(raw[...].reshape(levels * parts * width, capacity))
    for j in range(count):
        copies[1 + j].wait()
        out[j * height : (j + 1) * height, :] = dot(block[j, 0], pair[0]) + dot(block[j, 1], pair[1])
    copies[-1].wait()


def field_kernel(leaves, bucket, tops, levels, arrived, right, flags, *rest):
    pair, targets, send, keep, whole = rest
    capacity = leaves * bucket
    padded = arrived.shape[1]
    part = leaves * 8
    groups = targets.shape[0]
    core = jnp.bitwise_and(lax.axis_index("member"), 1)
    last = arrived[:, padded - 16 :, :].reshape(leaves * 16, 128)
    row = iota((leaves * 16, part), 0)
    spread = jnp.right_shift(iota((leaves * 16, part), 1), 3) * 16 + bucket % 16 == row
    spread_offsets = dot(last, hot(spread), (0, 0))[: groups * 8].reshape(groups, 8, part)
    lane_window = jnp.bitwise_and(iota((8, part), 1), 7)
    own = (lane_window == iota((8, part), 0))[None]
    target = jnp.sum(jnp.where(own, spread_offsets, 0.0), axis=1).astype(I32)
    target = target + lane_window[:1, :] * leaves
    targets[...] = target
    for g in range(groups):
        size = min(part, capacity - g * part)
        if g % 2 == 0:
            both = arrived[:, g * 8 : g * 8 + 16, :].astype(F32)
        chunk = both[:, g % 2 * 8 : g % 2 * 8 + 8, :].reshape(part, 128).astype(BF16)
        placed = dot(hot(iota((part, part), 0) == target[g : g + 1, :]), chunk)
        pair[0, g * part : g * part + size, :] = placed[:size].astype(BF16)
        pair[1, g * part : g * part + size, :] = turn(placed)[:size].astype(BF16)
    plain = jnp.transpose(pair[0])
    turned = jnp.concatenate([-plain[64:], plain[:64]], axis=0)
    upper = dot(plain, right[:capacity, :]) + dot(turned, right[capacity : 2 * capacity, :])
    top_rows = tops * 128
    for level in range(tops):
        whole[level * 128 : (level + 1) * 128, :] = upper[:, level * 128 : (level + 1) * 128]
    rows = whole.shape[0] - top_rows
    width = rows // levels
    lower = jnp.zeros((rows, 128), F32)
    at = 2 * capacity
    for low in range(0, capacity, 256):
        for p in range(2):
            lower += dot(right[at : at + rows, :], pair[p, low : low + 256, :])
            at += rows
    whole[top_rows:, :] = jnp.where(flags[8:, :] > 0, lower, 0.0)
    at = 0
    low = 0
    for half in [tops * 64] + [width // 2] * (levels - 1):
        mine = pl.multiple_of(low + core * half, 8)
        other = pl.multiple_of(low + (1 - core) * half, 8)
        keep[at : at + half, :] = whole[pl.ds(mine, half), :]
        send[at : at + half, :] = whole[pl.ds(other, half), :]
        at += half
        low += 2 * half
    send[at : at + width, :] = whole[whole.shape[0] - width :, :]
    power = []
    for low, high in [(level * 128, level * 128 + 128) for level in range(tops)] + [
        (top_rows + level * width, top_rows + (level + 1) * width) for level in range(levels - 1)
    ]:
        largest = jnp.max(jnp.abs(whole[low:high, :]), axis=0, keepdims=True)
        power.append(jnp.clip(jnp.ceil(jnp.log2(largest + 1e-30)) + 1.0, -100.0, 126.0))
    line = iota((8, 128), 0)
    shared = jnp.zeros((8, 128), F32)
    for i, row in enumerate(power[tops:]):
        shared = jnp.where(line == 1 + i, row, shared)
    send[at + width :, :] = jnp.where(line == 0, jnp.where(core == 0, power[1], power[0]), shared)
    keep[at:, :] = jnp.where(line == 0, jnp.where(core == 0, power[0], power[1]), shared)


def diag_kernel(first, block_in, pair, after, out, block, sems):
    count, _, height, _ = block.shape
    copies = []
    for j in range(count):
        rows = pl.ds((first + j) * height, height)
        copies.append(pltpu.make_async_copy(block_in.at[:, rows, :], block.at[j], sems.at[j]))
        copies[j].start()
    for j in range(count):
        copies[j].wait()
        out[j * height : (j + 1) * height, :] = dot(block[j, 0], pair[0]) + dot(block[j, 1], pair[1])


def merged(core, own, theirs, at, half):
    a, b = own[at : at + half, :].astype(F32), theirs[at : at + half, :].astype(F32)
    return jnp.concatenate([jnp.where(core == 0, a, b), jnp.where(core == 0, b, a)], axis=0)


def low_kernel(pieces, *rest):
    bases = rest[:pieces]
    left_low, nearest, own, theirs, out = rest[pieces:]
    width = nearest.shape[0]
    levels = left_low.shape[1] // (2 * width)
    core = jnp.bitwise_and(lax.axis_index("member"), 1)
    half = width // 2
    stacked = []
    for level in range(levels):
        if level < levels - 1:
            coef = merged(core, own, theirs, level * half, half)
        else:
            coef = nearest[...]
        stacked += [coef, turn(coef)]
    stacked = jnp.concatenate(stacked, axis=0).astype(BF16)
    low = 0
    for base in bases:
        rows = slice(low, low + base.shape[0])
        out[rows, :] = base[...] + dot(left_low[rows, :], stacked)
        low += base.shape[0]


def out_kernel(bucket, flags, base, left_top, own, theirs, slots, packed, spare, ordered):
    capacity = base.shape[0]
    part = slots.shape[1]
    groups = slots.shape[0] // part
    leaves = part // 8
    first = flags[:1, :] > 0
    levels = left_top.shape[0]
    half = own.shape[0]
    stacked = []
    for level in range(levels):
        pick = (own, theirs) if level == 0 else (theirs, own)
        coef = jnp.where(first, pick[0][...].astype(F32), pick[1][...].astype(F32))
        coef = jnp.where(flags[1 + level : 2 + level, :] > 0, coef, 0.0)
        turned = jnp.concatenate([-coef[half // 2 :], coef[: half // 2]], axis=0)
        stacked += [jnp.transpose(coef), jnp.transpose(turned)]
    stacked = jnp.concatenate(stacked, axis=0).astype(BF16)
    if groups * part > capacity:
        spare[capacity:, :] = jnp.zeros((groups * part - capacity, 128), BF16)
    factors = [left_top[level, p] for level in range(levels) for p in range(2)]
    total = base[...] + dot(jnp.concatenate(factors, axis=1), stacked)
    spare[:capacity, :] = total.astype(BF16)
    for g in range(groups):
        moved = dot(slots[g * part : (g + 1) * part, :], spare[g * part : (g + 1) * part, :])
        ordered[:, g * 8 : g * 8 + 8, :] = moved.reshape(leaves, 8, 128)
    packed[...] = ordered[:, :bucket, :].reshape(capacity, 128).astype(BF16)


def unpack_kernel(order, upper, returned, out, near, sems):
    count, folded = order.shape
    wide = jnp.concatenate([returned[:folded, :], returned[folded:, :]], axis=1)
    block = 256
    copies = []
    for low in range(0, count, block):
        rows = pl.ds(low, block)
        both = dot(order[low : low + block, :], wide)
        near[rows, :] = jnp.where(upper[low : low + block, :] != 0, both[:, 128:], both[:, :128])
        copies.append(pltpu.make_async_copy(near.at[rows, :], out.at[rows, :], sems.at[low // block]))
        copies[-1].start()
    for copy in copies:
        copy.wait()


def on_device(
    mesh_vector,
    cluster_position,
    cluster_sizes,
    block_ranks,
    diag_block,
    top_left,
    top_right,
    low_left,
    low_right,
):
    groups = lax.axis_size("group")
    members = lax.axis_size("member")
    leaves = groups * members
    group_levels = groups.bit_length() - 1
    member_levels = members.bit_length() - 1
    capacity = diag_block.shape[1]
    bucket = capacity // leaves
    padded = (bucket + 16) // 16 * 16
    filled = (bucket + 7) // 8 * 8
    count, columns = mesh_vector.shape
    everyone = ("group", "member")
    low_left = jnp.swapaxes(low_left, 2, 3)
    low_right = jnp.swapaxes(low_right, 2, 3)
    width = low_left.shape[2]
    top_width = top_left.shape[3]
    far_flops = 4 * capacity * columns * (group_levels * top_width + member_levels * width)

    packed, places = call(
        functools.partial(pack_kernel, leaves, bucket),
        [
            jax.ShapeDtypeStruct((leaves, padded, columns), BF16),
            jax.ShapeDtypeStruct((1, count), I32),
        ],
        [HBM] * 3,
        far(cluster_sizes, cluster_position.reshape(1, count), mesh_vector),
        2 * count * count * columns,
        4 << 20,
        16,
        out_specs=[HBM, VMEM],
        scratch=[
            pltpu.SMEM((leaves,), I32),
            pltpu.VMEM((1, count), I32),
            pltpu.VMEM((count, columns), BF16),
            pltpu.VMEM((count + padded, columns), F32),
            pltpu.VMEM((leaves, padded, columns), BF16),
            DMA((3,)),
            DMA((8,)),
        ],
    )
    arrived = lax.all_to_all(packed, everyone, split_axis=0, concat_axis=0, tiled=True)
    ranked = group_levels * top_width + member_levels * width
    right, flags = call(
        near_kernel,
        [
            pltpu.VMEM((2 * ranked * capacity // 256, 256), BF16),
            jax.ShapeDtypeStruct((8 + member_levels * width, columns), F32),
        ],
        [SMEM, HBM, HBM],
        (block_ranks, *far(top_right, low_right)),
        0,
        6 << 20,
        16,
        scratch=[DMA((2 * group_levels + 2 * member_levels * capacity // 256,))],
    )
    tops = group_levels * columns // 2
    shared = tops + (member_levels - 1) * width // 2
    pair, targets, send, keep = call(
        functools.partial(field_kernel, leaves, bucket, group_levels, member_levels),
        [
            jax.ShapeDtypeStruct((2, capacity, columns), BF16),
            jax.ShapeDtypeStruct((filled // 8, leaves * 8), I32),
            jax.ShapeDtypeStruct((shared + width + 8, columns), F32),
            jax.ShapeDtypeStruct((shared + 8, columns), F32),
        ],
        [VMEM] * 3,
        (arrived, right, flags),
        far_flops,
        6 << 20,
        24,
        scratch=[pltpu.VMEM((2 * shared + width, columns), F32)],
    )
    height = capacity // 8

    def diagonal(first, chunks, after):
        return call(
            functools.partial(diag_kernel, first),
            [jax.ShapeDtypeStruct((chunks * height, columns), F32)],
            [HBM, VMEM, pl.BlockSpec(memory_space=pl.ANY)],
            (*far(diag_block), pair, after),
            4 * chunks * height * capacity * columns,
            4 * chunks * height * capacity,
            24,
            scratch=[pltpu.VMEM((chunks, 2, height, capacity), BF16), DMA((chunks,))],
        )[0]

    received = partner(send, "member", 0)
    slots, order, upper = call(
        way_kernel,
        [
            jax.ShapeDtypeStruct((leaves * filled, leaves * 8), BF16),
            jax.ShapeDtypeStruct((count, capacity // 2), BF16),
            jax.ShapeDtypeStruct((count, 128), I32),
        ],
        [VMEM, VMEM, pl.BlockSpec(memory_space=pl.ANY)],
        (targets, places, send),
        0,
        8 << 20,
        16,
    )
    received, slots, order, upper = lax.optimization_barrier((received, slots, order, upper))
    nearest = received[shared : shared + width]
    running = keep[:shared] + received[:shared]
    power = bound(keep[shared:], received[shared + width :])
    heights = [columns] + [width // 2] * (member_levels - 1)
    bases = []
    coefs = []
    for bit in range(1, member_levels):
        rest = running.shape[0] - width // 2
        received = partner(narrow(running, power, heights), "member", bit)
        if bit == 1:
            bases.append(diagonal(0, 3, running))
            received, bases[0] = lax.optimization_barrier((received, bases[0]))
        if bit == member_levels - 1:
            bases.append(diagonal(3, 4, running))
            received, bases[1] = lax.optimization_barrier((received, bases[1]))
        received, other = widen(received, heights)
        power = bound(power, other)
        heights = heights[:-1]
        coefs.insert(0, received[rest:].astype(BF16))
        running = running[:rest] + received[:rest]
    own_low = jnp.concatenate(coefs)
    their_low = partner(own_low, "member", 0)
    routes = [[], []]
    for low in range(groups):
        for near in range(0, members, 2):
            at = low * members + near
            routes[0] += [(at, (low ^ 2) * members + near), (at + 1, (low ^ 1) * members + near + 1)]
            routes[1] += [(at, (low ^ 3) * members + near), (at + 1, low * members + (near ^ 2) + 1)]
    sums = narrow(running, power, heights)
    heard = [lax.ppermute(sums, everyone, route) for route in routes]
    left_top, left_low, last = call(
        functools.partial(stage_kernel, 7),
        [
            pltpu.VMEM(top_left.shape, BF16),
            pltpu.VMEM((capacity, member_levels * 2 * width), BF16),
            jax.ShapeDtypeStruct((height, columns), F32),
        ],
        [HBM, HBM, HBM, VMEM, pl.BlockSpec(memory_space=pl.ANY)],
        (*far(top_left, low_left, diag_block), pair, their_low),
        4 * height * capacity * columns,
        10 << 20,
        24,
        scratch=[
            pltpu.VMEM(low_left.shape, BF16),
            pltpu.VMEM((1, 2, height, capacity), BF16),
            DMA((3,)),
        ],
    )
    bases.append(last)
    heard, left_top, left_low = lax.optimization_barrier((heard, left_top, left_low))
    heard = [widen(block, heights)[0] for block in heard]
    own = (heard[0] + jnp.where(flags[:1] > 0, heard[1], 0.0)).astype(BF16)
    their_low, own = lax.optimization_barrier((their_low, own))
    theirs = partner(own, "member", 0)
    base = call(
        functools.partial(low_kernel, len(bases)),
        [jax.ShapeDtypeStruct((capacity, columns), F32)],
        [VMEM] * (len(bases) + 4),
        (*bases, left_low, nearest, own_low, their_low),
        4 * capacity * columns * member_levels * width,
        3 << 20,
        16,
    )[0]

    leaving = call(
        functools.partial(out_kernel, bucket),
        [jax.ShapeDtypeStruct((capacity, columns), BF16)],
        [VMEM] * 6,
        (flags, base, left_top, own, theirs, slots),
        4 * capacity * columns * group_levels * top_width,
        4 << 20,
        24,
        scratch=[
            pltpu.VMEM((leaves * filled, 128), BF16),
            pltpu.VMEM((leaves, filled, 128), F32),
        ],
    )[0]
    returned = lax.all_to_all(
        leaving.reshape(leaves, bucket, columns), everyone, split_axis=0, concat_axis=0, tiled=True
    )
    return call(
        unpack_kernel,
        [jax.ShapeDtypeStruct((count, columns), F32)],
        [VMEM] * 3,
        (order, upper, returned.reshape(capacity, columns)),
        2 * capacity * count * columns,
        4 << 20,
        16,
        out_specs=[HBM],
        scratch=[pltpu.VMEM((count, 128), F32), DMA((count // 256,))],
    )[0]


def solution(mesh):
    return jax.shard_map(
        on_device,
        mesh=mesh,
        in_specs=(
            P(("group", "member"), None),
            P(("group", "member")),
            P(),
            P(),
            P(None, ("group", "member"), None),
            P(None, None, ("group", "member"), None),
            P(None, None, ("group", "member"), None),
            P(None, None, ("group", "member"), None),
            P(None, None, ("group", "member"), None),
        ),
        out_specs=P(("group", "member"), None),
        check_vma=False,
    )
```

```python
import functools

import jax
import jax.numpy as jnp
from jax import lax
from jax.experimental import pallas as pl
from jax.experimental.pallas import tpu as pltpu
from jax.sharding import PartitionSpec as P

F32 = jnp.float32
BF16 = jnp.bfloat16
F16 = jnp.float16
I32 = jnp.int32
VMEM = pl.BlockSpec(memory_space=pltpu.VMEM)
SMEM = pl.BlockSpec(memory_space=pltpu.SMEM)
HBM = pl.BlockSpec(memory_space=pltpu.HBM)
DMA = pltpu.SemaphoreType.DMA


def iota(shape, dim):
    return lax.broadcasted_iota(I32, shape, dim)


def hot(mask):
    return jnp.where(mask, 1.0, 0.0).astype(BF16)


def dot(a, b, over=(1, 0)):
    return lax.dot_general(
        a, b, (((over[0],), (over[1],)), ((), ())), preferred_element_type=F32
    )


def call(kernel, outs, ins, args, flops, moved, limit, scratch=(), **more):
    return pl.pallas_call(
        kernel,
        out_shape=outs,
        in_specs=ins,
        out_specs=more.pop("out_specs", [VMEM] * len(outs)),
        scratch_shapes=scratch,
        cost_estimate=pl.CostEstimate(flops=flops, bytes_accessed=moved, transcendentals=0),
        compiler_params=pltpu.CompilerParams(vmem_limit_bytes=limit << 20),
        **more,
    )(*args)


def partner(block, axis, apart):
    count = lax.axis_size(axis)
    route = []
    for low in range(count):
        high = low | 1 << apart
        if high != low and high < count:
            route += [(low, high), (high, low)]
    return lax.ppermute(block, axis, route)


def far(*arrays):
    return [pltpu.with_memory_space_constraint(array, pltpu.HBM) for array in arrays]


def bound(mine, other):
    return jnp.clip(jnp.maximum(mine, other) + 1.0, -100.0, 126.0)


def stretch(power, heights):
    parts = [jnp.broadcast_to(power[i : i + 1], (h, power.shape[1])) for i, h in enumerate(heights)]
    return jnp.concatenate(parts)


def narrow(rows, power, heights):
    return jnp.concatenate([rows * jnp.exp2(14.0 - stretch(power, heights)), power]).astype(F16)


def widen(sent, heights):
    power = sent[-8:].astype(F32)
    return sent[:-8].astype(F32) * jnp.exp2(stretch(power, heights) - 14.0), power


def turn(block):
    half = block.shape[1] // 2
    return jnp.where(iota(block.shape, 1) < half, -1.0, 1.0) * pltpu.roll(block, half, 1)


def rank_of(ranks, level, levels, other=0):
    device = lax.axis_index("group") * lax.axis_size("member") + lax.axis_index("member")
    node = jnp.bitwise_xor(jnp.right_shift(device, levels - level), other)
    return ranks[(1 << level) - 2 + node]


def pack_kernel(leaves, bucket, sizes_in, position_in, rows_in, packed, places, *scratch):
    sizes, position, rows, ordered, near, sems, out_sems = scratch
    copies = [
        pltpu.make_async_copy(source, target, sems.at[i])
        for i, (source, target) in enumerate(
            [(position_in, position), (rows_in, rows), (sizes_in, sizes)]
        )
    ]
    for copy in copies:
        copy.start()
    copies[0].wait()
    count = rows.shape[0]
    padded = packed.shape[1]
    shift = leaves.bit_length() - 1
    here = position[...]
    window = jnp.right_shift(here, shift)
    copies[1].wait()
    values = rows[...]
    block = 256
    for low in range(0, count, block):
        ordered[low : low + block, :] = dot(hot(iota((block, count), 0) + low == window), values)
    ordered[count:, :] = jnp.zeros((padded, 128), F32)
    copies[2].wait()
    zero = jnp.zeros((1, count), I32)
    owner, first = zero, zero
    starts = [0]
    for c in range(leaves):
        starts.append(starts[-1] + jnp.right_shift(sizes[c], shift))
        beyond = window >= starts[-1]
        owner = owner + beyond.astype(I32)
        first = jnp.where(beyond, starts[-1], first)
    offset = jnp.bitwise_and(here, leaves - 1).astype(F32)
    picked = jnp.where(iota((leaves, count), 0) == owner, offset, 0.0).astype(BF16)
    offsets = dot(picked, hot(iota((128, count), 0) == window - first), (1, 1))
    places[...] = owner * bucket + window - first
    line = iota((padded, 128), 0)
    chunk = leaves // 8
    out = []
    for c in range(leaves):
        data = ordered[pl.ds(starts[c], padded), :]
        data = jnp.where(line < starts[c + 1] - starts[c], data, 0.0)
        data = jnp.where(line == bucket, offsets[c : c + 1, :], data)
        near[c] = data.astype(BF16)
        if c % chunk == chunk - 1:
            part = pl.ds(c + 1 - chunk, chunk)
            out.append(pltpu.make_async_copy(near.at[part], packed.at[part], out_sems.at[c // chunk]))
            out[-1].start()
    for copy in out:
        copy.wait()


def near_kernel(ranks, right_top_in, right_low_in, right, flags, sems):
    tops, parts, capacity, width = right_top_in.shape
    levels, _, rows, _ = right_low_in.shape
    pairs = []
    for level in range(tops):
        for p in range(parts):
            place = (pl.ds(p * capacity, capacity), pl.ds(level * width, width))
            pairs.append((right_top_in.at[level, p], right.at[place]))
    at = parts * capacity
    for low in range(0, capacity, 256):
        for p in range(parts):
            for level in range(levels):
                source = right_low_in.at[level, p, :, pl.ds(low, 256)]
                pairs.append((source, right.at[pl.ds(at, rows), :]))
                at += rows
    copies = [pltpu.make_async_copy(a, b, sems.at[i]) for i, (a, b) in enumerate(pairs)]
    for copy in copies:
        copy.start()
    row, lane = iota(flags.shape, 0), iota(flags.shape, 1)
    marks = jnp.where(row == 0, 1 - jnp.bitwise_and(lax.axis_index("member"), 1), 0)
    for level in range(1, tops + 1):
        counts = (lane < rank_of(ranks, level, tops + levels)).astype(I32)
        marks = jnp.where(row == level, counts, marks)
    for level in range(levels):
        inside = row - 8 - level * rows
        counts = (inside < rank_of(ranks, 1 + tops + level, tops + levels, 1)).astype(I32)
        marks = jnp.where(inside >= 0, counts, marks)
    flags[...] = marks.astype(F32)
    for copy in copies:
        copy.wait()


def way_kernel(targets, places, after, slots, order, upper):
    groups, part = targets.shape
    lanes = iota((part, 128), 1)
    for g in range(groups):
        target = jnp.transpose(jnp.broadcast_to(targets[g : g + 1, :], (128, part)))
        for low in range(0, part, 128):
            slots[g * part : (g + 1) * part, low : low + 128] = hot(target == lanes + low)
    count, folded = order.shape
    place = jnp.transpose(jnp.broadcast_to(places[...], (128, count)))
    beyond = place >= folded
    upper[...] = beyond.astype(I32)
    place = jnp.where(beyond, place - folded, place)
    block = 256
    lanes = iota((block, 128), 1)
    for low in range(0, count, block):
        for at in range(0, folded, 128):
            order[low : low + block, at : at + 128] = hot(place[low : low + block] == lanes + at)


def stage_kernel(first, left_top_in, left_low_in, block_in, pair, after, *rest):
    left_top, left_low, out, raw, block, sems = rest
    copies = [pltpu.make_async_copy(left_low_in, raw, sems.at[0])]
    count, _, height, _ = block.shape
    for j in range(count):
        rows = pl.ds((first + j) * height, height)
        copies.append(pltpu.make_async_copy(block_in.at[:, rows, :], block.at[j], sems.at[1 + j]))
    copies.append(pltpu.make_async_copy(left_top_in, left_top, sems.at[1 + count]))
    for copy in copies:
        copy.start()
    copies[0].wait()
    levels, parts, width, capacity = raw.shape
    left_low[...] = jnp.transpose(raw[...].reshape(levels * parts * width, capacity))
    for j in range(count):
        copies[1 + j].wait()
        out[j * height : (j + 1) * height, :] = dot(block[j, 0], pair[0]) + dot(block[j, 1], pair[1])
    copies[-1].wait()


def field_kernel(leaves, bucket, tops, levels, arrived, right, flags, *rest):
    pair, targets, send, keep, whole = rest
    capacity = leaves * bucket
    padded = arrived.shape[1]
    part = leaves * 8
    groups = targets.shape[0]
    core = jnp.bitwise_and(lax.axis_index("member"), 1)
    last = arrived[:, padded - 16 :, :].reshape(leaves * 16, 128)
    row = iota((leaves * 16, part), 0)
    spread = jnp.right_shift(iota((leaves * 16, part), 1), 3) * 16 + bucket % 16 == row
    spread_offsets = dot(last, hot(spread), (0, 0))[: groups * 8].reshape(groups, 8, part)
    lane_window = jnp.bitwise_and(iota((8, part), 1), 7)
    own = (lane_window == iota((8, part), 0))[None]
    target = jnp.sum(jnp.where(own, spread_offsets, 0.0), axis=1).astype(I32)
    target = target + lane_window[:1, :] * leaves
    targets[...] = target
    for g in range(groups):
        size = min(part, capacity - g * part)
        if g % 2 == 0:
            both = arrived[:, g * 8 : g * 8 + 16, :].astype(F32)
        chunk = both[:, g % 2 * 8 : g % 2 * 8 + 8, :].reshape(part, 128).astype(BF16)
        placed = dot(hot(iota((part, part), 0) == target[g : g + 1, :]), chunk)
        pair[0, g * part : g * part + size, :] = placed[:size].astype(BF16)
        pair[1, g * part : g * part + size, :] = turn(placed)[:size].astype(BF16)
    plain = jnp.transpose(pair[0])
    turned = jnp.concatenate([-plain[64:], plain[:64]], axis=0)
    upper = dot(plain, right[:capacity, :]) + dot(turned, right[capacity : 2 * capacity, :])
    top_rows = tops * 128
    for level in range(tops):
        whole[level * 128 : (level + 1) * 128, :] = upper[:, level * 128 : (level + 1) * 128]
    rows = whole.shape[0] - top_rows
    width = rows // levels
    lower = jnp.zeros((rows, 128), F32)
    at = 2 * capacity
    for low in range(0, capacity, 256):
        for p in range(2):
            lower += dot(right[at : at + rows, :], pair[p, low : low + 256, :])
            at += rows
    whole[top_rows:, :] = jnp.where(flags[8:, :] > 0, lower, 0.0)
    at = 0
    low = 0
    for half in [tops * 64] + [width // 2] * (levels - 1):
        mine = pl.multiple_of(low + core * half, 8)
        other = pl.multiple_of(low + (1 - core) * half, 8)
        keep[at : at + half, :] = whole[pl.ds(mine, half), :]
        send[at : at + half, :] = whole[pl.ds(other, half), :]
        at += half
        low += 2 * half
    send[at : at + width, :] = whole[whole.shape[0] - width :, :]
    power = []
    for low, high in [(level * 128, level * 128 + 128) for level in range(tops)] + [
        (top_rows + level * width, top_rows + (level + 1) * width) for level in range(levels - 1)
    ]:
        largest = jnp.max(jnp.abs(whole[low:high, :]), axis=0, keepdims=True)
        power.append(jnp.clip(jnp.ceil(jnp.log2(largest + 1e-30)) + 1.0, -100.0, 126.0))
    line = iota((8, 128), 0)
    shared = jnp.zeros((8, 128), F32)
    for i, row in enumerate(power[tops:]):
        shared = jnp.where(line == 1 + i, row, shared)
    send[at + width :, :] = jnp.where(line == 0, jnp.where(core == 0, power[1], power[0]), shared)
    keep[at:, :] = jnp.where(line == 0, jnp.where(core == 0, power[0], power[1]), shared)


def diag_kernel(first, block_in, pair, after, out, block, sems):
    count, _, height, _ = block.shape
    copies = []
    for j in range(count):
        rows = pl.ds((first + j) * height, height)
        for p in range(2):
            source = block_in.at[p, rows, :]
            copies.append(pltpu.make_async_copy(source, block.at[j, p], sems.at[2 * j + p]))
            copies[-1].start()
    for j in range(count):
        copies[2 * j].wait()
        real = dot(block[j, 0], pair[0])
        copies[2 * j + 1].wait()
        out[j * height : (j + 1) * height, :] = real + dot(block[j, 1], pair[1])


def merged(core, own, theirs, at, half):
    a, b = own[at : at + half, :].astype(F32), theirs[at : at + half, :].astype(F32)
    return jnp.concatenate([jnp.where(core == 0, a, b), jnp.where(core == 0, b, a)], axis=0)


def low_kernel(pieces, *rest):
    bases = rest[:pieces]
    left_low, nearest, own, theirs, out = rest[pieces:]
    width = nearest.shape[0]
    levels = left_low.shape[1] // (2 * width)
    core = jnp.bitwise_and(lax.axis_index("member"), 1)
    half = width // 2
    stacked = []
    for level in range(levels):
        if level < levels - 1:
            coef = merged(core, own, theirs, level * half, half)
        else:
            coef = nearest[...]
        stacked += [coef, turn(coef)]
    stacked = jnp.concatenate(stacked, axis=0).astype(BF16)
    low = 0
    for base in bases:
        rows = slice(low, low + base.shape[0])
        out[rows, :] = base[...] + dot(left_low[rows, :], stacked)
        low += base.shape[0]


def out_kernel(bucket, flags, base, left_top, own, theirs, slots, packed, spare, ordered):
    capacity = base.shape[0]
    part = slots.shape[1]
    groups = slots.shape[0] // part
    leaves = part // 8
    first = flags[:1, :] > 0
    levels = left_top.shape[0]
    half = own.shape[0]
    stacked = []
    for level in range(levels):
        pick = (own, theirs) if level == 0 else (theirs, own)
        coef = jnp.where(first, pick[0][...].astype(F32), pick[1][...].astype(F32))
        coef = jnp.where(flags[1 + level : 2 + level, :] > 0, coef, 0.0)
        turned = jnp.concatenate([-coef[half // 2 :], coef[: half // 2]], axis=0)
        stacked += [jnp.transpose(coef), jnp.transpose(turned)]
    stacked = jnp.concatenate(stacked, axis=0).astype(BF16)
    if groups * part > capacity:
        spare[capacity:, :] = jnp.zeros((groups * part - capacity, 128), BF16)
    factors = [left_top[level, p] for level in range(levels) for p in range(2)]
    total = base[...] + dot(jnp.concatenate(factors, axis=1), stacked)
    spare[:capacity, :] = total.astype(BF16)
    for g in range(groups):
        moved = dot(slots[g * part : (g + 1) * part, :], spare[g * part : (g + 1) * part, :])
        ordered[:, g * 8 : g * 8 + 8, :] = moved.reshape(leaves, 8, 128)
    packed[...] = ordered[:, :bucket, :].reshape(capacity, 128).astype(BF16)


def unpack_kernel(order, upper, returned, out, near, sems):
    count, folded = order.shape
    wide = jnp.concatenate([returned[:folded, :], returned[folded:, :]], axis=1)
    block = 256
    copies = []
    for low in range(0, count, block):
        rows = pl.ds(low, block)
        both = dot(order[low : low + block, :], wide)
        near[rows, :] = jnp.where(upper[low : low + block, :] != 0, both[:, 128:], both[:, :128])
        copies.append(pltpu.make_async_copy(near.at[rows, :], out.at[rows, :], sems.at[low // block]))
        copies[-1].start()
    for copy in copies:
        copy.wait()


def on_device(
    mesh_vector,
    cluster_position,
    cluster_sizes,
    block_ranks,
    diag_block,
    top_left,
    top_right,
    low_left,
    low_right,
):
    groups = lax.axis_size("group")
    members = lax.axis_size("member")
    leaves = groups * members
    group_levels = groups.bit_length() - 1
    member_levels = members.bit_length() - 1
    capacity = diag_block.shape[1]
    bucket = capacity // leaves
    padded = (bucket + 16) // 16 * 16
    filled = (bucket + 7) // 8 * 8
    count, columns = mesh_vector.shape
    everyone = ("group", "member")
    low_left = jnp.swapaxes(low_left, 2, 3)
    low_right = jnp.swapaxes(low_right, 2, 3)
    width = low_left.shape[2]
    top_width = top_left.shape[3]
    far_flops = 4 * capacity * columns * (group_levels * top_width + member_levels * width)

    packed, places = call(
        functools.partial(pack_kernel, leaves, bucket),
        [
            jax.ShapeDtypeStruct((leaves, padded, columns), BF16),
            jax.ShapeDtypeStruct((1, count), I32),
        ],
        [HBM] * 3,
        far(cluster_sizes, cluster_position.reshape(1, count), mesh_vector),
        2 * count * count * columns,
        4 << 20,
        16,
        out_specs=[HBM, VMEM],
        scratch=[
            pltpu.SMEM((leaves,), I32),
            pltpu.VMEM((1, count), I32),
            pltpu.VMEM((count, columns), BF16),
            pltpu.VMEM((count + padded, columns), F32),
            pltpu.VMEM((leaves, padded, columns), BF16),
            DMA((3,)),
            DMA((8,)),
        ],
    )
    arrived = lax.all_to_all(packed, everyone, split_axis=0, concat_axis=0, tiled=True)
    ranked = group_levels * top_width + member_levels * width
    right, flags = call(
        near_kernel,
        [
            pltpu.VMEM((2 * ranked * capacity // 256, 256), BF16),
            jax.ShapeDtypeStruct((8 + member_levels * width, columns), F32),
        ],
        [SMEM, HBM, HBM],
        (block_ranks, *far(top_right, low_right)),
        0,
        6 << 20,
        16,
        scratch=[DMA((2 * group_levels + 2 * member_levels * capacity // 256,))],
    )
    tops = group_levels * columns // 2
    shared = tops + (member_levels - 1) * width // 2
    pair, targets, send, keep = call(
        functools.partial(field_kernel, leaves, bucket, group_levels, member_levels),
        [
            jax.ShapeDtypeStruct((2, capacity, columns), BF16),
            jax.ShapeDtypeStruct((filled // 8, leaves * 8), I32),
            jax.ShapeDtypeStruct((shared + width + 8, columns), F32),
            jax.ShapeDtypeStruct((shared + 8, columns), F32),
        ],
        [VMEM] * 3,
        (arrived, right, flags),
        far_flops,
        6 << 20,
        24,
        scratch=[pltpu.VMEM((2 * shared + width, columns), F32)],
    )
    height = capacity // 8

    def diagonal(first, chunks, after):
        return call(
            functools.partial(diag_kernel, first),
            [jax.ShapeDtypeStruct((chunks * height, columns), F32)],
            [HBM, VMEM, pl.BlockSpec(memory_space=pl.ANY)],
            (*far(diag_block), pair, after),
            4 * chunks * height * capacity * columns,
            4 * chunks * height * capacity,
            24,
            scratch=[pltpu.VMEM((chunks, 2, height, capacity), BF16), DMA((2 * chunks,))],
        )[0]

    received = partner(send, "member", 0)
    slots, order, upper = call(
        way_kernel,
        [
            jax.ShapeDtypeStruct((leaves * filled, leaves * 8), BF16),
            jax.ShapeDtypeStruct((count, capacity // 2), BF16),
            jax.ShapeDtypeStruct((count, 128), I32),
        ],
        [VMEM, VMEM, pl.BlockSpec(memory_space=pl.ANY)],
        (targets, places, send),
        0,
        8 << 20,
        16,
    )
    received, slots, order, upper = lax.optimization_barrier((received, slots, order, upper))
    nearest = received[shared : shared + width]
    running = keep[:shared] + received[:shared]
    power = bound(keep[shared:], received[shared + width :])
    heights = [columns] + [width // 2] * (member_levels - 1)
    bases = []
    coefs = []
    for bit in range(1, member_levels):
        rest = running.shape[0] - width // 2
        received = partner(narrow(running, power, heights), "member", bit)
        if bit == 1:
            bases.append(diagonal(0, 3, running))
            received, bases[0] = lax.optimization_barrier((received, bases[0]))
        if bit == member_levels - 1:
            bases.append(diagonal(3, 3, running))
            received, bases[1] = lax.optimization_barrier((received, bases[1]))
        received, other = widen(received, heights)
        power = bound(power, other)
        heights = heights[:-1]
        coefs.insert(0, received[rest:].astype(BF16))
        running = running[:rest] + received[:rest]
    routes = [[], []]
    for low in range(groups):
        for near in range(0, members, 2):
            at = low * members + near
            routes[0] += [(at, (low ^ 2) * members + near), (at + 1, (low ^ 1) * members + near + 1)]
            routes[1] += [(at, (low ^ 3) * members + near), (at + 1, low * members + (near ^ 2) + 1)]
    sums = narrow(running, power, heights)
    heard = [lax.ppermute(sums, everyone, route) for route in routes]
    left_top, left_low, last = call(
        functools.partial(stage_kernel, 6),
        [
            pltpu.VMEM(top_left.shape, BF16),
            pltpu.VMEM((capacity, member_levels * 2 * width), BF16),
            jax.ShapeDtypeStruct((2 * height, columns), F32),
        ],
        [HBM, HBM, HBM, VMEM, pl.BlockSpec(memory_space=pl.ANY)],
        (*far(top_left, low_left, diag_block), pair, running),
        8 * height * capacity * columns,
        12 << 20,
        24,
        scratch=[
            pltpu.VMEM(low_left.shape, BF16),
            pltpu.VMEM((2, 2, height, capacity), BF16),
            DMA((4,)),
        ],
    )
    bases.append(last)
    heard, left_top, left_low = lax.optimization_barrier((heard, left_top, left_low))
    heard = [widen(block, heights)[0] for block in heard]
    own = (heard[0] + jnp.where(flags[:1] > 0, heard[1], 0.0)).astype(BF16)
    own_low = jnp.concatenate(coefs)
    their_low, own = lax.optimization_barrier((partner(own_low, "member", 0), own))
    theirs = partner(own, "member", 0)
    base = call(
        functools.partial(low_kernel, len(bases)),
        [jax.ShapeDtypeStruct((capacity, columns), F32)],
        [VMEM] * (len(bases) + 4),
        (*bases, left_low, nearest, own_low, their_low),
        4 * capacity * columns * member_levels * width,
        3 << 20,
        16,
    )[0]

    leaving = call(
        functools.partial(out_kernel, bucket),
        [jax.ShapeDtypeStruct((capacity, columns), BF16)],
        [VMEM] * 6,
        (flags, base, left_top, own, theirs, slots),
        4 * capacity * columns * group_levels * top_width,
        4 << 20,
        24,
        scratch=[
            pltpu.VMEM((leaves * filled, 128), BF16),
            pltpu.VMEM((leaves, filled, 128), F32),
        ],
    )[0]
    returned = lax.all_to_all(
        leaving.reshape(leaves, bucket, columns), everyone, split_axis=0, concat_axis=0, tiled=True
    )
    return call(
        unpack_kernel,
        [jax.ShapeDtypeStruct((count, columns), F32)],
        [VMEM] * 3,
        (order, upper, returned.reshape(capacity, columns)),
        2 * capacity * count * columns,
        4 << 20,
        16,
        out_specs=[HBM],
        scratch=[pltpu.VMEM((count, 128), F32), DMA((count // 256,))],
    )[0]


def solution(mesh):
    return jax.shard_map(
        on_device,
        mesh=mesh,
        in_specs=(
            P(("group", "member"), None),
            P(("group", "member")),
            P(),
            P(),
            P(None, ("group", "member"), None),
            P(None, None, ("group", "member"), None),
            P(None, None, ("group", "member"), None),
            P(None, None, ("group", "member"), None),
            P(None, None, ("group", "member"), None),
        ),
        out_specs=P(("group", "member"), None),
        check_vma=False,
    )
```
